128 devices in a mesh: expert: 8 (over x_hi, z), fsdp: 16 (over x_lo, y, core).
Axes of the slice: x: 4 (x_hi: 2, x_lo: 2; x = x_hi * 2 + x_lo), y: 4, z: 4, core: 2. Of those that a mesh axis runs over, the one named last changes fastest.
Arguments:
- tokens: bfloat16 [16384, 1536], P(('expert', 'fsdp')), may hold values from -6 to 6
- cotangent: bfloat16 [16384, 1536], P(('expert', 'fsdp')), may hold values from -6 to 6
- routes: int32 [16384, 8], P(('expert', 'fsdp')), may hold values from 0 to 39, all different within a row; in each aligned block of 128 rows (0 to 127, 128 to 255, ...) at most 32 rows name the same one
- norm_one: bfloat16 [1536], P('fsdp'), may hold values from 0.5 to 1.5
- w_query: bfloat16 [1536, 1536], P('fsdp'), may hold values from -0.15625 to 0.15625
- key_weight: bfloat16 [1536, 512], P('fsdp'), may hold values from -0.15625 to 0.15625
- value_weight: bfloat16 [1536, 512], P('fsdp'), may hold values from -0.15625 to 0.15625
- w_out: bfloat16 [1536, 1536], P('fsdp'), may hold values from -0.4375 to 0.4375
- norm_two: bfloat16 [1536], P('fsdp'), may hold values from 0.5 to 1.5
- w_router: bfloat16 [1536, 40], P('fsdp'), may hold values from -0.078125 to 0.078125
- w_gate: bfloat16 [40, 1536, 512], P('expert', 'fsdp'), may hold values from -0.15625 to 0.15625
- w_up: bfloat16 [40, 1536, 512], P('expert', 'fsdp'), may hold values from -0.15625 to 0.15625
- w_down: bfloat16 [40, 512, 1536], P('expert', None, 'fsdp'), may hold values from -0.75 to 0.75
Outputs:
- mixed_out: bfloat16 [16384, 1536], P(('expert', 'fsdp'))
- grad_tokens: float32 [16384, 1536], P(('expert', 'fsdp'))
- grad_norm_one: float32 [1536], P('fsdp')
- grad_query: float32 [1536, 1536], P('fsdp')
- grad_key: float32 [1536, 512], P('fsdp')
- grad_value: float32 [1536, 512], P('fsdp')
- grad_out: float32 [1536, 1536], P('fsdp')
- grad_norm_two: float32 [1536], P('fsdp')
- grad_router: float32 [1536, 40], P('fsdp')
- grad_gate: float32 [40, 1536, 512], P('expert', 'fsdp')
- grad_up: float32 [40, 1536, 512], P('expert', 'fsdp')
- grad_down: float32 [40, 512, 1536], P('expert', None, 'fsdp')
The draws below stay inside these ranges and needn't reach their ends.
Inputs may be any that keep to these rules, and one draw needn't show every extreme that they name: In the rows of one device, no expert is named by more than 32 routes, a bound that some block reaches; the 8 experts of a token differ.
All inputs are finite; a program needn't handle non-finite values.
Results may differ from the reference program's by a relative error of at most 0.025.
Values may be sent and summed in bfloat16 or wider, within the bound.
No kernel may reach another device: no remote copies, remote signals or barrier semaphores. Data moves between devices by JAX's collectives and lax.ppermute only.
A program may use at most 192 MiB of HBM per device.

```python
import math
import jax
import jax.numpy as jnp
import numpy as np
from jax import lax

MODEL_DIM = 1536
QUERY_HEADS = 24
KEY_VALUE_HEADS = 8
HEAD_DIM = 64
E = 40
H = 512
TOPK = 8
TOKENS_PER_CARD = 128
CAP = 32
TOKENS = 16384


def levels(key, extent, shards, least, largest):
    level, own = 1.0, jax.random.fold_in(key, 6)
    for dim, blocks in shards:
        heights = jnp.exp(jax.random.uniform(jax.random.fold_in(own, dim), (blocks,), jnp.float32, least / len(shards), largest / len(shards)))
        level = level * jnp.repeat(heights, extent[dim] // blocks).reshape([-1 if axis == dim else 1 for axis in range(len(extent))])
    return level


def deal_out(own_key, own, number, rows, amount, top, bound, skew):
    sequence = jax.random.permutation(own_key, amount)
    packed, ordinary = portions_of(amount, rows * top, bound, skew, True), portions_of(amount, rows * top, bound, skew, False)
    places = jnp.arange(amount)

    def named(sizes, turn):
        used = int((sizes > 0).sum())
        fixed = max(1, used // 4)
        shifted = fixed + (places - fixed + turn * (used - fixed)) % max(1, amount - fixed)
        return jnp.zeros((amount,), jnp.int32).at[sequence[jnp.where(places < fixed, places, shifted)]].set(jnp.asarray(sizes, jnp.int32))

    sizes = jnp.where(number % 4 == 0, named(packed, number // 4), named(ordinary, number - number // 4 - 1))
    mixed = jax.random.permutation(jax.random.fold_in(own, 3), amount)
    giver, sink = mixed[0:amount // 2 * 2:2], mixed[1:amount // 2 * 2:2]
    room = jnp.minimum(sizes[giver] - 1, bound - sizes[sink]) // 2
    room = jnp.where((giver == sequence[0]) | (sink == sequence[0]) | (sizes[sink] == 0), 0, jnp.maximum(room, 0))
    shifted = jax.random.randint(jax.random.fold_in(own, 4), (amount // 2,), 0, 1 << 20) % (room + 1)
    sizes = sizes.at[giver].add(-shifted).at[sink].add(shifted)
    members = jnp.searchsorted(jnp.cumsum(sizes), jnp.arange(rows * top), side="right").astype(jnp.int32)
    grid = members.reshape(top, rows).T
    grid = grid[jax.random.permutation(jax.random.fold_in(own, 1), rows)]
    turn = jax.random.randint(jax.random.fold_in(own, 2), (rows, 1), 0, top)
    return jnp.take_along_axis(grid, (jnp.arange(top)[None, :] + turn) % top, axis=1)


def portions_of(number_of, total, reach, slope, full):
    weights = [(1 << 20) // math.isqrt(standing ** slope) + 1 for standing in range(1, number_of + 1)]
    largest = reach if full else min(reach, max(-(-total // number_of), total * weights[0] // sum(weights)))
    least = 1 if total - largest >= number_of - 1 else 0
    given, surplus = [largest] + [least] * (number_of - 1), total - largest - least * (number_of - 1)
    while surplus > 0:
        candidates = [i for i in range(1, number_of) if given[i] < largest] or [i for i in range(1, number_of) if given[i] < reach]
        pool, budget = sum([weights[i] for i in candidates]), surplus
        for i in candidates:
            more = min(reach - given[i], max(1, budget * weights[i] // pool), surplus)
            given[i] = given[i] + more
            surplus = surplus - more
    return np.array(given)


def normal_values(stream_key, dims, width, most, cuts=(), kind=jnp.bfloat16):
    result = width * jax.random.normal(stream_key, dims, jnp.float32)
    if cuts:
        result = result * levels(stream_key, dims, cuts, -0.22, 0.18)
    return jnp.clip(result, -most, most).astype(kind)


def setup_inputs(seed: int = 0) -> dict:
    splits = jax.random.split(jax.random.key(seed), 14)
    tokens = normal_values(splits[0], (TOKENS, MODEL_DIM), 1.0, 6.0, ((0, 128),))
    cotangent = normal_values(splits[1], (TOKENS, MODEL_DIM), 1.0, 6.0, ((0, 128),))
    routes_keys = jax.random.split(jax.random.fold_in(splits[2], 1), TOKENS // TOKENS_PER_CARD)
    routes_turns = jax.random.permutation(jax.random.fold_in(splits[2], 3), TOKENS // TOKENS_PER_CARD)
    routes = jax.vmap(lambda own, number: deal_out(jax.random.fold_in(splits[2], 2), own, number, TOKENS_PER_CARD, E, TOPK, CAP, 1))(routes_keys, routes_turns).reshape((TOKENS, TOPK))
    norm_one = jnp.clip(1.0 + 0.1 * jax.random.normal(splits[3], (MODEL_DIM,), jnp.float32), 0.5, 1.5).astype(jnp.bfloat16)
    w_query = normal_values(splits[4], (MODEL_DIM, QUERY_HEADS * HEAD_DIM), MODEL_DIM ** -0.5, 0.15625, ((0, 16),))
    key_weight = normal_values(splits[5], (MODEL_DIM, KEY_VALUE_HEADS * HEAD_DIM), MODEL_DIM ** -0.5, 0.15625, ((0, 16),))
    value_weight = normal_values(splits[6], (MODEL_DIM, KEY_VALUE_HEADS * HEAD_DIM), MODEL_DIM ** -0.5, 0.15625, ((0, 16),))
    w_out = normal_values(splits[7], (QUERY_HEADS * HEAD_DIM, MODEL_DIM), (QUERY_HEADS * HEAD_DIM // 8) ** -0.5, 0.4375, ((0, 16),))
    norm_two = jnp.clip(1.0 + 0.1 * jax.random.normal(splits[8], (MODEL_DIM,), jnp.float32), 0.5, 1.5).astype(jnp.bfloat16)
    w_router = normal_values(splits[9], (MODEL_DIM, E), (4 * MODEL_DIM) ** -0.5, 0.078125, ((0, 16),))
    w_gate = normal_values(splits[10], (E, MODEL_DIM, H), MODEL_DIM ** -0.5, 0.15625, ((0, 8), (1, 16)))
    w_up = normal_values(splits[11], (E, MODEL_DIM, H), MODEL_DIM ** -0.5, 0.15625, ((0, 8), (1, 16)))
    w_down = normal_values(splits[12], (E, H, MODEL_DIM), (H // 8) ** -0.5, 0.75, ((0, 8), (2, 16)))
    return dict(tokens=tokens, cotangent=cotangent, routes=routes, norm_one=norm_one, w_query=w_query, key_weight=key_weight, value_weight=value_weight, w_out=w_out, norm_two=norm_two, w_router=w_router, w_gate=w_gate, w_up=w_up, w_down=w_down)


NORM_EPSILON = 1e-05
HIGHEST_PRECISION = lax.Precision.HIGHEST

@jax.custom_vjp
def reduced_precision(v):
    return lax.optimization_barrier(v.astype(jnp.bfloat16)).astype(jnp.float32)

@jax.custom_vjp
def reduced_precision_backward(v):
    return v

def low_keep(v):
    return (reduced_precision(v), None)

def low_pass(kept, grad):
    return (grad,)

def back_keep(v):
    return (v, None)

def back_low(kept, grad):
    return (reduced_precision(grad),)
reduced_precision.defvjp(low_keep, low_pass)
reduced_precision_backward.defvjp(back_keep, back_low)

def matrix_product(left, right):
    return jnp.dot(left, right, preferred_element_type=jnp.float32, precision=HIGHEST_PRECISION)

def rope_tables(sequence_length):
    half_dim = HEAD_DIM // 2
    frequency = jnp.exp(-jnp.log(10000.0) * jnp.arange(half_dim, dtype=jnp.float32) * 2.0 / HEAD_DIM)
    angles = jnp.arange(sequence_length, dtype=jnp.float32)[:, None] * frequency[None, :]
    cosine_table = jnp.concatenate([jnp.cos(angles), jnp.cos(angles)], axis=1)[:, None, :]
    sines_lookup = jnp.concatenate([jnp.sin(angles), jnp.sin(angles)], axis=1)[:, None, :]
    return (cosine_table, sines_lookup)

def apply_rotary(values, cosine_table, sines_lookup):
    half_dim = values.shape[-1] // 2
    turned = jnp.concatenate([-values[..., half_dim:], values[..., :half_dim]], axis=-1)
    return values * cosine_table + turned * sines_lookup

def norm_of(values, gain):
    return values * lax.rsqrt(lax.optimization_barrier(jnp.mean(values * values, axis=-1, keepdims=True)) + NORM_EPSILON) * gain

def softmax_last(values):
    row_peak = lax.optimization_barrier(jnp.max(values, axis=-1, keepdims=True))
    exponent = jnp.exp(values - row_peak)
    return exponent / lax.optimization_barrier(jnp.sum(exponent, axis=-1, keepdims=True))

def attend(pieces):
    query_matrix, rotated_keys, rows_of_value = pieces
    sequence_length = query_matrix.shape[1]
    scores = jnp.einsum('sqhgd,skhd->shgqk', query_matrix, rotated_keys, precision=HIGHEST_PRECISION) * HEAD_DIM ** (-0.5)
    scores = reduced_precision_backward(scores)
    visible = jnp.arange(sequence_length)[:, None] >= jnp.arange(sequence_length)[None, :]
    scores = jnp.where(visible, scores, -jnp.inf)
    probability = softmax_last(scores)
    return jnp.einsum('shgqk,skhd->sqhgd', reduced_precision(probability), rows_of_value, precision=HIGHEST_PRECISION)

def expert_apply(pieces):
    rows_in, gate_w, up_w, down_w = pieces
    gate_pre = reduced_precision_backward(matrix_product(rows_in, gate_w))
    up_pre = reduced_precision_backward(matrix_product(rows_in, up_w))
    activated = reduced_precision(gate_pre * jax.nn.sigmoid(gate_pre) * up_pre)
    return reduced_precision_backward(reduced_precision(matrix_product(activated, down_w)))

def reference(tokens, cotangent, routes, norm_one, w_query, key_weight, value_weight, w_out, norm_two, w_router, w_gate, w_up, w_down):
    block_list = TOKENS // TOKENS_PER_CARD
    route_count = TOKENS * TOPK
    route_flat = routes.reshape(block_list, TOKENS_PER_CARD * TOPK)
    onehot = (route_flat[:, :, None] == jnp.arange(E, dtype=jnp.int32)[None, None, :]).astype(jnp.int32)
    place_slot = lax.optimization_barrier(jnp.sum(onehot * (jnp.cumsum(onehot, axis=1) - 1), axis=2)).astype(jnp.int32)
    destination = route_flat * (block_list * CAP) + jnp.arange(block_list, dtype=jnp.int32)[:, None] * CAP + place_slot
    destination = destination.astype(jnp.int32).reshape(-1)
    table_route = jnp.full((E * block_list * CAP,), route_count, jnp.int32).at[destination].set(jnp.arange(route_count, dtype=jnp.int32))
    table_token = jnp.where(table_route < route_count, table_route // TOPK, TOKENS).astype(jnp.int32)
    member = routes[:, :, None] == jnp.arange(E, dtype=jnp.int32)[None, None, :]
    cosine_table, sines_lookup = rope_tables(TOKENS_PER_CARD)
    group_width = min(block_list, max(1, 4096 // TOKENS_PER_CARD))

    def head_list(values, head_count):
        return values.reshape(block_list // group_width, group_width, TOKENS_PER_CARD, head_count, HEAD_DIM)

    def forward(source, gain_one, query_w, key_matrix, value_matrix, out_w, gain_two, router_w, gate_w, up_w, down_w):
        first_hidden = reduced_precision(norm_of(source, gain_one))
        query_matrix = reduced_precision(apply_rotary(reduced_precision_backward(head_list(matrix_product(first_hidden, query_w), QUERY_HEADS)), cosine_table, sines_lookup))
        query_matrix = query_matrix.reshape(block_list // group_width, group_width, TOKENS_PER_CARD, KEY_VALUE_HEADS, QUERY_HEADS // KEY_VALUE_HEADS, HEAD_DIM)
        rotated_keys = reduced_precision(apply_rotary(reduced_precision_backward(head_list(matrix_product(first_hidden, key_matrix), KEY_VALUE_HEADS)), cosine_table, sines_lookup))
        rows_of_value = reduced_precision(reduced_precision_backward(head_list(matrix_product(first_hidden, value_matrix), KEY_VALUE_HEADS)))
        attended = lax.map(jax.checkpoint(attend), (query_matrix, rotated_keys, rows_of_value)).reshape(TOKENS, QUERY_HEADS * HEAD_DIM)
        residual = source + reduced_precision_backward(matrix_product(reduced_precision_backward(reduced_precision(attended)), out_w))
        hidden_two = reduced_precision(norm_of(residual, gain_two))
        logits = reduced_precision_backward(matrix_product(hidden_two, router_w))
        chosen = lax.optimization_barrier(jnp.sum(jnp.where(member, logits[:, None, :], 0.0), axis=-1))
        gate_weights = softmax_last(chosen)
        padded = jnp.concatenate([hidden_two, jnp.zeros((1, MODEL_DIM), jnp.float32)], axis=0)
        buffer_rows = reduced_precision_backward(padded[table_token]).reshape(E, block_list * CAP, MODEL_DIM)
        expert_rows = lax.map(jax.checkpoint(expert_apply), (buffer_rows, gate_w, up_w, down_w)).reshape(E * block_list * CAP, MODEL_DIM)
        gate_flat = jnp.concatenate([gate_weights.reshape(-1), jnp.zeros((1,), jnp.float32)])
        weighted = expert_rows * gate_flat[table_route][:, None]
        combined = jnp.zeros((TOKENS + 1, MODEL_DIM), jnp.float32).at[table_token].add(weighted)[:TOKENS]
        return residual + combined
    primal = tuple((piece.astype(jnp.float32) for piece in (tokens, norm_one, w_query, key_weight, value_weight, w_out, norm_two, w_router, w_gate, w_up, w_down)))
    output, pull_back = jax.vjp(forward, *primal)
    gradients = pull_back(cotangent.astype(jnp.float32))
    return (output.astype(jnp.bfloat16), gradients[0], gradients[1], gradients[2], gradients[3], gradients[4], gradients[5], gradients[6], gradients[7], gradients[8], gradients[9], gradients[10])
```

```python
import functools

import jax
import jax.numpy as jnp
import numpy as np
from jax import lax
from jax.experimental import pallas as pl
from jax.experimental.pallas import tpu as pltpu
from jax.sharding import PartitionSpec as P

QUERY_HEADS = 24
KEY_VALUE_HEADS = 8
GROUP = QUERY_HEADS // KEY_VALUE_HEADS
HEAD_DIM = 64
HALF = HEAD_DIM // 2
E = 40
H = 512
D = 1536
T = 128
CAP = 32
NORM_EPSILON = 1e-05
SCALE = HEAD_DIM ** (-0.5)

Z = 4
PEERS = 8
LOCAL = E // PEERS
SLOTS = LOCAL * CAP
LANES = 128
BLOCK = 512
PACK = 4096 + LANES
VMEM_LIMIT = 60 * 1024 * 1024

F32 = jnp.float32
BF16 = jnp.bfloat16


def peer(index, hop, back=False):
    shift = hop % Z
    turned = (index % Z + (Z - shift if back else shift)) % Z
    return (index // Z + hop // Z) % 2 * Z + turned


def send(value, hop, back=False):
    if hop == 0:
        return value
    return lax.ppermute(value, "expert", [(i, peer(i, hop, back)) for i in range(PEERS)])


def mm(left, right):
    return jnp.dot(left, right, preferred_element_type=F32)


def mm_nt(left, right):
    return lax.dot_general(left, right, (((1,), (1,)), ((), ())), preferred_element_type=F32)


def mm_tn(left, right):
    return lax.dot_general(left, right, (((0,), (0,)), ((), ())), preferred_element_type=F32)


def rope_tables():
    frequency = np.exp(-np.log(10000.0) * np.arange(HALF, dtype=np.float64) * 2.0 / HEAD_DIM)
    angles = np.arange(T, dtype=np.float64)[:, None] * frequency[None, :]
    cosine = np.tile(np.cos(angles), (1, 4)).astype(np.float32)
    sine = np.sin(angles)
    signed = np.tile(np.concatenate([-sine, sine], axis=1), (1, 2)).astype(np.float32)
    return cosine, signed


def swap_halves(values):
    width = values.shape[1]
    lane = lax.broadcasted_iota(jnp.int32, values.shape, 1)
    up = pltpu.roll(values, width - HALF, 1)
    down = pltpu.roll(values, HALF, 1)
    return jnp.where(lane % HEAD_DIM < HALF, up, down)


def wide(table, width):
    return jnp.concatenate([table] * (width // LANES), axis=1)


def rotate(values, cosine, signed):
    width = values.shape[1]
    return values * wide(cosine, width) + swap_halves(values) * wide(signed, width)


def rotate_back(values, cosine, signed):
    width = values.shape[1]
    return values * wide(cosine, width) + swap_halves(values * wide(signed, width))


def gain_rows(small):
    pick = lax.broadcasted_iota(jnp.int32, (16, LANES), 1) == (
        lax.broadcasted_iota(jnp.int32, (16, LANES), 0) + E
    )
    return mm_nt(pick.astype(BF16), small)


def norm_of(values):
    inverse = lax.rsqrt(jnp.mean(values * values, axis=-1, keepdims=True) + NORM_EPSILON)
    return values * inverse, inverse


def head(ref, index):
    return ref[:, index * HEAD_DIM : (index + 1) * HEAD_DIM]


def probabilities(query, key):
    scores = mm_nt(query, key) * SCALE
    rows = lax.broadcasted_iota(jnp.int32, scores.shape, 0)
    cols = lax.broadcasted_iota(jnp.int32, scores.shape, 1)
    scores = jnp.where(rows >= cols, scores, -jnp.inf)
    exponent = jnp.exp(scores - jnp.max(scores, axis=-1, keepdims=True))
    return exponent / jnp.sum(exponent, axis=-1, keepdims=True)


def attention_forward_kernel(
    x_ref, w_ref, small_ref, cos_ref, sin_ref, q_ref, k_ref, v_ref, ob_ref, x1_ref, h2_ref, h1
):
    step = pl.program_id(0)

    @pl.when(step == 0)
    def _():
        gain = gain_rows(small_ref[...])[0:1, :]
        normed, _ = norm_of(x_ref[...].astype(F32))
        h1[...] = (normed * gain).astype(BF16)

    @pl.when(step < 3)
    def _():
        columns = pl.ds(pl.multiple_of(step * BLOCK, BLOCK), BLOCK)
        q_ref[:, columns] = rotate(mm(h1[...], w_ref[...]), cos_ref[...], sin_ref[...]).astype(BF16)

    @pl.when(step == 3)
    def _():
        k_ref[...] = rotate(mm(h1[...], w_ref[...]), cos_ref[...], sin_ref[...]).astype(BF16)

    @pl.when(step == 4)
    def _():
        v_ref[...] = mm(h1[...], w_ref[...]).astype(BF16)
        for group in range(KEY_VALUE_HEADS):
            key, value = head(k_ref, group), head(v_ref, group)
            for index in range(group * GROUP, (group + 1) * GROUP):
                probability = probabilities(head(q_ref, index), key).astype(BF16)
                ob_ref[:, index * HEAD_DIM : (index + 1) * HEAD_DIM] = mm(
                    probability, value
                ).astype(BF16)

    @pl.when(step > 4)
    def _():
        columns = pl.ds(pl.multiple_of((step - 5) * BLOCK, BLOCK), BLOCK)
        x1_ref[:, columns] = x_ref[:, columns].astype(F32) + mm(ob_ref[...], w_ref[...])

    @pl.when(step == 7)
    def _():
        gain = gain_rows(small_ref[...])[1:2, :]
        normed, _ = norm_of(x1_ref[...])
        h2_ref[...] = (normed * gain).astype(BF16)


def whole(shape):
    return pl.BlockSpec(shape, lambda *_: (0,) * len(shape))


def params(**more):
    return pltpu.CompilerParams(vmem_limit_bytes=VMEM_LIMIT, **more)


def cost(flops, moved):
    return pl.CostEstimate(flops=flops, bytes_accessed=moved, transcendentals=0)


def attention_forward(x, pack, cosine, signed):
    shape = jax.ShapeDtypeStruct
    return pl.pallas_call(
        attention_forward_kernel,
        grid=(8,),
        in_specs=[
            whole((T, D)),
            pl.BlockSpec((D, BLOCK), lambda i: (0, i)),
            pl.BlockSpec((D, LANES), lambda i: (0, 4096 // LANES)),
            whole((T, LANES)),
            whole((T, LANES)),
        ],
        out_specs=[
            whole((T, D)),
            whole((T, BLOCK)),
            whole((T, BLOCK)),
            whole((T, D)),
            whole((T, D)),
            whole((T, D)),
        ],
        out_shape=[
            shape((T, D), BF16),
            shape((T, BLOCK), BF16),
            shape((T, BLOCK), BF16),
            shape((T, D), BF16),
            shape((T, D), F32),
            shape((T, D), BF16),
        ],
        scratch_shapes=[pltpu.VMEM((T, D), BF16)],
        compiler_params=params(),
        cost_estimate=cost(2 * T * D * 4096, 14 << 20),
        name="attention_forward",
    )(x, pack, pack, cosine, signed)


def gate_kernel(small_ref, member_ref, chosen_ref, place_ref, *refs):
    rows, (gates_ref, slot_gate_ref, b_ref) = refs[:PEERS], refs[PEERS:]
    small = small_ref[...]
    for hop in range(PEERS):
        h2 = rows[hop][...]
        member = member_ref[hop] > 0.5
        logits = jnp.where(member, mm(h2, small), -jnp.inf)
        exponent = jnp.exp(logits - jnp.max(logits, axis=-1, keepdims=True))
        gates = exponent / jnp.sum(exponent, axis=-1, keepdims=True)
        gates_ref[hop] = gates
        high = gates.astype(BF16)
        low = (gates - high.astype(F32)).astype(BF16)
        place = place_ref[hop]
        spread = mm(place, high) + mm(place, low)
        picked = jnp.sum(spread * chosen_ref[...], axis=-1, keepdims=True)
        slot_gate_ref[:, hop] = picked.reshape(LOCAL, CAP, 1)
        b_ref[:, hop] = mm(place, h2).astype(BF16).reshape(LOCAL, CAP, D)


def gate_rows(small_pack, member, chosen, place, rows):
    shape = jax.ShapeDtypeStruct
    return pl.pallas_call(
        gate_kernel,
        grid=(1,),
        in_specs=[
            pl.BlockSpec((D, LANES), lambda i: (0, 4096 // LANES)),
            whole((PEERS, T, LANES)),
            whole((SLOTS, LANES)),
            whole((PEERS, SLOTS, T)),
        ]
        + [whole((T, D))] * PEERS,
        out_specs=[
            whole((PEERS, T, LANES)),
            whole((LOCAL, PEERS, CAP, 1)),
            whole((LOCAL, PEERS, CAP, D)),
        ],
        out_shape=[
            shape((PEERS, T, LANES), F32),
            shape((LOCAL, PEERS, CAP, 1), F32),
            shape((LOCAL, PEERS, CAP, D), BF16),
        ],
        compiler_params=params(),
        cost_estimate=cost(2 * PEERS * SLOTS * T * D, 8 << 20),
        name="gate_rows",
    )(small_pack, member, chosen, place, *rows)


def spread_kernel(place_ref, *refs):
    rows, out_ref = refs[:PEERS], refs[PEERS]
    for hop in range(PEERS):
        out_ref[:, hop] = (
            mm(place_ref[hop], rows[hop][:, :D]).astype(BF16).reshape(LOCAL, CAP, D)
        )


def spread_rows(place, rows):
    return pl.pallas_call(
        spread_kernel,
        grid=(1,),
        in_specs=[whole((PEERS, SLOTS, T))] + [whole(rows[0].shape)] * PEERS,
        out_specs=whole((LOCAL, PEERS, CAP, D)),
        out_shape=jax.ShapeDtypeStruct((LOCAL, PEERS, CAP, D), BF16),
        compiler_params=params(),
        cost_estimate=cost(2 * PEERS * SLOTS * T * D, 8 << 20),
        name="spread_rows",
    )(place, *rows)


def expert_kernel(b_ref, dyr_ref, gate_ref, w_ref, grad_ref, gy_ref, db_ref):
    rows = b_ref[0]
    gate = gate_ref[0]
    down = w_ref[0, :, 2 * H : 3 * H]
    pre = mm(rows, w_ref[0, :, 0 : 2 * H])
    gate_pre, up_pre = pre[:, :H], pre[:, H:]
    sigmoid = 1.0 / (1.0 + jnp.exp(-gate_pre))
    silu = gate_pre * sigmoid
    activated = (silu * up_pre).astype(BF16)
    result = mm_nt(activated, down).astype(BF16).astype(F32)
    raw = dyr_ref[0].astype(F32)
    gy_ref[0] = (gate * result).astype(BF16)
    inner = jnp.sum(raw * result, axis=-1, keepdims=True)
    grad_rows = (gate * raw).astype(BF16)
    grad_act = mm(grad_rows, down)
    grad_ref[0, :, 2 * H : 3 * H] = mm_tn(grad_rows, activated).astype(BF16)
    grad_gate = (grad_act * up_pre * sigmoid * (1.0 + gate_pre * (1.0 - sigmoid))).astype(BF16)
    grad_up = (grad_act * silu).astype(BF16)
    both = jnp.concatenate([grad_gate, grad_up], axis=1)
    db_ref[0, :, 0:D] = mm_nt(both, w_ref[0, :, 0 : 2 * H]).astype(BF16)
    grad_ref[0, :, 0 : 2 * H] = mm_tn(rows, both).astype(BF16)
    expert = pl.program_id(0)
    lane = lax.broadcasted_iota(jnp.int32, (PEERS * CAP, LANES), 1)
    high = inner.astype(BF16).astype(F32)
    low = inner - high
    tail = jnp.where(lane == expert, high, jnp.where(lane == expert + LOCAL, low, 0.0))
    db_ref[0, :, D : D + LANES] = tail.astype(BF16)


def experts(b, dyr, slot_gate, pack):
    shape = jax.ShapeDtypeStruct
    rows = PEERS * CAP
    return pl.pallas_call(
        expert_kernel,
        grid=(LOCAL,),
        in_specs=[
            pl.BlockSpec((1, rows, D), lambda e: (e, 0, 0)),
            pl.BlockSpec((1, rows, D), lambda e: (e, 0, 0)),
            pl.BlockSpec((1, rows, 1), lambda e: (e, 0, 0)),
            pl.BlockSpec((1, D, 3 * H), lambda e: (e, 0, 0)),
        ],
        out_specs=[
            pl.BlockSpec((1, D, 3 * H), lambda e: (e, 0, 0)),
            pl.BlockSpec((1, rows, D), lambda e: (e, 0, 0)),
            pl.BlockSpec((1, rows, D + LANES), lambda e: (e, 0, 0)),
        ],
        out_shape=[
            shape((LOCAL, D, 3 * H), BF16),
            shape((LOCAL, rows, D), BF16),
            shape((LOCAL, rows, D + LANES), BF16),
        ],
        compiler_params=params(),
        cost_estimate=cost(18 * LOCAL * rows * D * H, 60 << 20),
        name="experts",
    )(b, dyr, slot_gate, pack)


def collect_kernel(place_ref, value_ref, *out_refs):
    for hop in range(PEERS):
        rows = value_ref[:, hop].reshape(SLOTS, value_ref.shape[-1])
        out_refs[hop][...] = mm_tn(place_ref[hop], rows).astype(BF16)


def collect(place, values, name):
    width = values.shape[-1]
    return pl.pallas_call(
        collect_kernel,
        grid=(1,),
        in_specs=[whole((PEERS, SLOTS, T)), whole((LOCAL, PEERS, CAP, width))],
        out_specs=[whole((T, width))] * PEERS,
        out_shape=[jax.ShapeDtypeStruct((T, width), BF16)] * PEERS,
        compiler_params=params(),
        cost_estimate=cost(2 * PEERS * SLOTS * T * width, 8 << 20),
        name=name,
    )(place, values.reshape(LOCAL, PEERS, CAP, width))


def mixed_kernel(x1_ref, *refs):
    total = x1_ref[...]
    for ref in refs[:PEERS]:
        total = total + ref[...].astype(F32)
    refs[PEERS][...] = total.astype(BF16)


def mix(x1, parts):
    return pl.pallas_call(
        mixed_kernel,
        grid=(1,),
        in_specs=[whole((T, D))] * (1 + PEERS),
        out_specs=whole((T, D)),
        out_shape=jax.ShapeDtypeStruct((T, D), BF16),
        compiler_params=params(),
        cost_estimate=cost(T * D * 8, 5 << 20),
        name="mix",
    )(x1, *parts)


def norm_back(grad, normed, inverse, gain):
    scaled = grad * gain
    return inverse * (scaled - normed * jnp.mean(scaled * normed, axis=-1, keepdims=True))


def attention_backward_kernel(
    x_ref,
    x1_ref,
    h2_ref,
    dy_ref,
    gates_ref,
    place_ref,
    q_ref,
    k_ref,
    v_ref,
    ob_ref,
    w_ref,
    small_ref,
    cos_ref,
    sin_ref,
    *refs,
):
    parts = refs[:PEERS]
    grad_tokens_ref, pack_ref = refs[PEERS : PEERS + 2]
    h1, da, dx1, dob, dqf, dkf, dvf, dqkv, dh1, dh2, dlogits, stage, small_stage, sems = refs[
        PEERS + 2 :
    ]
    step = pl.program_id(0)
    slot = lax.rem(step, 2)

    def block_copy(at, which):
        column = lax.rem(at + 5, 8) * BLOCK
        return pltpu.make_async_copy(
            stage.at[which],
            pack_ref.at[:, pl.ds(pl.multiple_of(column, BLOCK), BLOCK)],
            sems.at[which],
        )

    @pl.when(step == 0)
    def _():
        grad = jnp.zeros((T, D), F32)
        inner = jnp.zeros((T, LANES), F32)
        for hop in range(PEERS):
            grad = grad + parts[hop][:, :D].astype(F32)
            inner = inner + mm(parts[hop][:, D:], place_ref[hop])
        gates = gates_ref[...]
        score = gates * (inner - jnp.sum(gates * inner, axis=-1, keepdims=True))
        dlogits[...] = score.astype(BF16)
        grad = grad + mm_nt(dlogits[...], small_ref[...])
        dh2[...] = grad
        gains = gain_rows(small_ref[...])
        normed_two, inverse_two = norm_of(x1_ref[...])
        through = dy_ref[...].astype(F32) + norm_back(grad, normed_two, inverse_two, gains[1:2, :])
        dx1[...] = through
        da[...] = through.astype(BF16)
        normed_one, _ = norm_of(x_ref[...].astype(F32))
        h1[...] = (normed_one * gains[0:1, :]).astype(BF16)
        dob[...] = jnp.zeros((T, D), F32)
        dh1[...] = jnp.zeros((T, D), F32)

    @pl.when(step >= 2)
    def _():
        block_copy(step - 2, slot).wait()

    @pl.when(step < 3)
    def _():
        columns = pl.ds(pl.multiple_of(step * BLOCK, BLOCK), BLOCK)
        piece = da[:, columns]
        dob[...] += mm_nt(piece, w_ref[...])
        stage[slot] = mm_tn(ob_ref[...], piece).astype(BF16)

    @pl.when(step == 3)
    def _():
        for group in range(KEY_VALUE_HEADS):
            key, value = head(k_ref, group), head(v_ref, group)
            grad_key = jnp.zeros((T, HEAD_DIM), F32)
            grad_value = jnp.zeros((T, HEAD_DIM), F32)
            for index in range(group * GROUP, (group + 1) * GROUP):
                query = head(q_ref, index)
                out_grad = head(dob, index).astype(BF16)
                probability = probabilities(query, key)
                grad_prob = mm_nt(out_grad, value)
                grad_value = grad_value + mm_tn(probability.astype(BF16), out_grad)
                held = jnp.sum(probability * grad_prob, axis=-1, keepdims=True)
                grad_scores = (probability * (grad_prob - held)).astype(BF16)
                dqf[:, index * HEAD_DIM : (index + 1) * HEAD_DIM] = mm(grad_scores, key) * SCALE
                grad_key = grad_key + mm_tn(grad_scores, query)
            dkf[:, group * HEAD_DIM : (group + 1) * HEAD_DIM] = grad_key * SCALE
            dvf[:, group * HEAD_DIM : (group + 1) * HEAD_DIM] = grad_value
        cosine, signed = cos_ref[...], sin_ref[...]
        dqkv[:, 0:D] = rotate_back(dqf[...], cosine, signed).astype(BF16)
        dqkv[:, D : D + BLOCK] = rotate_back(dkf[...], cosine, signed).astype(BF16)
        dqkv[:, D + BLOCK : D + 2 * BLOCK] = dvf[...].astype(BF16)

    @pl.when(step >= 3)
    def _():
        columns = pl.ds(pl.multiple_of((step - 3) * BLOCK, BLOCK), BLOCK)
        piece = dqkv[:, columns]
        dh1[...] += mm_nt(piece, w_ref[...])
        stage[slot] = mm_tn(h1[...], piece).astype(BF16)

    block_copy(step, slot).start()

    @pl.when(step == 7)
    def _():
        gains = gain_rows(small_ref[...])
        normed_one, inverse_one = norm_of(x_ref[...].astype(F32))
        grad = dh1[...]
        grad_tokens_ref[...] = dx1[...] + norm_back(grad, normed_one, inverse_one, gains[0:1, :])
        normed_two, _ = norm_of(x1_ref[...])
        lane = lax.broadcasted_iota(jnp.int32, (T, LANES), 1)
        total = mm_tn(h2_ref[...], dlogits[...])
        total += mm_tn((grad * normed_one).astype(BF16), (lane == E).astype(BF16))
        total += mm_tn((dh2[...] * normed_two).astype(BF16), (lane == E + 1).astype(BF16))
        small_stage[...] = total.astype(BF16)
        last = pltpu.make_async_copy(small_stage, pack_ref.at[:, pl.ds(4096, LANES)], sems.at[2])
        last.start()
        block_copy(step - 1, 1 - slot).wait()
        block_copy(step, slot).wait()
        last.wait()


def attention_backward(x, x1, h2, dy, gates, place, q, k, v, ob, pack, cosine, signed, parts):
    shape = jax.ShapeDtypeStruct
    return pl.pallas_call(
        attention_backward_kernel,
        grid=(8,),
        in_specs=[
            whole((T, D)),
            whole((T, D)),
            whole((T, D)),
            whole((T, D)),
            whole((T, LANES)),
            whole((PEERS, LANES, LANES)),
            whole((T, D)),
            whole((T, BLOCK)),
            whole((T, BLOCK)),
            whole((T, D)),
            pl.BlockSpec((D, BLOCK), lambda i: (0, lax.rem(i + 5, 8))),
            pl.BlockSpec((D, LANES), lambda i: (0, 4096 // LANES)),
            whole((T, LANES)),
            whole((T, LANES)),
        ]
        + [whole((T, D + LANES))] * PEERS,
        out_specs=[whole((T, D)), pl.BlockSpec(memory_space=pl.ANY)],
        out_shape=[shape((T, D), F32), shape((D, PACK), BF16)],
        scratch_shapes=[
            pltpu.VMEM((T, D), BF16),
            pltpu.VMEM((T, D), BF16),
            pltpu.VMEM((T, D), F32),
            pltpu.VMEM((T, D), F32),
            pltpu.VMEM((T, D), F32),
            pltpu.VMEM((T, BLOCK), F32),
            pltpu.VMEM((T, BLOCK), F32),
            pltpu.VMEM((T, D + 2 * BLOCK), BF16),
            pltpu.VMEM((T, D), F32),
            pltpu.VMEM((T, D), F32),
            pltpu.VMEM((T, LANES), BF16),
            pltpu.VMEM((2, D, BLOCK), BF16),
            pltpu.VMEM((D, LANES), BF16),
            pltpu.SemaphoreType.DMA((3,)),
        ],
        compiler_params=params(),
        cost_estimate=cost(4 * T * D * 4096, 30 << 20),
        name="attention_backward",
    )(x, x1, h2, dy, gates, place, q, k, v, ob, pack, pack, cosine, signed, *parts)


def spread_tables(all_routes, me):
    lane = jnp.arange(LANES, dtype=jnp.int32)
    member = jnp.sum((all_routes[..., None] == lane).astype(F32), axis=2)
    mine = me * LOCAL + jnp.arange(LOCAL, dtype=jnp.int32)
    own = jnp.sum((all_routes[..., None] == mine).astype(F32), axis=2)
    earlier = (np.arange(T)[:, None] > np.arange(T)[None, :]).astype(np.float32)
    before = jnp.einsum(
        "ts,rse->rte", jnp.asarray(earlier, BF16), own.astype(BF16), preferred_element_type=F32
    )
    slots = jnp.where(own > 0.5, before.astype(jnp.int32), -1)
    slots = jnp.swapaxes(slots, 1, 2)[:, :, None, :]
    place = slots == jnp.arange(CAP, dtype=jnp.int32)[None, None, :, None]
    return member, place.astype(BF16).reshape(PEERS, SLOTS, T)


def total_over_peers(share, me):
    wide_share = jnp.pad(share, ((0, 0), (0, PEERS * 640 - share.shape[1])))
    total = jnp.zeros((share.shape[0], 640), F32)
    for hop in range(PEERS):
        piece = lax.dynamic_slice_in_dim(wide_share, peer(me, hop) * 640, 640, 1)
        total = total + send(piece, hop).astype(F32)
    low = total.astype(BF16)
    result = jnp.zeros(wide_share.shape, BF16)
    for hop in range(PEERS):
        result = lax.dynamic_update_slice_in_dim(
            result, send(low, hop), peer(me, hop, True) * 640, 1
        )
    return result[:, : share.shape[1]]


def body(
    tokens,
    cotangent,
    routes,
    norm_one,
    w_query,
    key_weight,
    value_weight,
    w_out,
    norm_two,
    w_router,
    w_gate,
    w_up,
    w_down,
):
    me = lax.axis_index("expert")
    cosine, signed = (jnp.asarray(table) for table in rope_tables())
    rows = norm_one.shape[0]
    small = jnp.concatenate(
        [
            w_router,
            norm_one[:, None],
            norm_two[:, None],
            jnp.zeros((rows, LANES - E - 2), BF16),
        ],
        axis=1,
    )
    pack = lax.all_gather(
        jnp.concatenate([w_query, key_weight, value_weight, w_out, small], axis=1),
        "fsdp",
        axis=0,
        tiled=True,
    )
    expert_pack = lax.all_gather(
        jnp.concatenate([w_gate, w_up, jnp.swapaxes(w_down, 1, 2)], axis=2),
        "fsdp",
        axis=1,
        tiled=True,
    )

    early = jnp.concatenate(
        [cotangent, jnp.pad(routes, ((0, 0), (0, LANES - routes.shape[1]))).astype(BF16)], axis=1
    )
    early_rows = [send(early, hop) for hop in range(PEERS)]
    all_routes = jnp.stack(
        [r[:, D : D + routes.shape[1]].astype(jnp.int32) for r in early_rows]
    )
    member, place = spread_tables(all_routes, me)
    row_expert = me * LOCAL + jnp.arange(SLOTS, dtype=jnp.int32) // CAP
    chosen = (row_expert[:, None] == jnp.arange(LANES, dtype=jnp.int32)[None, :]).astype(F32)
    dyr = spread_rows(place, early_rows).reshape(LOCAL, PEERS * CAP, D)

    lane = jnp.arange(LANES, dtype=jnp.int32)
    homes = jnp.stack([peer(me, hop) for hop in range(PEERS)])[:, None] * LOCAL + (lane % LOCAL)
    homes = jnp.where(lane < 2 * LOCAL, homes, -1)
    back_place = (homes[:, :, None] == lane[None, None, :]).astype(BF16)

    q, k, v, ob, x1, h2 = attention_forward(tokens, pack, cosine, signed)
    h2_rows = [send(h2, hop) for hop in range(PEERS)]
    gates, slot_gate, b = gate_rows(pack, member, chosen, place, h2_rows)
    grad_pack, gy, db = experts(
        b.reshape(LOCAL, PEERS * CAP, D),
        dyr,
        slot_gate.reshape(LOCAL, PEERS * CAP, 1),
        expert_pack,
    )
    db_parts = collect(place, db, "collect_grads")
    parts = [send(db_parts[hop], hop, True) for hop in range(PEERS)]
    gy_parts = collect(place, gy, "collect_results")
    mixed_parts = [send(gy_parts[hop], hop, True) for hop in range(PEERS)]
    mixed_out = mix(x1, mixed_parts)

    expert_share = lax.psum_scatter(grad_pack, "fsdp", scatter_dimension=1, tiled=True)
    grad_tokens, attn_pack = attention_backward(
        tokens, x1, h2, cotangent, gates[0], back_place, q, k, v, ob, pack, cosine, signed, parts
    )
    share = lax.psum_scatter(attn_pack, "fsdp", scatter_dimension=0, tiled=True)
    total = total_over_peers(share, me).astype(F32)

    expert_share = expert_share.astype(F32)
    return (
        mixed_out,
        grad_tokens,
        total[:, 4096 + E],
        total[:, 0:D],
        total[:, D : D + BLOCK],
        total[:, D + BLOCK : D + 2 * BLOCK],
        total[:, D + 2 * BLOCK : 4096],
        total[:, 4096 + E + 1],
        total[:, 4096 : 4096 + E],
        expert_share[:, :, 0:H],
        expert_share[:, :, H : 2 * H],
        jnp.swapaxes(expert_share[:, :, 2 * H :], 1, 2),
    )


def solution(mesh):
    return jax.shard_map(
        body,
        mesh=mesh,
        in_specs=(
            P(("expert", "fsdp"), None),
            P(("expert", "fsdp"), None),
            P(("expert", "fsdp"), None),
            P("fsdp"),
            P("fsdp", None),
            P("fsdp", None),
            P("fsdp", None),
            P("fsdp", None),
            P("fsdp"),
            P("fsdp", None),
            P("expert", "fsdp", None),
            P("expert", "fsdp", None),
            P("expert", None, "fsdp"),
        ),
        out_specs=(
            P(("expert", "fsdp"), None),
            P(("expert", "fsdp"), None),
            P("fsdp"),
            P("fsdp", None),
            P("fsdp", None),
            P("fsdp", None),
            P("fsdp", None),
            P("fsdp"),
            P("fsdp", None),
            P("expert", "fsdp", None),
            P("expert", "fsdp", None),
            P("expert", None, "fsdp"),
        ),
        check_vma=False,
    )
```

```python
import jax
import jax.numpy as jnp
import numpy as np
from jax import lax
from jax.experimental import pallas as pl
from jax.experimental.pallas import tpu as pltpu
from jax.sharding import PartitionSpec as P

QUERY_HEADS = 24
KEY_VALUE_HEADS = 8
GROUP = QUERY_HEADS // KEY_VALUE_HEADS
HEAD_DIM = 64
HALF = HEAD_DIM // 2
E = 40
H = 512
D = 1536
T = 128
CAP = 32
NORM_EPSILON = 1e-05
SCALE = HEAD_DIM ** (-0.5)

Z = 4
PEERS = 8
LOCAL = E // PEERS
SLOTS = LOCAL * CAP
LANES = 128
CHIPS = 8
LINE = 4
TOPK = 8
SHARDS = 2 * CHIPS
ROWS = D // SHARDS
QH = QUERY_HEADS // Z
KH = KEY_VALUE_HEADS // Z
QW = QH * HEAD_DIM
KW = KH * HEAD_DIM
QKV = QW + 2 * KW
MAIN = QW + QKV
SLICE = MAIN + LANES
VMEM_LIMIT = 60 * 1024 * 1024

F32 = jnp.float32
BF16 = jnp.bfloat16


def peer(index, hop, back=False):
    shift = hop % Z
    turned = (index % Z + (Z - shift if back else shift)) % Z
    return (index // Z + hop // Z) % 2 * Z + turned


def send(value, hop, back=False):
    if hop == 0:
        return value
    return lax.ppermute(value, "expert", [(i, peer(i, hop, back)) for i in range(PEERS)])


def chip_at(index, hop, back=False):
    shift = hop % 4
    turned = (index // 2 % 4 + (4 - shift if back else shift)) % 4
    return (index // 8 + hop // 4) % 2 * 4 + turned


def send_chip(value, hop):
    if hop == 0:
        return value
    pairs = [(i, 2 * chip_at(i, hop) + i % 2) for i in range(SHARDS)]
    return lax.ppermute(value, "fsdp", pairs)


def after(value, *others):
    return lax.optimization_barrier((value, others))[0]


def send_across(pair):
    def flip(value, half, low):
        pairs = []
        for index in range(PEERS * SHARDS):
            group, place = index // SHARDS, index % SHARDS
            pairs.append((index, (group ^ (half * Z)) * SHARDS + (place ^ (low * CHIPS))))
        return lax.ppermute(value, ("expert", "fsdp"), pairs)

    return flip(pair[1], 0, 1), flip(pair[0], 1, 0), flip(pair[1], 1, 1)


def swap_core(value):
    return lax.ppermute(value, "fsdp", [(i, i ^ 1) for i in range(SHARDS)])


def mm(left, right):
    return jnp.dot(left, right, preferred_element_type=F32)


def mm_nt(left, right):
    return lax.dot_general(left, right, (((1,), (1,)), ((), ())), preferred_element_type=F32)


def mm_tn(left, right):
    return lax.dot_general(left, right, (((0,), (0,)), ((), ())), preferred_element_type=F32)


def rope_tables():
    frequency = np.exp(-np.log(10000.0) * np.arange(HALF, dtype=np.float64) * 2.0 / HEAD_DIM)
    angles = np.arange(T, dtype=np.float64)[:, None] * frequency[None, :]
    cosine = np.tile(np.cos(angles), (1, 4)).astype(np.float32)
    sine = np.sin(angles)
    signed = np.tile(np.concatenate([-sine, sine], axis=1), (1, 2)).astype(np.float32)
    return cosine, signed


def swap_halves(values):
    width = values.shape[1]
    lane = lax.broadcasted_iota(jnp.int32, values.shape, 1)
    up = pltpu.roll(values, width - HALF, 1)
    down = pltpu.roll(values, HALF, 1)
    return jnp.where(lane % HEAD_DIM < HALF, up, down)


def wide(table, width):
    return jnp.concatenate([table] * (width // LANES), axis=1)


def rotate(values, cosine, signed):
    width = values.shape[1]
    return values * wide(cosine, width) + swap_halves(values) * wide(signed, width)


def rotate_back(values, cosine, signed):
    width = values.shape[1]
    return values * wide(cosine, width) + swap_halves(values * wide(signed, width))


def gain_rows(small):
    pick = lax.broadcasted_iota(jnp.int32, (16, LANES), 1) == (
        lax.broadcasted_iota(jnp.int32, (16, LANES), 0) + E
    )
    return mm_nt(pick.astype(BF16), small)


def norm_of(values):
    inverse = lax.rsqrt(jnp.mean(values * values, axis=-1, keepdims=True) + NORM_EPSILON)
    return values * inverse, inverse


def head(ref, rows, index):
    return ref[rows, index * HEAD_DIM : (index + 1) * HEAD_DIM]


def stack_heads(ref, rows, first):
    return jnp.concatenate([head(ref, rows, first + index) for index in range(GROUP)], axis=0)


def probabilities(query, key):
    scores = mm_nt(query, key) * SCALE
    rows = lax.broadcasted_iota(jnp.int32, scores.shape, 0) % T
    cols = lax.broadcasted_iota(jnp.int32, scores.shape, 1)
    scores = jnp.where(rows >= cols, scores, -jnp.inf)
    exponent = jnp.exp(scores - jnp.max(scores, axis=-1, keepdims=True))
    return exponent / jnp.sum(exponent, axis=-1, keepdims=True)


def whole(shape):
    return pl.BlockSpec(shape, lambda *_: (0,) * len(shape))


SCALARS = pl.BlockSpec(memory_space=pltpu.SMEM)


def params(**more):
    return pltpu.CompilerParams(vmem_limit_bytes=VMEM_LIMIT, **more)


WEIGHT = 60


def cost(flops, moved):
    return pl.CostEstimate(flops=flops * WEIGHT, bytes_accessed=moved * WEIGHT, transcendentals=0)


def shape(dims, kind):
    return jax.ShapeDtypeStruct(dims, kind)


def call(kernel, name, inputs, in_specs, outputs, out_specs=None, scratch=(), flops=0, moved=0):
    in_specs = [whole(v.shape) if spec is None else spec for v, spec in zip(inputs, in_specs)]
    if out_specs is None:
        out_specs = [whole(o.shape) for o in outputs]
    return pl.pallas_call(
        kernel,
        grid=(1,),
        in_specs=in_specs,
        out_specs=out_specs,
        out_shape=outputs,
        scratch_shapes=list(scratch),
        compiler_params=params(),
        cost_estimate=cost(flops, moved),
        name=name,
    )(*inputs)


SMALL_SPEC = pl.BlockSpec((SHARDS, ROWS, LANES), lambda *_: (0, 0, MAIN // LANES))
X_SPEC = pl.BlockSpec((T, D), lambda *_: (0, 0))
DY_SPEC = pl.BlockSpec((T, D), lambda *_: (0, 1))
OUT_SPEC = pl.BlockSpec((SHARDS, ROWS, QW), lambda *_: (0, 0, 0))


def small_of(ref):
    return ref[...].reshape(D, LANES)


def columns_of(index):
    return pl.ds(pl.multiple_of(index * QW, QW), QW)


def pack_kernel(z_ref, out_ref, query_ref, key_ref, value_ref, router_ref, one_ref, two_ref, own_ref):
    own_ref[:, 0:QW] = out_ref[...]
    own_ref[:, QW : 2 * QW] = query_ref[...]
    own_ref[:, 2 * QW : 2 * QW + KW] = key_ref[...]
    own_ref[:, 2 * QW + KW : MAIN] = value_ref[...]
    narrow = [router_ref[...], one_ref[...], two_ref[...], jnp.zeros((LANES - E - 2, ROWS), BF16)]
    own_ref[:, MAIN:] = jnp.concatenate([v.astype(F32) for v in narrow], axis=0).T.astype(BF16)


def pack(z, w_out, w_query, key_weight, value_weight, router, one, two):
    def slice_of(width):
        return pl.BlockSpec((ROWS, width), lambda i, z: (0, z[0]))

    return pl.pallas_call(
        pack_kernel,
        grid_spec=pltpu.PrefetchScalarGridSpec(
            num_scalar_prefetch=1,
            grid=(1,),
            in_specs=[
                slice_of(QW),
                slice_of(QW),
                slice_of(KW),
                slice_of(KW),
                whole((E, ROWS)),
                whole((1, ROWS)),
                whole((1, ROWS)),
            ],
            out_specs=whole((ROWS, SLICE)),
        ),
        out_shape=shape((ROWS, SLICE), BF16),
        compiler_params=params(),
        cost_estimate=cost(ROWS * SLICE, 1 << 20),
        name="pack",
    )(z, w_out, w_query, key_weight, value_weight, router, one, two)


def project_kernel(order_ref, cos_ref, sin_ref, *refs):
    own, other, xs = refs[:LINE], refs[LINE : 2 * LINE], refs[2 * LINE : 2 * LINE + Z]
    w_ref, gains_ref, h1_ref, qkv_ref, ob_ref = refs[2 * LINE + Z :]
    for chip in range(CHIPS):
        w_ref[order_ref[chip]] = own[chip % LINE][chip // LINE]
        w_ref[order_ref[CHIPS + chip]] = other[chip % LINE][chip // LINE]
    gains = gain_rows(w_ref[:, :, MAIN:].reshape(D, LANES))
    gains_ref[...] = gains
    for hop in range(Z):
        normed, _ = norm_of(xs[hop][...].astype(F32))
        h1_ref[hop * T : (hop + 1) * T] = (normed * gains[0:1, :]).astype(BF16)
    pre = mm(h1_ref[...], w_ref[:, :, QW:MAIN].reshape(D, QKV))
    cosine = jnp.concatenate([cos_ref[...]] * Z, axis=0)
    signed = jnp.concatenate([sin_ref[...]] * Z, axis=0)
    qkv_ref[:, 0:QW] = rotate(pre[:, 0:QW], cosine, signed).astype(BF16)
    qkv_ref[:, QW : QW + KW] = rotate(pre[:, QW : QW + KW], cosine, signed).astype(BF16)
    qkv_ref[:, QW + KW :] = pre[:, QW + KW :].astype(BF16)
    for hop in range(Z):
        rows = slice(hop * T, (hop + 1) * T)
        for group in range(KH):
            key, value = head(qkv_ref, rows, QH + group), head(qkv_ref, rows, QH + KH + group)
            query = stack_heads(qkv_ref, rows, group * GROUP)
            result = mm(probabilities(query, key).astype(BF16), value).astype(BF16)
            for index in range(GROUP):
                at = (group * GROUP + index) * HEAD_DIM
                ob_ref[rows, at : at + HEAD_DIM] = result[index * T : (index + 1) * T]


def project(order, cosine, signed, own, other, xs):
    return call(
        project_kernel,
        "project",
        [order, cosine, signed, *own, *other, *xs],
        [SCALARS] + [None] * (2 + 2 * LINE) + [X_SPEC] * Z,
        [
            shape((SHARDS, ROWS, SLICE), BF16),
            shape((16, D), F32),
            shape((Z * T, D), BF16),
            shape((Z * T, QKV), BF16),
            shape((Z * T, QW), BF16),
        ],
        flops=2 * Z * T * D * QKV,
        moved=12 << 20,
    )


def out_project_kernel(peers_ref, w_ref, *refs):
    obs, full_ref, outs = refs[:Z], refs[Z], refs[Z + 1 :]
    total = jnp.zeros((Z * T, QW), F32)
    for hop in range(Z):
        peer_index = peers_ref[hop]
        blocks = [(row - hop) % Z for row in range(Z)]
        rows = jnp.concatenate([obs[hop][b * T : (b + 1) * T, :] for b in blocks], axis=0)
        full_ref[:, columns_of(peer_index)] = rows
        weight = w_ref[pl.ds(peer_index * Z, Z)].reshape(QW, QW)
        total = total + mm(rows, weight)
    for hop in range(Z):
        outs[hop][...] = total[hop * T : (hop + 1) * T].astype(BF16)


def out_project(peers, w, obs):
    return call(
        out_project_kernel,
        "out_project",
        [peers, w, *obs],
        [SCALARS, OUT_SPEC] + [None] * Z,
        [shape((Z * T, D), BF16)] + [shape((T, QW), BF16)] * Z,
        flops=2 * Z * T * D * QW,
        moved=6 << 20,
    )


def cut_out_kernel(peers_ref, w_ref, *outs):
    for hop in range(Z):
        outs[hop][...] = w_ref[pl.ds(peers_ref[hop] * Z, Z)].reshape(QW, QW)


def cut_out(peers, w):
    return call(
        cut_out_kernel,
        "cut_out",
        [peers, w],
        [SCALARS, OUT_SPEC],
        [shape((QW, QW), BF16)] * Z,
        flops=D * QW,
        moved=2 << 20,
    )


def residual_kernel(peers_ref, x_ref, gains_ref, *refs):
    pieces, (x1_ref, h2_ref) = refs[:Z], refs[Z:]
    x1_ref[...] = x_ref[...].astype(F32)
    for hop in range(Z):
        x1_ref[:, columns_of(peers_ref[hop])] += pieces[hop][...].astype(F32)
    normed, _ = norm_of(x1_ref[...])
    h2_ref[...] = (normed * gains_ref[1:2, :]).astype(BF16)


def residual(peers, x, gains, pieces):
    return call(
        residual_kernel,
        "residual",
        [peers, x, gains, *pieces],
        [SCALARS] + [None] * (2 + Z),
        [shape((T, D), F32), shape((T, D), BF16)],
        flops=T * D * 8,
        moved=2 << 20,
    )


def gate_kernel(small_ref, member_ref, chosen_ref, place_ref, *refs):
    rows, (gates_ref, slot_gate_ref, b_ref) = refs[:Z], refs[Z:]
    small = small_of(small_ref)
    for hop in range(Z):
        h2 = rows[hop][...]
        member = member_ref[hop] > 0.5
        logits = jnp.where(member, mm(h2, small), -jnp.inf)
        exponent = jnp.exp(logits - jnp.max(logits, axis=-1, keepdims=True))
        gates = exponent / jnp.sum(exponent, axis=-1, keepdims=True)
        gates_ref[hop] = gates
        high = gates.astype(BF16)
        low = (gates - high.astype(F32)).astype(BF16)
        place = place_ref[hop]
        spread = mm(place, high) + mm(place, low)
        picked = jnp.sum(spread * chosen_ref[...], axis=-1, keepdims=True)
        slot_gate_ref[:, hop] = picked.reshape(LOCAL, CAP, 1)
        b_ref[:, hop] = mm(place, h2).astype(BF16).reshape(LOCAL, CAP, D)


def gate_rows(half, w, member, chosen, place, rows):
    gates, slot_gate, b = call(
        gate_kernel,
        "gate_rows",
        [w, member, chosen, place, *rows],
        [
            SMALL_SPEC,
            pl.BlockSpec((Z, T, LANES), lambda *_: (half, 0, 0)),
            None,
            pl.BlockSpec((Z, SLOTS, T), lambda *_: (half, 0, 0)),
        ]
        + [None] * Z,
        [
            shape((Z, T, LANES), F32),
            shape((LOCAL, Z, CAP, 1), F32),
            shape((LOCAL, Z, CAP, D), BF16),
        ],
        flops=2 * Z * SLOTS * T * D,
        moved=5 << 20,
    )
    return gates, slot_gate.reshape(LOCAL, Z * CAP, 1), b.reshape(LOCAL, Z * CAP, D)


def spread_kernel(place_ref, *refs):
    rows, out_ref = refs[:PEERS], refs[PEERS]
    for hop in range(PEERS):
        out_ref[:, hop] = mm(place_ref[hop], rows[hop][...]).astype(BF16).reshape(LOCAL, CAP, D)


def spread_rows(place, line, other):
    return call(
        spread_kernel,
        "spread_rows",
        [place, *line, *other],
        [None] + [DY_SPEC] * Z + [X_SPEC] * Z,
        [shape((LOCAL, PEERS, CAP, D), BF16)],
        flops=2 * PEERS * SLOTS * T * D,
        moved=8 << 20,
    )[0].reshape(LOCAL, PEERS * CAP, D)


def expert_kernel(
    me_ref, b0_ref, b1_ref, dyr_ref, gate0_ref, gate1_ref, w_ref, gy_ref, db_ref, grad_ref
):
    rows = jnp.concatenate([b0_ref[0], b1_ref[0]], axis=0)
    gate = jnp.concatenate([gate0_ref[0], gate1_ref[0]], axis=0)
    down = w_ref[0, :, 2 * H : 3 * H]
    pre = mm(rows, w_ref[0, :, 0 : 2 * H])
    gate_pre, up_pre = pre[:, :H], pre[:, H:]
    sigmoid = 1.0 / (1.0 + jnp.exp(-gate_pre))
    silu = gate_pre * sigmoid
    activated = (silu * up_pre).astype(BF16)
    result = mm_nt(activated, down).astype(BF16).astype(F32)
    raw = dyr_ref[0].astype(F32)
    gy_ref[0] = (gate * result).astype(BF16)
    inner = jnp.sum(raw * result, axis=-1, keepdims=True)
    grad_rows = (gate * raw).astype(BF16)
    grad_act = mm(grad_rows, down)
    grad_ref[0, :, 2 * H : 3 * H] = mm_tn(grad_rows, activated).astype(BF16)
    grad_gate = (grad_act * up_pre * sigmoid * (1.0 + gate_pre * (1.0 - sigmoid))).astype(BF16)
    grad_up = (grad_act * silu).astype(BF16)
    both = jnp.concatenate([grad_gate, grad_up], axis=1)
    db_ref[0, :, 0:D] = mm_nt(both, w_ref[0, :, 0 : 2 * H]).astype(BF16)
    grad_ref[0, :, 0 : 2 * H] = mm_tn(rows, both).astype(BF16)
    expert = me_ref[0] * LOCAL + pl.program_id(0)
    lane = lax.broadcasted_iota(jnp.int32, (PEERS * CAP, LANES), 1)
    high = inner.astype(BF16).astype(F32)
    low = inner - high
    tail = jnp.where(lane == expert, high, jnp.where(lane == expert + E, low, 0.0))
    db_ref[0, :, D : D + LANES] = tail.astype(BF16)


def per_expert(*dims):
    return pl.BlockSpec((1,) + dims, lambda e: (e, 0, 0))


def experts(me, b, dyr, slot_gate, pack):
    rows = PEERS * CAP
    return pl.pallas_call(
        expert_kernel,
        grid=(LOCAL,),
        in_specs=[
            SCALARS,
            per_expert(rows // 2, D),
            per_expert(rows // 2, D),
            per_expert(rows, D),
            per_expert(rows // 2, 1),
            per_expert(rows // 2, 1),
            per_expert(D, 3 * H),
        ],
        out_specs=[
            per_expert(rows, D),
            per_expert(rows, D + LANES),
            per_expert(D, 3 * H),
        ],
        out_shape=[
            shape((LOCAL, rows, D), BF16),
            shape((LOCAL, rows, D + LANES), BF16),
            shape((LOCAL, D, 3 * H), BF16),
        ],
        compiler_params=params(),
        cost_estimate=cost(18 * LOCAL * rows * D * H, 60 << 20),
        name="experts",
    )(me, *b, dyr, *slot_gate, pack)


def collect_kernel(place_ref, value_ref, *out_refs):
    for hop in range(PEERS):
        rows = value_ref[:, hop].reshape(SLOTS, value_ref.shape[-1])
        out_refs[hop][...] = mm_tn(place_ref[hop], rows).astype(BF16)


def collect(place, values, name):
    width = values.shape[-1]
    return call(
        collect_kernel,
        name,
        [place, values.reshape(LOCAL, PEERS, CAP, width)],
        [None, None],
        [shape((T, width), BF16)] * PEERS,
        flops=2 * PEERS * SLOTS * T * width,
        moved=8 << 20,
    )


def mix(x1, returns, other):
    return call(
        add_kernel,
        "mix",
        [x1, *returns, other],
        [None] + [DY_SPEC] * Z + [None],
        [shape((T, D), BF16)],
        flops=T * D * Z,
        moved=4 << 20,
    )[0]


def norm_back(grad, normed, inverse, gain):
    scaled = grad * gain
    return inverse * (scaled - normed * jnp.mean(scaled * normed, axis=-1, keepdims=True))


def token_back_kernel(
    x1_ref, dy_ref, gates_ref, small_ref, gains_ref, *refs
):
    parts, (dx1_ref, dlogits_ref, scaled_ref, da_ref) = refs[: Z + 1], refs[Z + 1 :]
    total = parts[0][...].astype(F32)
    for ref in parts[1:]:
        total = total + ref[...].astype(F32)
    grad, tail = total[:, :D], total[:, D:]
    lane = lax.broadcasted_iota(jnp.int32, (T, LANES), 1)
    inner = jnp.where(lane < E, tail + pltpu.roll(tail, LANES - E, 1), 0.0)
    gates = gates_ref[0]
    score = gates * (inner - jnp.sum(gates * inner, axis=-1, keepdims=True))
    dlogits_ref[...] = score.astype(BF16)
    grad = grad + mm_nt(dlogits_ref[...], small_of(small_ref))
    normed, inverse = norm_of(x1_ref[...])
    scaled_ref[...] = (grad * normed).astype(BF16)
    through = dy_ref[...].astype(F32) + norm_back(grad, normed, inverse, gains_ref[1:2, :])
    dx1_ref[...] = through
    da_ref[...] = through.astype(BF16)


def token_back(x1, dy, gates, w, gains, parts):
    return call(
        token_back_kernel,
        "token_back",
        [x1, dy, gates, w, gains, *parts],
        [None, None, pl.BlockSpec((1, T, LANES), lambda *_: (0, 0, 0)), SMALL_SPEC]
        + [None] * (1 + len(parts)),
        [
            shape((T, D), F32),
            shape((T, LANES), BF16),
            shape((T, D), BF16),
            shape((T, D), BF16),
        ],
        flops=T * D * 64,
        moved=6 << 20,
    )


def shadow_kernel(qkv_ref, h2_ref, dlogits_ref, scaled_ref, *refs):
    xs, (small_ref, inverse_ref, prob_ref) = refs[:Z], refs[Z:]
    lane = lax.broadcasted_iota(jnp.int32, (T, LANES), 1)
    small = mm_tn(h2_ref[...], dlogits_ref[...])
    small_ref[...] = small + mm_tn(scaled_ref[...], (lane == E + 1).astype(BF16))
    for hop in range(Z):
        rows = slice(hop * T, (hop + 1) * T)
        _, inverse = norm_of(xs[hop][...].astype(F32))
        inverse_ref[rows] = inverse
        for group in range(KH):
            query = stack_heads(qkv_ref, rows, group * GROUP)
            prob_ref[hop * KH + group] = probabilities(query, head(qkv_ref, rows, QH + group))


def shadow(qkv, h2, dlogits, scaled, xs):
    return call(
        shadow_kernel,
        "shadow",
        [qkv, h2, dlogits, scaled, *xs],
        [None] * 4 + [X_SPEC] * Z,
        [
            shape((D, LANES), F32),
            shape((Z * T, 1), F32),
            shape((Z * KH, GROUP * T, T), F32),
        ],
        flops=Z * T * D * QW,
        moved=6 << 20,
    )


def head_back_kernel(
    behind_ref,
    parity_ref,
    qkv_ref,
    h1_ref,
    w_ref,
    full_ref,
    partial_ref,
    inverse_ref,
    prob_ref,
    cos_ref,
    sin_ref,
    *refs,
):
    xs, das, weights, results, outs = (refs[at * Z : at * Z + Z] for at in range(5))
    keep_ref, give_ref, dob, dqk, dqkv = refs[5 * Z :]
    total = jnp.zeros((Z * T, QW), F32)
    for hop in range(Z):
        columns = columns_of(behind_ref[hop])
        rows = jnp.concatenate([ref[:, columns] for ref in das], axis=0)
        total = total + mm_nt(rows, weights[hop][...])
        if hop == 0:
            own_columns = rows
    dob[...] = total.astype(BF16)
    for hop in range(Z):
        rows = slice(hop * T, (hop + 1) * T)
        for group in range(KH):
            key, value = head(qkv_ref, rows, QH + group), head(qkv_ref, rows, QH + KH + group)
            query = stack_heads(qkv_ref, rows, group * GROUP)
            out_grad = stack_heads(dob, rows, group * GROUP)
            probability = prob_ref[hop * KH + group]
            grad_prob = mm_nt(out_grad, value)
            held = jnp.sum(probability * grad_prob, axis=-1, keepdims=True)
            grad_scores = (probability * (grad_prob - held)).astype(BF16)
            grad_query = mm(grad_scores, key) * SCALE
            for index in range(GROUP):
                at = (group * GROUP + index) * HEAD_DIM
                dqk[rows, at : at + HEAD_DIM] = grad_query[index * T : (index + 1) * T]
            at = QW + group * HEAD_DIM
            dqk[rows, at : at + HEAD_DIM] = mm_tn(grad_scores, query) * SCALE
            dqkv[rows, at + KW : at + KW + HEAD_DIM] = mm_tn(
                probability.astype(BF16), out_grad
            ).astype(BF16)
    cosine = jnp.concatenate([cos_ref[...]] * Z, axis=0)
    signed = jnp.concatenate([sin_ref[...]] * Z, axis=0)
    dqkv[:, 0 : QW + KW] = rotate_back(dqk[...], cosine, signed).astype(BF16)
    even = parity_ref[0] == 0

    def store(grads, columns):
        pair = grads.astype(BF16).reshape(CHIPS, 2, ROWS, grads.shape[1])
        keep_ref[:, :, columns] = jnp.where(even, pair[:, 0], pair[:, 1])
        give_ref[:, :, columns] = jnp.where(even, pair[:, 1], pair[:, 0])

    store(mm_tn(full_ref[...], own_columns), slice(0, QW))
    store(mm_tn(h1_ref[...], dqkv[...]), slice(QW, MAIN))
    dh1 = mm_nt(dqkv[...], w_ref[:, :, QW:MAIN].reshape(D, QKV))
    lane = lax.broadcasted_iota(jnp.int32, (T, LANES), 1)
    first = (lane == E).astype(BF16)
    small = partial_ref[...]
    for hop in range(Z):
        rows = slice(hop * T, (hop + 1) * T)
        piece = dh1[rows]
        normed = xs[hop][...].astype(F32) * inverse_ref[rows]
        small += mm_tn((piece * normed).astype(BF16), first)
        outs[hop][:, 0:D] = piece.astype(BF16)
        outs[hop][:, D:] = results[hop][...]
    store(small, slice(MAIN, SLICE))


def head_back(behind, parity, qkv, h1, w, full, shadows, cosine, signed, xs, das, weights, results):
    return call(
        head_back_kernel,
        "head_back",
        [behind, parity, qkv, h1, w, full, *shadows, cosine, signed, *xs, *das, *weights, *results],
        [SCALARS] * 2 + [None] * 9 + [X_SPEC] * Z + [None] * (3 * Z),
        [shape((T, 2 * D), BF16)] * Z + [shape((CHIPS, ROWS, SLICE), BF16)] * 2,
        scratch=[
            pltpu.VMEM((Z * T, QW), BF16),
            pltpu.VMEM((Z * T, QW + KW), F32),
            pltpu.VMEM((Z * T, QKV), BF16),
        ],
        flops=4 * Z * T * D * QKV,
        moved=16 << 20,
    )


def token_grad_kernel(x_ref, gains_ref, dx1_ref, *refs):
    grad = refs[0][...].astype(F32)
    for hop in range(1, Z):
        grad = grad + refs[hop][...].astype(F32)
    normed, inverse = norm_of(x_ref[...].astype(F32))
    refs[Z][...] = dx1_ref[...] + norm_back(grad, normed, inverse, gains_ref[0:1, :])


def token_grad(x, gains, dx1, pieces):
    return call(
        token_grad_kernel,
        "token_grad",
        [x, gains, dx1, *pieces],
        [None] * 3 + [X_SPEC] * Z,
        [shape((T, D), F32)],
        flops=T * D * 16,
        moved=4 << 20,
    )[0]


def split_kernel(order_ref, keep_ref, got_ref, *outs):
    for chip in range(CHIPS):
        at = order_ref[chip]
        total = (keep_ref[at].astype(F32) + got_ref[at].astype(F32)).astype(BF16)
        outs[chip % 4][chip // 4] = total


def split(order, keep, got):
    return call(
        split_kernel,
        "split",
        [order, keep, got],
        [SCALARS, None, None],
        [shape((2, ROWS, SLICE), BF16)] * 4,
        flops=CHIPS * ROWS * SLICE,
        moved=6 << 20,
    )


def add_kernel(*refs):
    total = refs[0][...].astype(F32)
    for ref in refs[1:-1]:
        total = total + ref[...].astype(F32)
    refs[-1][...] = total.astype(BF16)


def add_all(parts, name):
    return call(
        add_kernel,
        name,
        list(parts),
        [None] * len(parts),
        [shape(parts[0].shape, BF16)],
        flops=parts[0].size * len(parts),
        moved=2 * parts[0].size * (len(parts) + 1),
    )[0]


def across_kernel(a_ref, b_ref, c_ref, d_ref, out_ref):
    here = a_ref[...].astype(F32) + b_ref[...].astype(F32)
    there = c_ref[...].astype(F32) + d_ref[...].astype(F32)
    out_ref[...] = (here + there).astype(BF16)


def sum_across(parts):
    return call(
        across_kernel,
        "sum_across",
        list(parts),
        [None] * 4,
        [shape((ROWS, SLICE), BF16)],
        flops=4 * ROWS * SLICE,
        moved=10 * ROWS * SLICE,
    )[0]


def finish_kernel(order_ref, *refs):
    parts, (q_ref, k_ref, v_ref, o_ref, small_ref, narrow) = refs[:Z], refs[Z:]
    for hop in range(Z):
        at = order_ref[hop]
        part = parts[hop][...].astype(F32)
        o_ref[:, columns_of(at)] = part[:, 0:QW]
        q_ref[:, columns_of(at)] = part[:, QW : 2 * QW]
        heads = pl.ds(pl.multiple_of(at * KW, KW), KW)
        k_ref[:, heads] = part[:, 2 * QW : 2 * QW + KW]
        v_ref[:, heads] = part[:, 2 * QW + KW : MAIN]
        narrow[at] = part[:, MAIN:]
    small_ref[...] = (narrow[0] + narrow[1] + narrow[2] + narrow[3]).T


def finish(order, parts):
    return call(
        finish_kernel,
        "finish",
        [order, *parts],
        [SCALARS] + [None] * Z,
        [
            shape((ROWS, D), F32),
            shape((ROWS, KEY_VALUE_HEADS * HEAD_DIM), F32),
            shape((ROWS, KEY_VALUE_HEADS * HEAD_DIM), F32),
            shape((ROWS, D), F32),
            shape((LANES, ROWS), F32),
        ],
        scratch=[pltpu.VMEM((Z, ROWS, LANES), F32)],
        flops=ROWS * SLICE * Z,
        moved=3 << 20,
    )


def unpack_kernel(share_ref, gate_ref, up_ref, down_ref):
    value = share_ref[0].astype(F32)
    gate_ref[0] = value[:, 0:H]
    up_ref[0] = value[:, H : 2 * H]
    down_ref[0] = value[:, 2 * H :]


def unpack(share):
    return pl.pallas_call(
        unpack_kernel,
        grid=(LOCAL,),
        in_specs=[per_expert(ROWS, 3 * H)],
        out_specs=[per_expert(ROWS, H)] * 3,
        out_shape=[shape((LOCAL, ROWS, H), F32)] * 3,
        compiler_params=params(),
        cost_estimate=cost(LOCAL * ROWS * 3 * H, 5 << 20),
        name="unpack",
    )(share)


def spread_tables(all_routes, me):
    lane = jnp.arange(LANES, dtype=jnp.int32)
    member = jnp.sum((all_routes[..., None] == lane).astype(F32), axis=2)
    mine = me * LOCAL + jnp.arange(LOCAL, dtype=jnp.int32)
    own = jnp.sum((all_routes[..., None] == mine).astype(F32), axis=2)
    earlier = (np.arange(T)[:, None] > np.arange(T)[None, :]).astype(np.float32)
    before = jnp.einsum(
        "ts,rse->rte", jnp.asarray(earlier, BF16), own.astype(BF16), preferred_element_type=F32
    )
    slots = jnp.where(own > 0.5, before.astype(jnp.int32), -1)
    slots = jnp.swapaxes(slots, 1, 2)[:, :, None, :]
    place = slots == jnp.arange(CAP, dtype=jnp.int32)[None, None, :, None]
    return member, place.astype(BF16).reshape(PEERS, SLOTS, T)


def body(
    tokens,
    cotangent,
    routes,
    norm_one,
    w_query,
    key_weight,
    value_weight,
    w_out,
    norm_two,
    w_router,
    w_gate,
    w_up,
    w_down,
):
    me = lax.axis_index("expert")
    place_in_group = lax.axis_index("fsdp")
    z = me % Z
    core = place_in_group % 2
    cosine, signed = (jnp.asarray(table) for table in rope_tables())

    own = pack(
        z.astype(jnp.int32)[None],
        w_out,
        w_query,
        key_weight,
        value_weight,
        w_router.T,
        norm_one[None, :],
        norm_two[None, :],
    )
    pair = jnp.stack([own, send_chip(own, LINE)])
    own = [send_chip(pair, hop) for hop in range(LINE)]
    other = [swap_core(value) for value in own]
    sources = jnp.stack([chip_at(place_in_group, hop, True) for hop in range(CHIPS)])
    order = jnp.concatenate([2 * sources + core, 2 * sources + 1 - core]).astype(jnp.int32)
    expert_pack = lax.all_gather(
        jnp.concatenate([w_gate, w_up, jnp.swapaxes(w_down, 1, 2)], axis=2),
        "fsdp",
        axis=1,
        tiled=True,
    )

    behind = jnp.stack([(z + Z - hop) % Z for hop in range(Z)]).astype(jnp.int32)
    ahead = jnp.stack([(z + hop) % Z for hop in range(Z)]).astype(jnp.int32)

    marks = jnp.pad(routes, ((0, 0), (0, LANES - TOPK))).astype(BF16)
    early = jnp.concatenate([cotangent, marks], axis=1)
    whole_row = jnp.concatenate([tokens, early], axis=1)
    xs = [send(whole_row, hop) for hop in (0, 1, 3)]
    xs.insert(2, send(after(whole_row, xs[1]), 2))
    w, gains, h1, qkv, ob = project(order, cosine, signed, own, other, xs)
    obs = [send(ob, hop) for hop in range(Z)]
    early_other = send(after(early, xs[3]), Z)
    early_other = after(early_other, *obs[1:])
    early_other = [send(early_other, hop) for hop in range(Z)]
    ob_full, *x1_columns = out_project(behind, w, obs)
    x1_pieces = [send(x1_columns[hop], hop, True) for hop in range(Z)]
    x1, h2 = residual(ahead, tokens, gains, x1_pieces)
    h2_other = send(h2, Z)
    h2_line = [send(h2, hop) for hop in range(Z)]
    h2_other = [send(h2_other, hop) for hop in range(Z)]

    all_routes = jnp.stack(
        [r[:, 2 * D : 2 * D + TOPK].astype(jnp.int32) for r in xs]
        + [r[:, D : D + TOPK].astype(jnp.int32) for r in early_other]
    )
    member, place = spread_tables(all_routes, me)
    row_expert = me * LOCAL + jnp.arange(SLOTS, dtype=jnp.int32) // CAP
    chosen = (row_expert[:, None] == jnp.arange(LANES, dtype=jnp.int32)[None, :]).astype(F32)
    dyr = spread_rows(place, xs, early_other)

    gates, gate0, b0 = gate_rows(0, w, member, chosen, place, h2_line)
    _, gate1, b1 = gate_rows(1, w, member, chosen, place, h2_other)
    b, slot_gate = (b0, b1), (gate0, gate1)
    weights = after(cut_out(ahead, after(w, x1)), b1)
    slot_gate = after(slot_gate, *weights)
    weights = [send(weights[hop], hop) for hop in range(Z)]
    gy, db, grad_pack = experts(me.astype(jnp.int32)[None], b, dyr, slot_gate, expert_pack)
    db_parts = collect(place, after(db, *weights[1:]), "collect_grads")
    grad_cross = [send(db_parts[Z + hop], hop, True) for hop in range(Z)]
    grad_line = after(db_parts[:Z], *grad_cross[1:])
    grad_line = [send(grad_line[hop], hop, True) for hop in range(Z)]
    grad_other = send(add_all(grad_cross, "line_grads"), Z)
    expert_share = lax.psum_scatter(
        after(grad_pack, *weights[1:]), "fsdp", scatter_dimension=1, tiled=True
    )
    results = collect(place, gy, "collect_results")
    grad_line = after(grad_line, results)
    dx1, dlogits, scaled, da = token_back(x1, cotangent, gates, w, gains, [*grad_line, grad_other])
    das = [send(da, hop) for hop in range(Z)]
    shadows = shadow(qkv, h2, dlogits, scaled, xs)
    results = after(results, *das[1:])
    results_cross = [send(results[Z + hop], hop, True) for hop in range(Z)]
    *returns, keep, give = head_back(
        behind,
        core.astype(jnp.int32)[None],
        qkv,
        h1,
        w,
        ob_full,
        shadows,
        cosine,
        signed,
        xs,
        das,
        weights,
        results[:Z],
    )
    dests = jnp.stack([chip_at(place_in_group, hop) for hop in range(CHIPS)]).astype(jnp.int32)
    parts = split(dests, keep, swap_core(after(give, *results_cross[1:])))
    lines = [send_chip(parts[hop], hop) for hop in range(LINE)]
    results_other = send(add_all(results_cross, "line_results"), Z)
    first, third = send(returns[1], 1, True), send(returns[3], 3, True)
    lines[0] = after(lines[0], first, third)
    second = send(after(returns[2], first, third), 2, True)
    returns = [returns[0], first, second, third]
    share = add_all(lines, "sum_lines")
    share = sum_across([share[0], *send_across(share)])
    share = after(share, second)
    shares = [send(share, hop) for hop in range(Z)]
    grad_gate, grad_up, grad_down = unpack(expert_share)
    grad_tokens = token_grad(tokens, gains, dx1, returns)
    mixed_out = mix(x1, returns, results_other)
    shares = after(shares, grad_tokens, mixed_out, grad_gate)
    grad_query, grad_key, grad_value, grad_out, narrow = finish(behind, shares)

    return (
        mixed_out,
        grad_tokens,
        narrow[E],
        grad_query,
        grad_key,
        grad_value,
        grad_out,
        narrow[E + 1],
        narrow[0:E].T,
        grad_gate,
        grad_up,
        jnp.swapaxes(grad_down, 1, 2),
    )


def solution(mesh):
    return jax.shard_map(
        body,
        mesh=mesh,
        in_specs=(
            P(("expert", "fsdp"), None),
            P(("expert", "fsdp"), None),
            P(("expert", "fsdp"), None),
            P("fsdp"),
            P("fsdp", None),
            P("fsdp", None),
            P("fsdp", None),
            P("fsdp", None),
            P("fsdp"),
            P("fsdp", None),
            P("expert", "fsdp", None),
            P("expert", "fsdp", None),
            P("expert", None, "fsdp"),
        ),
        out_specs=(
            P(("expert", "fsdp"), None),
            P(("expert", "fsdp"), None),
            P("fsdp"),
            P("fsdp", None),
            P("fsdp", None),
            P("fsdp", None),
            P("fsdp", None),
            P("fsdp"),
            P("fsdp", None),
            P("expert", "fsdp", None),
            P("expert", "fsdp", None),
            P("expert", None, "fsdp"),
        ),
        check_vma=False,
    )
```

```python
import jax
import jax.numpy as jnp
import numpy as np
from jax import lax
from jax.experimental import pallas as pl
from jax.experimental.pallas import tpu as pltpu
from jax.sharding import PartitionSpec as P

QUERY_HEADS = 24
KEY_VALUE_HEADS = 8
GROUP = QUERY_HEADS // KEY_VALUE_HEADS
HEAD_DIM = 64
HALF = HEAD_DIM // 2
E = 40
H = 512
D = 1536
T = 128
CAP = 32
NORM_EPSILON = 1e-05
SCALE = HEAD_DIM ** (-0.5)

Z = 4
PEERS = 8
LOCAL = E // PEERS
SLOTS = LOCAL * CAP
EXTRA = 1
PLAIN = LOCAL - EXTRA
LANES = 128
CHIPS = 8
LINE = 4
TOPK = 8
SHARDS = 2 * CHIPS
ROWS = D // SHARDS
QH = QUERY_HEADS // Z
KH = KEY_VALUE_HEADS // Z
QW = QH * HEAD_DIM
KW = KH * HEAD_DIM
QKV = QW + 2 * KW
MAIN = QW + QKV
SLICE = MAIN + LANES
VMEM_LIMIT = 60 * 1024 * 1024

F32 = jnp.float32
BF16 = jnp.bfloat16


def peer(index, hop, back=False):
    shift = hop % Z
    turned = (index % Z + (Z - shift if back else shift)) % Z
    return (index // Z + hop // Z) % 2 * Z + turned


def send(value, hop, back=False):
    if hop == 0:
        return value
    return lax.ppermute(value, "expert", [(i, peer(i, hop, back)) for i in range(PEERS)])


def chip_at(index, hop, back=False):
    shift = hop % 4
    turned = (index // 2 % 4 + (4 - shift if back else shift)) % 4
    return (index // 8 + hop // 4) % 2 * 4 + turned


def send_chip(value, hop):
    if hop == 0:
        return value
    pairs = [(i, 2 * chip_at(i, hop) + i % 2) for i in range(SHARDS)]
    return lax.ppermute(value, "fsdp", pairs)


def after(value, *others):
    return lax.optimization_barrier((value, others))[0]


def swap_core(value):
    return lax.ppermute(value, "fsdp", [(i, i ^ 1) for i in range(SHARDS)])


def mm(left, right):
    return jnp.dot(left, right, preferred_element_type=F32)


def mm_nt(left, right):
    return lax.dot_general(left, right, (((1,), (1,)), ((), ())), preferred_element_type=F32)


def mm_tn(left, right):
    return lax.dot_general(left, right, (((0,), (0,)), ((), ())), preferred_element_type=F32)


def rope_tables():
    frequency = np.exp(-np.log(10000.0) * np.arange(HALF, dtype=np.float64) * 2.0 / HEAD_DIM)
    angles = np.arange(T, dtype=np.float64)[:, None] * frequency[None, :]
    cosine = np.tile(np.cos(angles), (1, 4)).astype(np.float32)
    sine = np.sin(angles)
    signed = np.tile(np.concatenate([-sine, sine], axis=1), (1, 2)).astype(np.float32)
    return cosine, signed


def swap_halves(values):
    width = values.shape[1]
    lane = lax.broadcasted_iota(jnp.int32, values.shape, 1)
    up = pltpu.roll(values, width - HALF, 1)
    down = pltpu.roll(values, HALF, 1)
    return jnp.where(lane % HEAD_DIM < HALF, up, down)


def wide(table, width):
    return jnp.concatenate([table] * (width // LANES), axis=1)


def rotate(values, cosine, signed):
    width = values.shape[1]
    return values * wide(cosine, width) + swap_halves(values) * wide(signed, width)


def rotate_back(values, cosine, signed):
    width = values.shape[1]
    return values * wide(cosine, width) + swap_halves(values * wide(signed, width))


def gain_rows(small):
    pick = lax.broadcasted_iota(jnp.int32, (16, LANES), 1) == (
        lax.broadcasted_iota(jnp.int32, (16, LANES), 0) + E
    )
    return mm_nt(pick.astype(BF16), small)


def norm_of(values):
    inverse = lax.rsqrt(jnp.mean(values * values, axis=-1, keepdims=True) + NORM_EPSILON)
    return values * inverse, inverse


def head(ref, rows, index):
    return ref[rows, index * HEAD_DIM : (index + 1) * HEAD_DIM]


def stack_heads(ref, rows, first):
    return jnp.concatenate([head(ref, rows, first + index) for index in range(GROUP)], axis=0)


def probabilities(query, key):
    scores = mm_nt(query, key) * SCALE
    rows = lax.broadcasted_iota(jnp.int32, scores.shape, 0) % T
    cols = lax.broadcasted_iota(jnp.int32, scores.shape, 1)
    scores = jnp.where(rows >= cols, scores, -jnp.inf)
    exponent = jnp.exp(scores - jnp.max(scores, axis=-1, keepdims=True))
    return exponent / jnp.sum(exponent, axis=-1, keepdims=True)


def whole(shape):
    return pl.BlockSpec(shape, lambda *_: (0,) * len(shape))


SCALARS = pl.BlockSpec(memory_space=pltpu.SMEM)


def params(**more):
    return pltpu.CompilerParams(vmem_limit_bytes=VMEM_LIMIT, **more)


WEIGHT = 60


def cost(flops, moved):
    return pl.CostEstimate(flops=flops * WEIGHT, bytes_accessed=moved * WEIGHT, transcendentals=0)


def shape(dims, kind):
    return jax.ShapeDtypeStruct(dims, kind)


def call(kernel, name, inputs, in_specs, outputs, out_specs=None, scratch=(), flops=0, moved=0):
    in_specs = [whole(v.shape) if spec is None else spec for v, spec in zip(inputs, in_specs)]
    if out_specs is None:
        out_specs = [whole(o.shape) for o in outputs]
    return pl.pallas_call(
        kernel,
        grid=(1,),
        in_specs=in_specs,
        out_specs=out_specs,
        out_shape=outputs,
        scratch_shapes=list(scratch),
        compiler_params=params(),
        cost_estimate=cost(flops, moved),
        name=name,
    )(*inputs)


SMALL_SPEC = pl.BlockSpec((SHARDS, ROWS, LANES), lambda *_: (0, 0, QKV // LANES))
X_SPEC = pl.BlockSpec((T, D), lambda *_: (0, 0))
DY_SPEC = pl.BlockSpec((T, D), lambda *_: (0, 1))


def small_of(ref):
    return ref[...].reshape(D, LANES)


def columns_of(index):
    return pl.ds(pl.multiple_of(index * QW, QW), QW)


def pack_kernel(
    z_ref, out_ref, query_ref, key_ref, value_ref, router_ref, one_ref, two_ref, first_ref, second_ref
):
    first_ref[:, 0:QW] = query_ref[...]
    first_ref[:, QW : QW + KW] = key_ref[...]
    first_ref[:, QW + KW : QKV] = value_ref[...]
    narrow = [router_ref[...], one_ref[...], two_ref[...], jnp.zeros((LANES - E - 2, ROWS), BF16)]
    first_ref[:, QKV:] = jnp.concatenate([v.astype(F32) for v in narrow], axis=0).T.astype(BF16)
    second_ref[...] = out_ref[...]


def pack(z, w_out, w_query, key_weight, value_weight, router, one, two):
    def slice_of(width):
        return pl.BlockSpec((ROWS, width), lambda i, z: (0, z[0]))

    return pl.pallas_call(
        pack_kernel,
        grid_spec=pltpu.PrefetchScalarGridSpec(
            num_scalar_prefetch=1,
            grid=(1,),
            in_specs=[
                slice_of(QW),
                slice_of(QW),
                slice_of(KW),
                slice_of(KW),
                whole((E, ROWS)),
                whole((1, ROWS)),
                whole((1, ROWS)),
            ],
            out_specs=[whole((ROWS, QKV + LANES)), whole((ROWS, QW))],
        ),
        out_shape=[shape((ROWS, QKV + LANES), BF16), shape((ROWS, QW), BF16)],
        compiler_params=params(),
        cost_estimate=cost(ROWS * SLICE, 1 << 20),
        name="pack",
    )(z, w_out, w_query, key_weight, value_weight, router, one, two)


def project_kernel(order_ref, cos_ref, sin_ref, *refs):
    own, other, xs = refs[:LINE], refs[LINE : 2 * LINE], refs[2 * LINE : 2 * LINE + Z]
    w_ref, gains_ref, h1_ref, qkv_ref, ob_ref = refs[2 * LINE + Z :]
    for chip in range(CHIPS):
        w_ref[order_ref[chip]] = own[chip % LINE][chip // LINE]
        w_ref[order_ref[CHIPS + chip]] = other[chip % LINE][chip // LINE]
    gains = gain_rows(w_ref[:, :, QKV:].reshape(D, LANES))
    gains_ref[...] = gains
    for hop in range(Z):
        normed, _ = norm_of(xs[hop][...].astype(F32))
        h1_ref[hop * T : (hop + 1) * T] = (normed * gains[0:1, :]).astype(BF16)
    pre = mm(h1_ref[...], w_ref[:, :, 0:QKV].reshape(D, QKV))
    cosine = jnp.concatenate([cos_ref[...]] * Z, axis=0)
    signed = jnp.concatenate([sin_ref[...]] * Z, axis=0)
    qkv_ref[:, 0:QW] = rotate(pre[:, 0:QW], cosine, signed).astype(BF16)
    qkv_ref[:, QW : QW + KW] = rotate(pre[:, QW : QW + KW], cosine, signed).astype(BF16)
    qkv_ref[:, QW + KW :] = pre[:, QW + KW :].astype(BF16)
    for hop in range(Z):
        rows = slice(hop * T, (hop + 1) * T)
        for group in range(KH):
            key, value = head(qkv_ref, rows, QH + group), head(qkv_ref, rows, QH + KH + group)
            query = stack_heads(qkv_ref, rows, group * GROUP)
            result = mm(probabilities(query, key).astype(BF16), value).astype(BF16)
            for index in range(GROUP):
                at = (group * GROUP + index) * HEAD_DIM
                ob_ref[rows, at : at + HEAD_DIM] = result[index * T : (index + 1) * T]


def project(order, cosine, signed, own, other, xs):
    return call(
        project_kernel,
        "project",
        [order, cosine, signed, *own, *other, *xs],
        [SCALARS] + [None] * (2 + 2 * LINE) + [X_SPEC] * Z,
        [
            shape((SHARDS, ROWS, QKV + LANES), BF16),
            shape((16, D), F32),
            shape((Z * T, D), BF16),
            shape((Z * T, QKV), BF16),
            shape((Z * T, QW), BF16),
        ],
        flops=2 * Z * T * D * QKV,
        moved=12 << 20,
    )


def out_project_kernel(peers_ref, order_ref, *refs):
    own, other, obs = refs[:LINE], refs[LINE : 2 * LINE], refs[2 * LINE : 2 * LINE + Z]
    w_ref, full_ref, *outs = refs[2 * LINE + Z :]
    for chip in range(CHIPS):
        w_ref[order_ref[chip]] = own[chip % LINE][chip // LINE]
        w_ref[order_ref[CHIPS + chip]] = other[chip % LINE][chip // LINE]
    total = jnp.zeros((Z * T, QW), F32)
    for hop in range(Z):
        peer_index = peers_ref[hop]
        blocks = [(row - hop) % Z for row in range(Z)]
        rows = jnp.concatenate([obs[hop][b * T : (b + 1) * T, :] for b in blocks], axis=0)
        full_ref[:, columns_of(peer_index)] = rows
        weight = w_ref[pl.ds(peer_index * Z, Z)].reshape(QW, QW)
        total = total + mm(rows, weight)
    for hop in range(Z):
        outs[hop][...] = total[hop * T : (hop + 1) * T].astype(BF16)


def out_project(peers, order, own, other, obs):
    return call(
        out_project_kernel,
        "out_project",
        [peers, order, *own, *other, *obs],
        [SCALARS] * 2 + [None] * (2 * LINE + Z),
        [shape((SHARDS, ROWS, QW), BF16), shape((Z * T, D), BF16)] + [shape((T, QW), BF16)] * Z,
        flops=2 * Z * T * D * QW,
        moved=6 << 20,
    )


def cut_out_kernel(peers_ref, w_ref, *outs):
    for hop in range(Z):
        outs[hop][...] = w_ref[pl.ds(peers_ref[hop] * Z, Z)].reshape(QW, QW)


def cut_out(peers, w):
    return call(
        cut_out_kernel,
        "cut_out",
        [peers, w],
        [SCALARS, None],
        [shape((QW, QW), BF16)] * Z,
        flops=D * QW,
        moved=2 << 20,
    )


def residual_kernel(peers_ref, x_ref, gains_ref, *refs):
    pieces, (x1_ref, h2_ref) = refs[:Z], refs[Z:]
    x1_ref[...] = x_ref[...].astype(F32)
    for hop in range(Z):
        x1_ref[:, columns_of(peers_ref[hop])] += pieces[hop][...].astype(F32)
    normed, _ = norm_of(x1_ref[...])
    h2_ref[...] = (normed * gains_ref[1:2, :]).astype(BF16)


def residual(peers, x, gains, pieces):
    return call(
        residual_kernel,
        "residual",
        [peers, x, gains, *pieces],
        [SCALARS] + [None] * (2 + Z),
        [shape((T, D), F32), shape((T, D), BF16)],
        flops=T * D * 8,
        moved=2 << 20,
    )


def gate_kernel(small_ref, member_ref, chosen_ref, place_ref, *refs):
    rows, (gates_ref, slot_gate_ref, b_ref) = refs[:Z], refs[Z:]
    small = small_of(small_ref)
    for hop in range(Z):
        h2 = rows[hop][...]
        member = member_ref[hop] > 0.5
        logits = jnp.where(member, mm(h2, small), -jnp.inf)
        exponent = jnp.exp(logits - jnp.max(logits, axis=-1, keepdims=True))
        gates = exponent / jnp.sum(exponent, axis=-1, keepdims=True)
        gates_ref[hop] = gates
        high = gates.astype(BF16)
        low = (gates - high.astype(F32)).astype(BF16)
        place = place_ref[hop]
        spread = mm(place, high) + mm(place, low)
        picked = jnp.sum(spread * chosen_ref[...], axis=-1, keepdims=True)
        slot_gate_ref[:, hop] = picked.reshape(LOCAL, CAP, 1)
        b_ref[:, hop] = mm(place, h2).astype(BF16).reshape(LOCAL, CAP, D)


def gate_rows(half, w, member, chosen, place, rows):
    gates, slot_gate, b = call(
        gate_kernel,
        "gate_rows",
        [w, member, chosen, place, *rows],
        [
            SMALL_SPEC,
            pl.BlockSpec((Z, T, LANES), lambda *_: (half, 0, 0)),
            None,
            pl.BlockSpec((Z, SLOTS, T), lambda *_: (half, 0, 0)),
        ]
        + [None] * Z,
        [
            shape((Z, T, LANES), F32),
            shape((LOCAL, Z, CAP, 1), F32),
            shape((LOCAL, Z, CAP, D), BF16),
        ],
        flops=2 * Z * SLOTS * T * D,
        moved=5 << 20,
    )
    return gates, slot_gate.reshape(LOCAL, Z * CAP, 1), b.reshape(LOCAL, Z * CAP, D)


def spread_kernel(place_ref, *refs):
    rows, out_ref = refs[:PEERS], refs[PEERS]
    for hop in range(PEERS):
        out_ref[:, hop] = mm(place_ref[hop], rows[hop][...]).astype(BF16).reshape(LOCAL, CAP, D)


def spread_rows(place, line, other):
    return call(
        spread_kernel,
        "spread_rows",
        [place, *line, *other],
        [None] + [DY_SPEC] * Z + [X_SPEC] * Z,
        [shape((LOCAL, PEERS, CAP, D), BF16)],
        flops=2 * PEERS * SLOTS * T * D,
        moved=8 << 20,
    )[0].reshape(LOCAL, PEERS * CAP, D)


def expert_step(expert, b_refs, dyr_ref, gate_refs, first, down, gy_ref, db_ref):
    rows = jnp.concatenate([ref[0] for ref in b_refs], axis=0)
    gate = jnp.concatenate([ref[0] for ref in gate_refs], axis=0)
    pre = mm(rows, first())
    gate_pre, up_pre = pre[:, :H], pre[:, H:]
    sigmoid = 1.0 / (1.0 + jnp.exp(-gate_pre))
    silu = gate_pre * sigmoid
    activated = (silu * up_pre).astype(BF16)
    result = mm_nt(activated, down()).astype(BF16).astype(F32)
    raw = dyr_ref[0].astype(F32)
    gy_ref[0] = (gate * result).astype(BF16)
    inner = jnp.sum(raw * result, axis=-1, keepdims=True)
    grad_rows = (gate * raw).astype(BF16)
    grad_act = mm(grad_rows, down())
    grad_gate = (grad_act * up_pre * sigmoid * (1.0 + gate_pre * (1.0 - sigmoid))).astype(BF16)
    grad_up = (grad_act * silu).astype(BF16)
    both = jnp.concatenate([grad_gate, grad_up], axis=1)
    db_ref[0, :, 0:D] = mm_nt(both, first()).astype(BF16)
    lane = lax.broadcasted_iota(jnp.int32, (PEERS * CAP, LANES), 1)
    high = inner.astype(BF16).astype(F32)
    low = inner - high
    tail = jnp.where(lane == expert, high, jnp.where(lane == expert + E, low, 0.0))
    db_ref[0, :, D : D + LANES] = tail.astype(BF16)
    return rows, both, grad_rows, activated


def expert_kernel(
    me_ref, b0_ref, b1_ref, dyr_ref, gate0_ref, gate1_ref, w_ref, gy_ref, db_ref, grad_ref
):
    rows, both, grad_rows, activated = expert_step(
        me_ref[0] * LOCAL + pl.program_id(0),
        (b0_ref, b1_ref),
        dyr_ref,
        (gate0_ref, gate1_ref),
        lambda: w_ref[0, :, 0 : 2 * H],
        lambda: w_ref[0, :, 2 * H : 3 * H],
        gy_ref,
        db_ref,
    )
    grad_ref[0, :, 0 : 2 * H] = mm_tn(rows, both).astype(BF16)
    grad_ref[0, :, 2 * H : 3 * H] = mm_tn(grad_rows, activated).astype(BF16)


def per_expert(*dims, first=0):
    return pl.BlockSpec((1,) + dims, lambda e: (e + first, 0, 0))


def row_specs(first):
    half = PEERS * CAP // 2
    return [
        SCALARS,
        per_expert(half, D, first=first),
        per_expert(half, D, first=first),
        per_expert(2 * half, D, first=first),
        per_expert(half, 1, first=first),
        per_expert(half, 1, first=first),
    ]


def experts(me, b, dyr, slot_gate, pack):
    rows = PEERS * CAP
    return pl.pallas_call(
        expert_kernel,
        grid=(PLAIN,),
        in_specs=row_specs(0) + [per_expert(D, 3 * H)],
        out_specs=[per_expert(rows, D), per_expert(rows, D + LANES), per_expert(D, 3 * H)],
        out_shape=[
            shape((PLAIN, rows, D), BF16),
            shape((PLAIN, rows, D + LANES), BF16),
            shape((PLAIN, D, 3 * H), BF16),
        ],
        compiler_params=params(),
        cost_estimate=cost(18 * PLAIN * rows * D * H, 12 * PLAIN << 20),
        name="experts",
    )(me, *b, dyr, *slot_gate, pack)


def extra_kernel(
    me_ref,
    b0_ref,
    b1_ref,
    dyr_ref,
    gate0_ref,
    gate1_ref,
    dests_ref,
    w_ref,
    gy_ref,
    db_ref,
    keep_ref,
    give_ref,
    grads,
):
    rows, both, grad_rows, activated = expert_step(
        me_ref[0] * LOCAL + PLAIN + pl.program_id(0),
        (b0_ref, b1_ref),
        dyr_ref,
        (gate0_ref, gate1_ref),
        lambda: w_ref[0, :, 0 : 2 * H],
        lambda: w_ref[0, :, 2 * H : 3 * H],
        gy_ref,
        db_ref,
    )
    grads[:, :, 0 : 2 * H] = mm_tn(rows, both).astype(BF16).reshape(SHARDS, ROWS, 2 * H)
    grads[:, :, 2 * H : 3 * H] = mm_tn(grad_rows, activated).astype(BF16).reshape(SHARDS, ROWS, H)
    for chip in range(CHIPS):
        keep_ref[chip, 0] = grads[dests_ref[chip]]
        give_ref[chip, 0] = grads[dests_ref[CHIPS + chip]]


def extra_experts(me, b, dyr, slot_gate, dests, pack):
    rows = PEERS * CAP
    blocks = pl.BlockSpec((CHIPS, 1, ROWS, 3 * H), lambda e: (0, e, 0, 0))
    return pl.pallas_call(
        extra_kernel,
        grid=(EXTRA,),
        in_specs=row_specs(PLAIN) + [SCALARS, per_expert(D, 3 * H, first=PLAIN)],
        out_specs=[per_expert(rows, D), per_expert(rows, D + LANES), blocks, blocks],
        out_shape=[
            shape((EXTRA, rows, D), BF16),
            shape((EXTRA, rows, D + LANES), BF16),
            shape((CHIPS, EXTRA, ROWS, 3 * H), BF16),
            shape((CHIPS, EXTRA, ROWS, 3 * H), BF16),
        ],
        scratch_shapes=[pltpu.VMEM((SHARDS, ROWS, 3 * H), BF16)],
        compiler_params=params(),
        cost_estimate=cost(18 * EXTRA * rows * D * H, 14 * EXTRA << 20),
        name="extra_experts",
    )(me, *b, dyr, *slot_gate, dests, pack)


def extra_halves_kernel(keep_ref, got_ref, line_ref, cross_ref):
    total = (keep_ref[0].astype(F32) + got_ref[0].astype(F32)).astype(BF16)

    @pl.when(pl.program_id(0) < LINE)
    def _():
        cross_ref[0] = total

    @pl.when(pl.program_id(0) >= LINE)
    def _():
        line_ref[0] = total


def extra_halves(keep, got):
    block = (1, EXTRA, ROWS, 3 * H)
    return pl.pallas_call(
        extra_halves_kernel,
        grid=(CHIPS,),
        in_specs=[pl.BlockSpec(block, lambda i: ((i + LINE) % CHIPS, 0, 0, 0))] * 2,
        out_specs=[
            pl.BlockSpec(block, lambda i: (jnp.maximum(i - LINE, 0), 0, 0, 0)),
            pl.BlockSpec(block, lambda i: (jnp.minimum(i, LINE - 1), 0, 0, 0)),
        ],
        out_shape=[shape((LINE, EXTRA, ROWS, 3 * H), BF16)] * 2,
        compiler_params=params(),
        cost_estimate=cost(keep.size, 6 * keep.size),
        name="extra_halves",
    )(keep, got)


def extra_lines_kernel(line_ref, got_ref, *outs):
    for hop in range(LINE):
        outs[hop][...] = (line_ref[hop].astype(F32) + got_ref[hop].astype(F32)).astype(BF16)


def extra_lines(line, got):
    return call(
        extra_lines_kernel,
        "extra_lines",
        [line, got],
        [None, None],
        [shape((EXTRA, ROWS, 3 * H), BF16)] * LINE,
        flops=line.size,
        moved=6 * line.size,
    )


def collect_kernel(place_ref, plain_ref, extra_ref, *out_refs):
    for hop in range(PEERS):
        rows = jnp.concatenate(
            [ref[:, hop].reshape(-1, ref.shape[-1]) for ref in (plain_ref, extra_ref)], axis=0
        )
        out_refs[hop][...] = mm_tn(place_ref[hop], rows).astype(BF16)


def collect(place, values, name):
    width = values[0].shape[-1]
    return call(
        collect_kernel,
        name,
        [place, *(v.reshape(-1, PEERS, CAP, width) for v in values)],
        [None] * 3,
        [shape((T, width), BF16)] * PEERS,
        flops=2 * PEERS * SLOTS * T * width,
        moved=8 << 20,
    )


def mix(x1, returns, other):
    return call(
        add_kernel,
        "mix",
        [x1, *returns, other],
        [None] + [DY_SPEC] * Z + [None],
        [shape((T, D), BF16)],
        flops=T * D * Z,
        moved=4 << 20,
    )[0]


def norm_back(grad, normed, inverse, gain):
    scaled = grad * gain
    return inverse * (scaled - normed * jnp.mean(scaled * normed, axis=-1, keepdims=True))


def token_back_kernel(
    x1_ref, dy_ref, gates_ref, small_ref, gains_ref, *refs
):
    parts, (dx1_ref, dlogits_ref, scaled_ref, da_ref) = refs[: Z + 1], refs[Z + 1 :]
    total = parts[0][...].astype(F32)
    for ref in parts[1:]:
        total = total + ref[...].astype(F32)
    grad, tail = total[:, :D], total[:, D:]
    lane = lax.broadcasted_iota(jnp.int32, (T, LANES), 1)
    inner = jnp.where(lane < E, tail + pltpu.roll(tail, LANES - E, 1), 0.0)
    gates = gates_ref[0]
    score = gates * (inner - jnp.sum(gates * inner, axis=-1, keepdims=True))
    dlogits_ref[...] = score.astype(BF16)
    grad = grad + mm_nt(dlogits_ref[...], small_of(small_ref))
    normed, inverse = norm_of(x1_ref[...])
    scaled_ref[...] = (grad * normed).astype(BF16)
    through = dy_ref[...].astype(F32) + norm_back(grad, normed, inverse, gains_ref[1:2, :])
    dx1_ref[...] = through
    da_ref[...] = through.astype(BF16)


def token_back(x1, dy, gates, w, gains, parts):
    return call(
        token_back_kernel,
        "token_back",
        [x1, dy, gates, w, gains, *parts],
        [None, None, pl.BlockSpec((1, T, LANES), lambda *_: (0, 0, 0)), SMALL_SPEC]
        + [None] * (1 + len(parts)),
        [
            shape((T, D), F32),
            shape((T, LANES), BF16),
            shape((T, D), BF16),
            shape((T, D), BF16),
        ],
        flops=T * D * 64,
        moved=6 << 20,
    )


def shadow_kernel(qkv_ref, h2_ref, dlogits_ref, scaled_ref, *refs):
    xs, (small_ref, inverse_ref, prob_ref) = refs[:Z], refs[Z:]
    lane = lax.broadcasted_iota(jnp.int32, (T, LANES), 1)
    small = mm_tn(h2_ref[...], dlogits_ref[...])
    small_ref[...] = small + mm_tn(scaled_ref[...], (lane == E + 1).astype(BF16))
    for hop in range(Z):
        rows = slice(hop * T, (hop + 1) * T)
        _, inverse = norm_of(xs[hop][...].astype(F32))
        inverse_ref[rows] = inverse
        for group in range(KH):
            query = stack_heads(qkv_ref, rows, group * GROUP)
            prob_ref[hop * KH + group] = probabilities(query, head(qkv_ref, rows, QH + group))


def shadow(qkv, h2, dlogits, scaled, xs):
    return call(
        shadow_kernel,
        "shadow",
        [qkv, h2, dlogits, scaled, *xs],
        [None] * 4 + [X_SPEC] * Z,
        [
            shape((D, LANES), F32),
            shape((Z * T, 1), F32),
            shape((Z * KH, GROUP * T, T), F32),
        ],
        flops=Z * T * D * QW,
        moved=6 << 20,
    )


def head_back_kernel(
    behind_ref,
    parity_ref,
    qkv_ref,
    h1_ref,
    w_ref,
    full_ref,
    partial_ref,
    inverse_ref,
    prob_ref,
    cos_ref,
    sin_ref,
    *refs,
):
    xs, das, weights, results, outs = (refs[at * Z : at * Z + Z] for at in range(5))
    keep_ref, give_ref, dob, dqk, dqkv = refs[5 * Z :]
    total = jnp.zeros((Z * T, QW), F32)
    for hop in range(Z):
        columns = columns_of(behind_ref[hop])
        rows = jnp.concatenate([ref[:, columns] for ref in das], axis=0)
        total = total + mm_nt(rows, weights[hop][...])
        if hop == 0:
            own_columns = rows
    dob[...] = total.astype(BF16)
    for hop in range(Z):
        rows = slice(hop * T, (hop + 1) * T)
        for group in range(KH):
            key, value = head(qkv_ref, rows, QH + group), head(qkv_ref, rows, QH + KH + group)
            query = stack_heads(qkv_ref, rows, group * GROUP)
            out_grad = stack_heads(dob, rows, group * GROUP)
            probability = prob_ref[hop * KH + group]
            grad_prob = mm_nt(out_grad, value)
            held = jnp.sum(probability * grad_prob, axis=-1, keepdims=True)
            grad_scores = (probability * (grad_prob - held)).astype(BF16)
            grad_query = mm(grad_scores, key) * SCALE
            for index in range(GROUP):
                at = (group * GROUP + index) * HEAD_DIM
                dqk[rows, at : at + HEAD_DIM] = grad_query[index * T : (index + 1) * T]
            at = QW + group * HEAD_DIM
            dqk[rows, at : at + HEAD_DIM] = mm_tn(grad_scores, query) * SCALE
            dqkv[rows, at + KW : at + KW + HEAD_DIM] = mm_tn(
                probability.astype(BF16), out_grad
            ).astype(BF16)
    cosine = jnp.concatenate([cos_ref[...]] * Z, axis=0)
    signed = jnp.concatenate([sin_ref[...]] * Z, axis=0)
    dqkv[:, 0 : QW + KW] = rotate_back(dqk[...], cosine, signed).astype(BF16)
    even = parity_ref[0] == 0

    def store(grads, columns):
        pair = grads.astype(BF16).reshape(CHIPS, 2, ROWS, grads.shape[1])
        keep_ref[:, :, columns] = jnp.where(even, pair[:, 0], pair[:, 1])
        give_ref[:, :, columns] = jnp.where(even, pair[:, 1], pair[:, 0])

    store(mm_tn(full_ref[...], own_columns), slice(0, QW))
    store(mm_tn(h1_ref[...], dqkv[...]), slice(QW, MAIN))
    dh1 = mm_nt(dqkv[...], w_ref[:, :, 0:QKV].reshape(D, QKV))
    lane = lax.broadcasted_iota(jnp.int32, (T, LANES), 1)
    first = (lane == E).astype(BF16)
    small = partial_ref[...]
    for hop in range(Z):
        rows = slice(hop * T, (hop + 1) * T)
        piece = dh1[rows]
        normed = xs[hop][...].astype(F32) * inverse_ref[rows]
        small += mm_tn((piece * normed).astype(BF16), first)
        outs[hop][:, 0:D] = piece.astype(BF16)
        outs[hop][:, D:] = results[hop][...]
    store(small, slice(MAIN, SLICE))


def head_back(behind, parity, qkv, h1, w, full, shadows, cosine, signed, xs, das, weights, results):
    return call(
        head_back_kernel,
        "head_back",
        [behind, parity, qkv, h1, w, full, *shadows, cosine, signed, *xs, *das, *weights, *results],
        [SCALARS] * 2 + [None] * 9 + [X_SPEC] * Z + [None] * (3 * Z),
        [shape((T, 2 * D), BF16)] * Z + [shape((CHIPS, ROWS, SLICE), BF16)] * 2,
        scratch=[
            pltpu.VMEM((Z * T, QW), BF16),
            pltpu.VMEM((Z * T, QW + KW), F32),
            pltpu.VMEM((Z * T, QKV), BF16),
        ],
        flops=4 * Z * T * D * QKV,
        moved=16 << 20,
    )


def token_grad_kernel(x_ref, gains_ref, dx1_ref, *refs):
    grad = refs[0][...].astype(F32)
    for hop in range(1, Z):
        grad = grad + refs[hop][...].astype(F32)
    normed, inverse = norm_of(x_ref[...].astype(F32))
    refs[Z][...] = dx1_ref[...] + norm_back(grad, normed, inverse, gains_ref[0:1, :])


def token_grad(x, gains, dx1, pieces):
    return call(
        token_grad_kernel,
        "token_grad",
        [x, gains, dx1, *pieces],
        [None] * 3 + [X_SPEC] * Z,
        [shape((T, D), F32)],
        flops=T * D * 16,
        moved=4 << 20,
    )[0]


def split_kernel(order_ref, keep_ref, got_ref, *outs):
    for chip in range(CHIPS):
        at = order_ref[chip]
        total = (keep_ref[at].astype(F32) + got_ref[at].astype(F32)).astype(BF16)
        outs[chip % 4][chip // 4] = total


def split(order, keep, got):
    return call(
        split_kernel,
        "split",
        [order, keep, got],
        [SCALARS, None, None],
        [shape((2, ROWS, SLICE), BF16)] * 4,
        flops=CHIPS * ROWS * SLICE,
        moved=6 << 20,
    )


def add_kernel(*refs):
    total = refs[0][...].astype(F32)
    for ref in refs[1:-1]:
        total = total + ref[...].astype(F32)
    refs[-1][...] = total.astype(BF16)


def sum_lines_kernel(*refs):
    for at in range(2):
        total = refs[0][at].astype(F32)
        for ref in refs[1:LINE]:
            total = total + ref[at].astype(F32)
        refs[LINE + at][...] = total.astype(BF16)


def sum_lines(parts):
    return call(
        sum_lines_kernel,
        "sum_lines",
        list(parts),
        [None] * LINE,
        [shape((ROWS, SLICE), BF16)] * 2,
        flops=LINE * ROWS * SLICE,
        moved=12 * ROWS * SLICE,
    )


def add_all(parts, name):
    return call(
        add_kernel,
        name,
        list(parts),
        [None] * len(parts),
        [shape(parts[0].shape, BF16)],
        flops=parts[0].size * len(parts),
        moved=2 * parts[0].size * (len(parts) + 1),
    )[0]


def finish_kernel(order_ref, *refs):
    parts, (q_ref, k_ref, v_ref, o_ref, router_ref, one_ref, two_ref, narrow) = refs[:Z], refs[Z:]
    for hop in range(Z):
        at = order_ref[hop]
        part = parts[hop][...].astype(F32)
        o_ref[:, columns_of(at)] = part[:, 0:QW]
        q_ref[:, columns_of(at)] = part[:, QW : 2 * QW]
        heads = pl.ds(pl.multiple_of(at * KW, KW), KW)
        k_ref[:, heads] = part[:, 2 * QW : 2 * QW + KW]
        v_ref[:, heads] = part[:, 2 * QW + KW : MAIN]
        narrow[at] = part[:, MAIN:]
    small = (narrow[0] + narrow[1] + narrow[2] + narrow[3]).T
    router_ref[...] = small[0:E]
    one_ref[...] = small[E : E + 1]
    two_ref[...] = small[E + 1 : E + 2]


def finish(order, parts):
    return call(
        finish_kernel,
        "finish",
        [order, *parts],
        [SCALARS] + [None] * Z,
        [
            shape((ROWS, D), F32),
            shape((ROWS, KEY_VALUE_HEADS * HEAD_DIM), F32),
            shape((ROWS, KEY_VALUE_HEADS * HEAD_DIM), F32),
            shape((ROWS, D), F32),
            shape((E, ROWS), F32),
            shape((1, ROWS), F32),
            shape((1, ROWS), F32),
        ],
        scratch=[pltpu.VMEM((Z, ROWS, LANES), F32)],
        flops=ROWS * SLICE * Z,
        moved=3 << 20,
    )


def unpack_kernel(share_ref, *refs):
    parts, outs = refs[:LINE], refs[LINE:]

    def store(value):
        for at in range(3):
            outs[at][0] = value[:, at * H : (at + 1) * H]

    @pl.when(pl.program_id(0) < PLAIN)
    def _():
        store(share_ref[0].astype(F32))

    @pl.when(pl.program_id(0) >= PLAIN)
    def _():
        total = parts[0][0].astype(F32)
        for ref in parts[1:]:
            total = total + ref[0].astype(F32)
        store(total)


def unpack(share, parts):
    block = (1, ROWS, 3 * H)
    return pl.pallas_call(
        unpack_kernel,
        grid=(LOCAL,),
        in_specs=[pl.BlockSpec(block, lambda e: (jnp.minimum(e, PLAIN - 1), 0, 0))]
        + [pl.BlockSpec(block, lambda e: (jnp.maximum(e - PLAIN, 0), 0, 0))] * LINE,
        out_specs=[per_expert(ROWS, H)] * 3,
        out_shape=[shape((LOCAL, ROWS, H), F32)] * 3,
        compiler_params=params(),
        cost_estimate=cost(LOCAL * ROWS * 3 * H, 5 << 20),
        name="unpack",
    )(share, *parts)


def spread_tables(all_routes, me):
    lane = jnp.arange(LANES, dtype=jnp.int32)
    member = jnp.sum((all_routes[..., None] == lane).astype(F32), axis=2)
    mine = me * LOCAL + jnp.arange(LOCAL, dtype=jnp.int32)
    own = jnp.sum((all_routes[..., None] == mine).astype(F32), axis=2)
    earlier = (np.arange(T)[:, None] > np.arange(T)[None, :]).astype(np.float32)
    before = jnp.einsum(
        "ts,rse->rte", jnp.asarray(earlier, BF16), own.astype(BF16), preferred_element_type=F32
    )
    slots = jnp.where(own > 0.5, before.astype(jnp.int32), -1)
    slots = jnp.swapaxes(slots, 1, 2)[:, :, None, :]
    place = slots == jnp.arange(CAP, dtype=jnp.int32)[None, None, :, None]
    return member, place.astype(BF16).reshape(PEERS, SLOTS, T)


def body(
    tokens,
    cotangent,
    routes,
    norm_one,
    w_query,
    key_weight,
    value_weight,
    w_out,
    norm_two,
    w_router,
    w_gate,
    w_up,
    w_down,
):
    me = lax.axis_index("expert")
    place_in_group = lax.axis_index("fsdp")
    z = me % Z
    core = place_in_group % 2
    cosine, signed = (jnp.asarray(table) for table in rope_tables())

    first, second = pack(
        z.astype(jnp.int32)[None],
        w_out,
        w_query,
        key_weight,
        value_weight,
        w_router.T,
        norm_one[None, :],
        norm_two[None, :],
    )
    def spread_over_chips(value):
        pair = jnp.stack([value, send_chip(value, LINE)])
        own = [send_chip(pair, hop) for hop in range(LINE)]
        return own, [swap_core(value) for value in own]

    own, other = spread_over_chips(first)
    out_own, out_other = spread_over_chips(after(second, own[1]))
    sources = jnp.stack([chip_at(place_in_group, hop, True) for hop in range(CHIPS)])
    order = jnp.concatenate([2 * sources + core, 2 * sources + 1 - core]).astype(jnp.int32)
    dests = jnp.stack([chip_at(place_in_group, hop) for hop in range(CHIPS)]).astype(jnp.int32)
    twins = jnp.concatenate([2 * dests + core, 2 * dests + 1 - core])
    expert_pack = lax.all_gather(
        jnp.concatenate([w_gate, w_up, jnp.swapaxes(w_down, 1, 2)], axis=2),
        "fsdp",
        axis=1,
        tiled=True,
    )

    behind = jnp.stack([(z + Z - hop) % Z for hop in range(Z)]).astype(jnp.int32)
    ahead = jnp.stack([(z + hop) % Z for hop in range(Z)]).astype(jnp.int32)

    marks = jnp.pad(routes, ((0, 0), (0, LANES - TOPK))).astype(BF16)
    early = jnp.concatenate([cotangent, marks], axis=1)
    whole_row = jnp.concatenate([tokens, early], axis=1)
    xs = [send(whole_row, hop) for hop in (0, 1, 3)]
    xs.insert(2, send(whole_row, 2))
    w, gains, h1, qkv, ob = project(order, cosine, signed, own, other, xs)
    obs = [send(ob, hop) for hop in range(Z)]
    early_other = send(after(early, xs[3]), Z)
    early_other = after(early_other, *obs[1:])
    early_other = [send(early_other, hop) for hop in range(Z)]
    w_out_slice, ob_full, *x1_columns = out_project(behind, order, out_own, out_other, obs)
    x1_pieces = [send(x1_columns[hop], hop, True) for hop in range(Z)]
    x1, h2 = residual(ahead, tokens, gains, x1_pieces)
    h2_other = send(h2, Z)
    h2_line = [send(h2, hop) for hop in range(Z)]
    h2_other = [send(h2_other, hop) for hop in range(Z)]

    all_routes = jnp.stack(
        [r[:, 2 * D : 2 * D + TOPK].astype(jnp.int32) for r in xs]
        + [r[:, D : D + TOPK].astype(jnp.int32) for r in early_other]
    )
    member, place = spread_tables(all_routes, me)
    row_expert = me * LOCAL + jnp.arange(SLOTS, dtype=jnp.int32) // CAP
    chosen = (row_expert[:, None] == jnp.arange(LANES, dtype=jnp.int32)[None, :]).astype(F32)
    dyr = spread_rows(place, xs, early_other)

    gates, gate0, b0 = gate_rows(0, w, member, chosen, place, h2_line)
    _, gate1, b1 = gate_rows(1, w, member, chosen, place, h2_other)
    b, slot_gate = (b0, b1), (gate0, gate1)
    weights = after(cut_out(ahead, after(w_out_slice, x1)), b1)
    slot_gate = after(slot_gate, *weights)
    weights = [send(weights[hop], hop) for hop in range(Z)]
    number = me.astype(jnp.int32)[None]
    gy, db, grad_pack = experts(number, b, dyr, slot_gate, expert_pack)
    extra_gy, extra_db, keep_extra, give_extra = extra_experts(
        after(number, db), b, dyr, slot_gate, twins, expert_pack
    )
    db_parts = collect(place, after((db, extra_db), *weights[1:]), "collect_grads")
    grad_cross = [send(db_parts[Z + hop], hop, True) for hop in range(Z)]
    grad_line = after(db_parts[:Z], *grad_cross[1:])
    grad_line = [send(grad_line[hop], hop, True) for hop in range(Z)]
    got_extra = swap_core(give_extra)
    grad_other = send(add_all(grad_cross, "line_grads"), Z)
    expert_share = lax.psum_scatter(
        after(grad_pack, *weights[1:]), "fsdp", scatter_dimension=1, tiled=True
    )
    results = collect(place, (gy, extra_gy), "collect_results")
    grad_line = after(grad_line, results)
    dx1, dlogits, scaled, da = token_back(x1, cotangent, gates, w, gains, [*grad_line, grad_other])
    das = [send(da, hop) for hop in range(Z)]
    extra_line, extra_cross = extra_halves(keep_extra, after(got_extra, da))
    shadows = shadow(after(qkv, extra_cross), h2, dlogits, scaled, xs)
    results = after(results, shadows[1], *das[1:])
    results_cross = [send(results[Z + hop], hop, True) for hop in range(Z)]
    *returns, keep, give = head_back(
        behind,
        core.astype(jnp.int32)[None],
        qkv,
        h1,
        w,
        ob_full,
        shadows,
        cosine,
        signed,
        xs,
        das,
        weights,
        results[:Z],
    )
    parts = split(dests, keep, swap_core(after(give, *results_cross[1:])))
    extra_got = send_chip(extra_cross, LINE)
    parts = after(parts, expert_share)
    lines = [send_chip(parts[hop], hop) for hop in range(LINE)]
    results_other = send(add_all(results_cross, "line_results"), Z)
    first, third = send(returns[1], 1, True), send(returns[3], 3, True)
    lines[0] = after(lines[0], first, third)
    second = send(after(returns[2], first, third), 2, True)
    returns = [returns[0], first, second, third]
    share = sum_lines(lines)
    extra_parts = extra_lines(extra_line, after(extra_got, share[1]))
    share = add_all([share[0], send_chip(share[1], LINE)], "sum_chips")
    share = add_all([share, send(share, Z)], "sum_halves")
    extra_first, extra_third = (send_chip(extra_parts[hop], hop) for hop in (1, 3))
    share = after(share, second)
    extra_second = send_chip(extra_parts[2], 2)
    extra_parts = [extra_parts[0], extra_first, extra_second, extra_third]
    shares = [send(share, hop) for hop in range(Z)]
    grad_gate, grad_up, grad_down = unpack(expert_share, extra_parts)
    grad_tokens = token_grad(tokens, gains, dx1, returns)
    mixed_out = mix(x1, returns, results_other)
    shares = after(shares, grad_tokens, mixed_out, grad_gate)
    grad_query, grad_key, grad_value, grad_out, router, one, two = finish(behind, shares)

    return (
        mixed_out,
        grad_tokens,
        one.reshape(ROWS),
        grad_query,
        grad_key,
        grad_value,
        grad_out,
        two.reshape(ROWS),
        router.T,
        grad_gate,
        grad_up,
        jnp.swapaxes(grad_down, 1, 2),
    )


def solution(mesh):
    return jax.shard_map(
        body,
        mesh=mesh,
        in_specs=(
            P(("expert", "fsdp"), None),
            P(("expert", "fsdp"), None),
            P(("expert", "fsdp"), None),
            P("fsdp"),
            P("fsdp", None),
            P("fsdp", None),
            P("fsdp", None),
            P("fsdp", None),
            P("fsdp"),
            P("fsdp", None),
            P("expert", "fsdp", None),
            P("expert", "fsdp", None),
            P("expert", None, "fsdp"),
        ),
        out_specs=(
            P(("expert", "fsdp"), None),
            P(("expert", "fsdp"), None),
            P("fsdp"),
            P("fsdp", None),
            P("fsdp", None),
            P("fsdp", None),
            P("fsdp", None),
            P("fsdp"),
            P("fsdp", None),
            P("expert", "fsdp", None),
            P("expert", "fsdp", None),
            P("expert", None, "fsdp"),
        ),
        check_vma=False,
    )
```

```python
import jax
import jax.numpy as jnp
import numpy as np
from jax import lax
from jax.experimental import pallas as pl
from jax.experimental.pallas import tpu as pltpu
from jax.sharding import PartitionSpec as P

QUERY_HEADS = 24
KEY_VALUE_HEADS = 8
GROUP = QUERY_HEADS // KEY_VALUE_HEADS
HEAD_DIM = 64
HALF = HEAD_DIM // 2
E = 40
H = 512
D = 1536
T = 128
CAP = 32
NORM_EPSILON = 1e-05
SCALE = HEAD_DIM ** (-0.5)

Z = 4
PEERS = 8
LOCAL = E // PEERS
SLOTS = LOCAL * CAP
EXTRA = 1
PLAIN = LOCAL - EXTRA
LANES = 128
CHIPS = 8
LINE = 4
TOPK = 8
SHARDS = 2 * CHIPS
ROWS = D // SHARDS
QH = QUERY_HEADS // Z
KH = KEY_VALUE_HEADS // Z
QW = QH * HEAD_DIM
KW = KH * HEAD_DIM
QKV = QW + 2 * KW
MAIN = QW + QKV
SLICE = MAIN + LANES
VMEM_LIMIT = 60 * 1024 * 1024

F32 = jnp.float32
BF16 = jnp.bfloat16


def peer(index, hop, back=False):
    shift = hop % Z
    turned = (index % Z + (Z - shift if back else shift)) % Z
    return (index // Z + hop // Z) % 2 * Z + turned


def send(value, hop, back=False):
    if hop == 0:
        return value
    return lax.ppermute(value, "expert", [(i, peer(i, hop, back)) for i in range(PEERS)])


def chip_at(index, hop, back=False):
    shift = hop % 4
    turned = (index // 2 % 4 + (4 - shift if back else shift)) % 4
    return (index // 8 + hop // 4) % 2 * 4 + turned


def send_chip(value, hop):
    if hop == 0:
        return value
    pairs = [(i, 2 * chip_at(i, hop) + i % 2) for i in range(SHARDS)]
    return lax.ppermute(value, "fsdp", pairs)


def after(value, *others):
    return lax.optimization_barrier((value, others))[0]


def swap_core(value):
    return lax.ppermute(value, "fsdp", [(i, i ^ 1) for i in range(SHARDS)])


def mm(left, right):
    return jnp.dot(left, right, preferred_element_type=F32)


def mm_nt(left, right):
    return lax.dot_general(left, right, (((1,), (1,)), ((), ())), preferred_element_type=F32)


def mm_tn(left, right):
    return lax.dot_general(left, right, (((0,), (0,)), ((), ())), preferred_element_type=F32)


def rope_tables():
    frequency = np.exp(-np.log(10000.0) * np.arange(HALF, dtype=np.float64) * 2.0 / HEAD_DIM)
    angles = np.arange(T, dtype=np.float64)[:, None] * frequency[None, :]
    cosine = np.tile(np.cos(angles), (1, 4)).astype(np.float32)
    sine = np.sin(angles)
    signed = np.tile(np.concatenate([-sine, sine], axis=1), (1, 2)).astype(np.float32)
    return cosine, signed


def swap_halves(values):
    width = values.shape[1]
    lane = lax.broadcasted_iota(jnp.int32, values.shape, 1)
    up = pltpu.roll(values, width - HALF, 1)
    down = pltpu.roll(values, HALF, 1)
    return jnp.where(lane % HEAD_DIM < HALF, up, down)


def wide(table, width):
    return jnp.concatenate([table] * (width // LANES), axis=1)


def rotate(values, cosine, signed):
    width = values.shape[1]
    return values * wide(cosine, width) + swap_halves(values) * wide(signed, width)


def rotate_back(values, cosine, signed):
    width = values.shape[1]
    return values * wide(cosine, width) + swap_halves(values * wide(signed, width))


def gain_rows(small):
    pick = lax.broadcasted_iota(jnp.int32, (16, LANES), 1) == (
        lax.broadcasted_iota(jnp.int32, (16, LANES), 0) + E
    )
    return mm_nt(pick.astype(BF16), small)


def norm_of(values):
    inverse = lax.rsqrt(jnp.mean(values * values, axis=-1, keepdims=True) + NORM_EPSILON)
    return values * inverse, inverse


def head(ref, rows, index):
    return ref[rows, index * HEAD_DIM : (index + 1) * HEAD_DIM]


def stack_heads(ref, rows, first):
    return jnp.concatenate([head(ref, rows, first + index) for index in range(GROUP)], axis=0)


def probabilities(query, key):
    scores = mm_nt(query, key) * SCALE
    rows = lax.broadcasted_iota(jnp.int32, scores.shape, 0) % T
    cols = lax.broadcasted_iota(jnp.int32, scores.shape, 1)
    scores = jnp.where(rows >= cols, scores, -jnp.inf)
    exponent = jnp.exp(scores - jnp.max(scores, axis=-1, keepdims=True))
    return exponent / jnp.sum(exponent, axis=-1, keepdims=True)


def whole(shape):
    return pl.BlockSpec(shape, lambda *_: (0,) * len(shape))


SCALARS = pl.BlockSpec(memory_space=pltpu.SMEM)
ANYWHERE = pl.BlockSpec(memory_space=pl.ANY)


def params(**more):
    return pltpu.CompilerParams(vmem_limit_bytes=VMEM_LIMIT, **more)


WEIGHT = 60


def cost(flops, moved):
    return pl.CostEstimate(flops=flops * WEIGHT, bytes_accessed=moved * WEIGHT, transcendentals=0)


def shape(dims, kind):
    return jax.ShapeDtypeStruct(dims, kind)


def call(kernel, name, inputs, in_specs, outputs, out_specs=None, scratch=(), flops=0, moved=0):
    in_specs = [whole(v.shape) if spec is None else spec for v, spec in zip(inputs, in_specs)]
    if out_specs is None:
        out_specs = [whole(o.shape) for o in outputs]
    return pl.pallas_call(
        kernel,
        grid=(1,),
        in_specs=in_specs,
        out_specs=out_specs,
        out_shape=outputs,
        scratch_shapes=list(scratch),
        compiler_params=params(),
        cost_estimate=cost(flops, moved),
        name=name,
    )(*inputs)


SMALL_SPEC = pl.BlockSpec((SHARDS, ROWS, LANES), lambda *_: (0, 0, QKV // LANES))
X_SPEC = pl.BlockSpec((T, D), lambda *_: (0, 0))
DY_SPEC = pl.BlockSpec((T, D), lambda *_: (0, 1))


def small_of(ref):
    return ref[...].reshape(D, LANES)


def columns_of(index):
    return pl.ds(pl.multiple_of(index * QW, QW), QW)


def pack_kernel(
    z_ref, out_ref, query_ref, key_ref, value_ref, router_ref, one_ref, two_ref, first_ref, second_ref
):
    first_ref[:, 0:QW] = query_ref[...]
    first_ref[:, QW : QW + KW] = key_ref[...]
    first_ref[:, QW + KW : QKV] = value_ref[...]
    narrow = [router_ref[...], one_ref[...], two_ref[...], jnp.zeros((LANES - E - 2, ROWS), BF16)]
    first_ref[:, QKV:] = jnp.concatenate([v.astype(F32) for v in narrow], axis=0).T.astype(BF16)
    second_ref[...] = out_ref[...]


def pack(z, w_out, w_query, key_weight, value_weight, router, one, two):
    def slice_of(width):
        return pl.BlockSpec((ROWS, width), lambda i, z: (0, z[0]))

    return pl.pallas_call(
        pack_kernel,
        grid_spec=pltpu.PrefetchScalarGridSpec(
            num_scalar_prefetch=1,
            grid=(1,),
            in_specs=[
                slice_of(QW),
                slice_of(QW),
                slice_of(KW),
                slice_of(KW),
                whole((E, ROWS)),
                whole((1, ROWS)),
                whole((1, ROWS)),
            ],
            out_specs=[whole((ROWS, QKV + LANES)), whole((ROWS, QW))],
        ),
        out_shape=[shape((ROWS, QKV + LANES), BF16), shape((ROWS, QW), BF16)],
        compiler_params=params(),
        cost_estimate=cost(ROWS * SLICE, 1 << 20),
        name="pack",
    )(z, w_out, w_query, key_weight, value_weight, router, one, two)


def project_kernel(order_ref, cos_ref, sin_ref, *refs):
    own, other, xs = refs[:LINE], refs[LINE : 2 * LINE], refs[2 * LINE : 2 * LINE + Z]
    w_ref, gains_ref, h1_ref, qkv_ref, ob_ref = refs[2 * LINE + Z :]
    for chip in range(CHIPS):
        w_ref[order_ref[chip]] = own[chip % LINE][chip // LINE]
        w_ref[order_ref[CHIPS + chip]] = other[chip % LINE][chip // LINE]
    gains = gain_rows(w_ref[:, :, QKV:].reshape(D, LANES))
    gains_ref[...] = gains
    for hop in range(Z):
        normed, _ = norm_of(xs[hop][...].astype(F32))
        h1_ref[hop * T : (hop + 1) * T] = (normed * gains[0:1, :]).astype(BF16)
    pre = mm(h1_ref[...], w_ref[:, :, 0:QKV].reshape(D, QKV))
    cosine = jnp.concatenate([cos_ref[...]] * Z, axis=0)
    signed = jnp.concatenate([sin_ref[...]] * Z, axis=0)
    qkv_ref[:, 0:QW] = rotate(pre[:, 0:QW], cosine, signed).astype(BF16)
    qkv_ref[:, QW : QW + KW] = rotate(pre[:, QW : QW + KW], cosine, signed).astype(BF16)
    qkv_ref[:, QW + KW :] = pre[:, QW + KW :].astype(BF16)
    for hop in range(Z):
        rows = slice(hop * T, (hop + 1) * T)
        for group in range(KH):
            key, value = head(qkv_ref, rows, QH + group), head(qkv_ref, rows, QH + KH + group)
            query = stack_heads(qkv_ref, rows, group * GROUP)
            result = mm(probabilities(query, key).astype(BF16), value).astype(BF16)
            for index in range(GROUP):
                at = (group * GROUP + index) * HEAD_DIM
                ob_ref[rows, at : at + HEAD_DIM] = result[index * T : (index + 1) * T]


def project(order, cosine, signed, own, other, xs):
    return call(
        project_kernel,
        "project",
        [order, cosine, signed, *own, *other, *xs],
        [SCALARS] + [None] * (2 + 2 * LINE) + [X_SPEC] * Z,
        [
            shape((SHARDS, ROWS, QKV + LANES), BF16),
            shape((16, D), F32),
            shape((Z * T, D), BF16),
            shape((Z * T, QKV), BF16),
            shape((Z * T, QW), BF16),
        ],
        flops=2 * Z * T * D * QKV,
        moved=12 << 20,
    )


def out_project_kernel(peers_ref, order_ref, *refs):
    own, other, obs = refs[:LINE], refs[LINE : 2 * LINE], refs[2 * LINE : 2 * LINE + Z]
    w_ref, full_ref, *outs = refs[2 * LINE + Z :]
    for chip in range(CHIPS):
        w_ref[order_ref[chip]] = own[chip % LINE][chip // LINE]
        w_ref[order_ref[CHIPS + chip]] = other[chip % LINE][chip // LINE]
    total = jnp.zeros((Z * T, QW), F32)
    for hop in range(Z):
        peer_index = peers_ref[hop]
        blocks = [(row - hop) % Z for row in range(Z)]
        rows = jnp.concatenate([obs[hop][b * T : (b + 1) * T, :] for b in blocks], axis=0)
        full_ref[:, columns_of(peer_index)] = rows
        weight = w_ref[pl.ds(peer_index * Z, Z)].reshape(QW, QW)
        total = total + mm(rows, weight)
    for hop in range(Z):
        outs[hop][...] = total[hop * T : (hop + 1) * T].astype(BF16)


def out_project(peers, order, own, other, obs):
    return call(
        out_project_kernel,
        "out_project",
        [peers, order, *own, *other, *obs],
        [SCALARS] * 2 + [None] * (2 * LINE + Z),
        [shape((SHARDS, ROWS, QW), BF16), shape((Z * T, D), BF16)] + [shape((T, QW), BF16)] * Z,
        flops=2 * Z * T * D * QW,
        moved=6 << 20,
    )


def cut_out_kernel(peers_ref, w_ref, *outs):
    for hop in range(Z):
        outs[hop][...] = w_ref[pl.ds(peers_ref[hop] * Z, Z)].reshape(QW, QW)


def cut_out(peers, w):
    return call(
        cut_out_kernel,
        "cut_out",
        [peers, w],
        [SCALARS, None],
        [shape((QW, QW), BF16)] * Z,
        flops=D * QW,
        moved=2 << 20,
    )


def residual_kernel(peers_ref, x_ref, gains_ref, *refs):
    pieces, (x1_ref, h2_ref) = refs[:Z], refs[Z:]
    x1_ref[...] = x_ref[...].astype(F32)
    for hop in range(Z):
        x1_ref[:, columns_of(peers_ref[hop])] += pieces[hop][...].astype(F32)
    normed, _ = norm_of(x1_ref[...])
    h2_ref[...] = (normed * gains_ref[1:2, :]).astype(BF16)


def residual(peers, x, gains, pieces):
    return call(
        residual_kernel,
        "residual",
        [peers, x, gains, *pieces],
        [SCALARS] + [None] * (2 + Z),
        [shape((T, D), F32), shape((T, D), BF16)],
        flops=T * D * 8,
        moved=2 << 20,
    )


def gate_kernel(small_ref, member_ref, chosen_ref, place_ref, *refs):
    rows, (gates_ref, slot_gate_ref, b_ref) = refs[:Z], refs[Z:]
    small = small_of(small_ref)
    for hop in range(Z):
        h2 = rows[hop][...]
        member = member_ref[hop] > 0.5
        logits = jnp.where(member, mm(h2, small), -jnp.inf)
        exponent = jnp.exp(logits - jnp.max(logits, axis=-1, keepdims=True))
        gates = exponent / jnp.sum(exponent, axis=-1, keepdims=True)
        gates_ref[hop] = gates
        high = gates.astype(BF16)
        low = (gates - high.astype(F32)).astype(BF16)
        place = place_ref[hop]
        spread = mm(place, high) + mm(place, low)
        picked = jnp.sum(spread * chosen_ref[...], axis=-1, keepdims=True)
        slot_gate_ref[:, hop] = picked.reshape(LOCAL, CAP, 1)
        b_ref[:, hop] = mm(place, h2).astype(BF16).reshape(LOCAL, CAP, D)


def gate_rows(half, w, member, chosen, place, rows):
    gates, slot_gate, b = call(
        gate_kernel,
        "gate_rows",
        [w, member, chosen, place, *rows],
        [
            SMALL_SPEC,
            pl.BlockSpec((Z, T, LANES), lambda *_: (half, 0, 0)),
            None,
            pl.BlockSpec((Z, SLOTS, T), lambda *_: (half, 0, 0)),
        ]
        + [None] * Z,
        [
            shape((Z, T, LANES), F32),
            shape((LOCAL, Z, CAP, 1), F32),
            shape((LOCAL, Z, CAP, D), BF16),
        ],
        flops=2 * Z * SLOTS * T * D,
        moved=5 << 20,
    )
    return gates, slot_gate.reshape(LOCAL, Z * CAP, 1), b.reshape(LOCAL, Z * CAP, D)


def spread_kernel(place_ref, *refs):
    rows, out_ref = refs[:PEERS], refs[PEERS]
    for hop in range(PEERS):
        out_ref[:, hop] = mm(place_ref[hop], rows[hop][...]).astype(BF16).reshape(LOCAL, CAP, D)


def spread_rows(place, line, other):
    return call(
        spread_kernel,
        "spread_rows",
        [place, *line, *other],
        [None] + [DY_SPEC] * Z + [X_SPEC] * Z,
        [shape((LOCAL, PEERS, CAP, D), BF16)],
        flops=2 * PEERS * SLOTS * T * D,
        moved=8 << 20,
    )[0].reshape(LOCAL, PEERS * CAP, D)


def expert_step(expert, b_refs, dyr_ref, gate_refs, first, down, gy_ref, db_ref):
    rows = jnp.concatenate([ref[0] for ref in b_refs], axis=0)
    gate = jnp.concatenate([ref[0] for ref in gate_refs], axis=0)
    pre = mm(rows, first())
    gate_pre, up_pre = pre[:, :H], pre[:, H:]
    sigmoid = 1.0 / (1.0 + jnp.exp(-gate_pre))
    silu = gate_pre * sigmoid
    activated = (silu * up_pre).astype(BF16)
    result = mm_nt(activated, down()).astype(BF16).astype(F32)
    raw = dyr_ref[0].astype(F32)
    gy_ref[0] = (gate * result).astype(BF16)
    inner = jnp.sum(raw * result, axis=-1, keepdims=True)
    grad_rows = (gate * raw).astype(BF16)
    grad_act = mm(grad_rows, down())
    grad_gate = (grad_act * up_pre * sigmoid * (1.0 + gate_pre * (1.0 - sigmoid))).astype(BF16)
    grad_up = (grad_act * silu).astype(BF16)
    both = jnp.concatenate([grad_gate, grad_up], axis=1)
    db_ref[0, :, 0:D] = mm_nt(both, first()).astype(BF16)
    lane = lax.broadcasted_iota(jnp.int32, (PEERS * CAP, LANES), 1)
    high = inner.astype(BF16).astype(F32)
    low = inner - high
    tail = jnp.where(lane == expert, high, jnp.where(lane == expert + E, low, 0.0))
    db_ref[0, :, D : D + LANES] = tail.astype(BF16)
    return rows, both, grad_rows, activated


def expert_kernel(
    me_ref, b0_ref, b1_ref, dyr_ref, gate0_ref, gate1_ref, w_ref, gy_ref, db_ref, grad_ref
):
    rows, both, grad_rows, activated = expert_step(
        me_ref[0] * LOCAL + pl.program_id(0),
        (b0_ref, b1_ref),
        dyr_ref,
        (gate0_ref, gate1_ref),
        lambda: w_ref[0, :, 0 : 2 * H],
        lambda: w_ref[0, :, 2 * H : 3 * H],
        gy_ref,
        db_ref,
    )
    grad_ref[0, :, 0 : 2 * H] = mm_tn(rows, both).astype(BF16)
    grad_ref[0, :, 2 * H : 3 * H] = mm_tn(grad_rows, activated).astype(BF16)


def per_expert(*dims, first=0):
    return pl.BlockSpec((1,) + dims, lambda e: (e + first, 0, 0))


def row_specs(first):
    half = PEERS * CAP // 2
    return [
        SCALARS,
        per_expert(half, D, first=first),
        per_expert(half, D, first=first),
        per_expert(2 * half, D, first=first),
        per_expert(half, 1, first=first),
        per_expert(half, 1, first=first),
    ]


def experts(me, b, dyr, slot_gate, pack):
    rows = PEERS * CAP
    return pl.pallas_call(
        expert_kernel,
        grid=(PLAIN,),
        in_specs=row_specs(0) + [per_expert(D, 3 * H)],
        out_specs=[per_expert(rows, D), per_expert(rows, D + LANES), per_expert(D, 3 * H)],
        out_shape=[
            shape((PLAIN, rows, D), BF16),
            shape((PLAIN, rows, D + LANES), BF16),
            shape((PLAIN, D, 3 * H), BF16),
        ],
        compiler_params=params(),
        cost_estimate=cost(18 * PLAIN * rows * D * H, 12 * PLAIN << 20),
        name="experts",
    )(me, *b, dyr, *slot_gate, pack)


def extra_kernel(
    me_ref,
    b0_ref,
    b1_ref,
    dyr_ref,
    gate0_ref,
    gate1_ref,
    dests_ref,
    w_ref,
    gy_ref,
    db_ref,
    keep_ref,
    give_ref,
    grads,
):
    rows, both, grad_rows, activated = expert_step(
        me_ref[0] * LOCAL + PLAIN + pl.program_id(0),
        (b0_ref, b1_ref),
        dyr_ref,
        (gate0_ref, gate1_ref),
        lambda: w_ref[0, :, 0 : 2 * H],
        lambda: w_ref[0, :, 2 * H : 3 * H],
        gy_ref,
        db_ref,
    )
    grads[:, :, 0 : 2 * H] = mm_tn(rows, both).astype(BF16).reshape(SHARDS, ROWS, 2 * H)
    grads[:, :, 2 * H : 3 * H] = mm_tn(grad_rows, activated).astype(BF16).reshape(SHARDS, ROWS, H)
    for chip in range(CHIPS):
        keep_ref[chip, 0] = grads[dests_ref[chip]]
        give_ref[chip, 0] = grads[dests_ref[CHIPS + chip]]


def extra_experts(me, b, dyr, slot_gate, dests, pack):
    rows = PEERS * CAP
    blocks = pl.BlockSpec((CHIPS, 1, ROWS, 3 * H), lambda e: (0, e, 0, 0))
    return pl.pallas_call(
        extra_kernel,
        grid=(EXTRA,),
        in_specs=row_specs(PLAIN) + [SCALARS, per_expert(D, 3 * H, first=PLAIN)],
        out_specs=[per_expert(rows, D), per_expert(rows, D + LANES), blocks, blocks],
        out_shape=[
            shape((EXTRA, rows, D), BF16),
            shape((EXTRA, rows, D + LANES), BF16),
            shape((CHIPS, EXTRA, ROWS, 3 * H), BF16),
            shape((CHIPS, EXTRA, ROWS, 3 * H), BF16),
        ],
        scratch_shapes=[pltpu.VMEM((SHARDS, ROWS, 3 * H), BF16)],
        compiler_params=params(),
        cost_estimate=cost(18 * EXTRA * rows * D * H, 14 * EXTRA << 20),
        name="extra_experts",
    )(me, *b, dyr, *slot_gate, dests, pack)


def extra_halves_kernel(keep_ref, got_ref, line_ref, cross_ref):
    total = (keep_ref[0].astype(F32) + got_ref[0].astype(F32)).astype(BF16)

    @pl.when(pl.program_id(0) < LINE)
    def _():
        cross_ref[0] = total

    @pl.when(pl.program_id(0) >= LINE)
    def _():
        line_ref[0] = total


def extra_halves(keep, got):
    block = (1, EXTRA, ROWS, 3 * H)
    return pl.pallas_call(
        extra_halves_kernel,
        grid=(CHIPS,),
        in_specs=[pl.BlockSpec(block, lambda i: ((i + LINE) % CHIPS, 0, 0, 0))] * 2,
        out_specs=[
            pl.BlockSpec(block, lambda i: (jnp.maximum(i - LINE, 0), 0, 0, 0)),
            pl.BlockSpec(block, lambda i: (jnp.minimum(i, LINE - 1), 0, 0, 0)),
        ],
        out_shape=[shape((LINE, EXTRA, ROWS, 3 * H), BF16)] * 2,
        compiler_params=params(),
        cost_estimate=cost(keep.size, 6 * keep.size),
        name="extra_halves",
    )(keep, got)


def extra_lines_kernel(line_ref, got_ref, *outs):
    for hop in range(LINE):
        outs[hop][...] = (line_ref[hop].astype(F32) + got_ref[hop].astype(F32)).astype(BF16)


def extra_lines(line, got):
    return call(
        extra_lines_kernel,
        "extra_lines",
        [line, got],
        [None, None],
        [shape((EXTRA, ROWS, 3 * H), BF16)] * LINE,
        flops=line.size,
        moved=6 * line.size,
    )


def collect_kernel(place_ref, plain_ref, extra_ref, *out_refs):
    for hop in range(PEERS):
        rows = jnp.concatenate(
            [ref[:, hop].reshape(-1, ref.shape[-1]) for ref in (plain_ref, extra_ref)], axis=0
        )
        out_refs[hop][...] = mm_tn(place_ref[hop], rows).astype(BF16)


def collect(place, values, name):
    width = values[0].shape[-1]
    return call(
        collect_kernel,
        name,
        [place, *(v.reshape(-1, PEERS, CAP, width) for v in values)],
        [None] * 3,
        [shape((T, width), BF16)] * PEERS,
        flops=2 * PEERS * SLOTS * T * width,
        moved=8 << 20,
    )


def mix(x1, returns, other):
    return call(
        add_kernel,
        "mix",
        [x1, *returns, other],
        [None] + [DY_SPEC] * Z + [None],
        [shape((T, D), BF16)],
        flops=T * D * Z,
        moved=4 << 20,
    )[0]


def norm_back(grad, normed, inverse, gain):
    scaled = grad * gain
    return inverse * (scaled - normed * jnp.mean(scaled * normed, axis=-1, keepdims=True))


def token_back_kernel(
    x1_ref, dy_ref, gates_ref, small_ref, gains_ref, *refs
):
    parts, (dx1_ref, dlogits_ref, scaled_ref, da_ref) = refs[: Z + 1], refs[Z + 1 :]
    total = parts[0][...].astype(F32)
    for ref in parts[1:]:
        total = total + ref[...].astype(F32)
    grad, tail = total[:, :D], total[:, D:]
    lane = lax.broadcasted_iota(jnp.int32, (T, LANES), 1)
    inner = jnp.where(lane < E, tail + pltpu.roll(tail, LANES - E, 1), 0.0)
    gates = gates_ref[0]
    score = gates * (inner - jnp.sum(gates * inner, axis=-1, keepdims=True))
    dlogits_ref[...] = score.astype(BF16)
    grad = grad + mm_nt(dlogits_ref[...], small_of(small_ref))
    normed, inverse = norm_of(x1_ref[...])
    scaled_ref[...] = (grad * normed).astype(BF16)
    through = dy_ref[...].astype(F32) + norm_back(grad, normed, inverse, gains_ref[1:2, :])
    dx1_ref[...] = through
    da_ref[...] = through.astype(BF16)


def token_back(x1, dy, gates, w, gains, parts):
    return call(
        token_back_kernel,
        "token_back",
        [x1, dy, gates, w, gains, *parts],
        [None, None, pl.BlockSpec((1, T, LANES), lambda *_: (0, 0, 0)), SMALL_SPEC]
        + [None] * (1 + len(parts)),
        [
            shape((T, D), F32),
            shape((T, LANES), BF16),
            shape((T, D), BF16),
            shape((T, D), BF16),
        ],
        flops=T * D * 64,
        moved=6 << 20,
    )


def shadow_kernel(qkv_ref, h2_ref, dlogits_ref, scaled_ref, *refs):
    xs, (small_ref, inverse_ref, prob_ref) = refs[:Z], refs[Z:]
    lane = lax.broadcasted_iota(jnp.int32, (T, LANES), 1)
    small = mm_tn(h2_ref[...], dlogits_ref[...])
    small_ref[...] = small + mm_tn(scaled_ref[...], (lane == E + 1).astype(BF16))
    for hop in range(Z):
        rows = slice(hop * T, (hop + 1) * T)
        _, inverse = norm_of(xs[hop][...].astype(F32))
        inverse_ref[rows] = inverse
        for group in range(KH):
            query = stack_heads(qkv_ref, rows, group * GROUP)
            prob_ref[hop * KH + group] = probabilities(query, head(qkv_ref, rows, QH + group))


def shadow(qkv, h2, dlogits, scaled, xs):
    return call(
        shadow_kernel,
        "shadow",
        [qkv, h2, dlogits, scaled, *xs],
        [None] * 4 + [X_SPEC] * Z,
        [
            shape((D, LANES), F32),
            shape((Z * T, 1), F32),
            shape((Z * KH, GROUP * T, T), F32),
        ],
        flops=Z * T * D * QW,
        moved=6 << 20,
    )


def head_back_kernel(
    behind_ref,
    parity_ref,
    qkv_ref,
    h1_ref,
    w_ref,
    full_ref,
    partial_ref,
    inverse_ref,
    prob_ref,
    cos_ref,
    sin_ref,
    *refs,
):
    xs, das, weights, results, outs = (refs[at * Z : at * Z + Z] for at in range(5))
    keep_ref, give_ref, dob, dqk, dqkv, h1, w, full, x, sems = refs[5 * Z :]
    late = [(h1_ref, h1), (w_ref, w), (full_ref, full)]
    late += [(xs[hop].at[:, pl.ds(0, D)], x.at[hop]) for hop in range(Z)]
    late += [(results[hop], outs[hop].at[:, pl.ds(D, D)]) for hop in range(Z)]
    late = [pltpu.make_async_copy(a, b, sems.at[at]) for at, (a, b) in enumerate(late)]
    for copy in late:
        copy.start()
    total = jnp.zeros((Z * T, QW), F32)
    for hop in range(Z):
        columns = columns_of(behind_ref[hop])
        rows = jnp.concatenate([ref[:, columns] for ref in das], axis=0)
        total = total + mm_nt(rows, weights[hop][...])
        if hop == 0:
            own_columns = rows
    dob[...] = total.astype(BF16)
    for hop in range(Z):
        rows = slice(hop * T, (hop + 1) * T)
        for group in range(KH):
            key, value = head(qkv_ref, rows, QH + group), head(qkv_ref, rows, QH + KH + group)
            query = stack_heads(qkv_ref, rows, group * GROUP)
            out_grad = stack_heads(dob, rows, group * GROUP)
            probability = prob_ref[hop * KH + group]
            grad_prob = mm_nt(out_grad, value)
            held = jnp.sum(probability * grad_prob, axis=-1, keepdims=True)
            grad_scores = (probability * (grad_prob - held)).astype(BF16)
            grad_query = mm(grad_scores, key) * SCALE
            for index in range(GROUP):
                at = (group * GROUP + index) * HEAD_DIM
                dqk[rows, at : at + HEAD_DIM] = grad_query[index * T : (index + 1) * T]
            at = QW + group * HEAD_DIM
            dqk[rows, at : at + HEAD_DIM] = mm_tn(grad_scores, query) * SCALE
            dqkv[rows, at + KW : at + KW + HEAD_DIM] = mm_tn(
                probability.astype(BF16), out_grad
            ).astype(BF16)
    cosine = jnp.concatenate([cos_ref[...]] * Z, axis=0)
    signed = jnp.concatenate([sin_ref[...]] * Z, axis=0)
    dqkv[:, 0 : QW + KW] = rotate_back(dqk[...], cosine, signed).astype(BF16)
    even = parity_ref[0] == 0

    def store(grads, columns):
        pair = grads.astype(BF16).reshape(CHIPS, 2, ROWS, grads.shape[1])
        keep_ref[:, :, columns] = jnp.where(even, pair[:, 0], pair[:, 1])
        give_ref[:, :, columns] = jnp.where(even, pair[:, 1], pair[:, 0])

    late[2].wait()
    store(mm_tn(full[...], own_columns), slice(0, QW))
    late[0].wait()
    store(mm_tn(h1[...], dqkv[...]), slice(QW, MAIN))
    late[1].wait()
    dh1 = mm_nt(dqkv[...], w[:, :, 0:QKV].reshape(D, QKV))
    lane = lax.broadcasted_iota(jnp.int32, (T, LANES), 1)
    first = (lane == E).astype(BF16)
    small = partial_ref[...]
    for hop in range(Z):
        rows = slice(hop * T, (hop + 1) * T)
        piece = dh1[rows]
        late[3 + hop].wait()
        normed = x[hop].astype(F32) * inverse_ref[rows]
        small += mm_tn((piece * normed).astype(BF16), first)
        outs[hop][:, 0:D] = piece.astype(BF16)
        late[3 + Z + hop].wait()
    store(small, slice(MAIN, SLICE))


def head_back(behind, parity, qkv, h1, w, full, shadows, cosine, signed, xs, das, weights, results):
    return call(
        head_back_kernel,
        "head_back",
        [behind, parity, qkv, h1, w, full, *shadows, cosine, signed, *xs, *das, *weights, *results],
        [SCALARS] * 2
        + [None, ANYWHERE, ANYWHERE, ANYWHERE]
        + [None] * 5
        + [ANYWHERE] * Z
        + [None] * (2 * Z)
        + [ANYWHERE] * Z,
        [shape((T, 2 * D), BF16)] * Z + [shape((CHIPS, ROWS, SLICE), BF16)] * 2,
        scratch=[
            pltpu.VMEM((Z * T, QW), BF16),
            pltpu.VMEM((Z * T, QW + KW), F32),
            pltpu.VMEM((Z * T, QKV), BF16),
            pltpu.VMEM((Z * T, D), BF16),
            pltpu.VMEM((SHARDS, ROWS, QKV + LANES), BF16),
            pltpu.VMEM((Z * T, D), BF16),
            pltpu.VMEM((Z, T, D), BF16),
            pltpu.SemaphoreType.DMA((3 + 2 * Z,)),
        ],
        flops=4 * Z * T * D * QKV,
        moved=16 << 20,
    )


def token_grad_kernel(x_ref, gains_ref, dx1_ref, *refs):
    grad = refs[0][...].astype(F32)
    for hop in range(1, Z):
        grad = grad + refs[hop][...].astype(F32)
    normed, inverse = norm_of(x_ref[...].astype(F32))
    refs[Z][...] = dx1_ref[...] + norm_back(grad, normed, inverse, gains_ref[0:1, :])


def token_grad(x, gains, dx1, pieces):
    return call(
        token_grad_kernel,
        "token_grad",
        [x, gains, dx1, *pieces],
        [None] * 3 + [X_SPEC] * Z,
        [shape((T, D), F32)],
        flops=T * D * 16,
        moved=4 << 20,
    )[0]


def split_kernel(order_ref, keep_ref, got_ref, *outs):
    for chip in range(CHIPS):
        at = order_ref[chip]
        total = (keep_ref[at].astype(F32) + got_ref[at].astype(F32)).astype(BF16)
        outs[chip % 4][chip // 4] = total


def split(order, keep, got):
    return call(
        split_kernel,
        "split",
        [order, keep, got],
        [SCALARS, None, None],
        [shape((2, ROWS, SLICE), BF16)] * 4,
        flops=CHIPS * ROWS * SLICE,
        moved=6 << 20,
    )


def add_kernel(*refs):
    total = refs[0][...].astype(F32)
    for ref in refs[1:-1]:
        total = total + ref[...].astype(F32)
    refs[-1][...] = total.astype(BF16)


def sum_lines_kernel(*refs):
    for at in range(2):
        total = refs[0][at].astype(F32)
        for ref in refs[1:LINE]:
            total = total + ref[at].astype(F32)
        refs[LINE + at][...] = total.astype(BF16)


def sum_lines(parts):
    return call(
        sum_lines_kernel,
        "sum_lines",
        list(parts),
        [None] * LINE,
        [shape((ROWS, SLICE), BF16)] * 2,
        flops=LINE * ROWS * SLICE,
        moved=12 * ROWS * SLICE,
    )


def add_all(parts, name):
    return call(
        add_kernel,
        name,
        list(parts),
        [None] * len(parts),
        [shape(parts[0].shape, BF16)],
        flops=parts[0].size * len(parts),
        moved=2 * parts[0].size * (len(parts) + 1),
    )[0]


def finish_kernel(order_ref, *refs):
    parts, (q_ref, k_ref, v_ref, o_ref, router_ref, one_ref, two_ref, narrow) = refs[:Z], refs[Z:]
    for hop in range(Z):
        at = order_ref[hop]
        part = parts[hop][...].astype(F32)
        o_ref[:, columns_of(at)] = part[:, 0:QW]
        q_ref[:, columns_of(at)] = part[:, QW : 2 * QW]
        heads = pl.ds(pl.multiple_of(at * KW, KW), KW)
        k_ref[:, heads] = part[:, 2 * QW : 2 * QW + KW]
        v_ref[:, heads] = part[:, 2 * QW + KW : MAIN]
        narrow[at] = part[:, MAIN:]
    small = (narrow[0] + narrow[1] + narrow[2] + narrow[3]).T
    router_ref[...] = small[0:E]
    one_ref[...] = small[E : E + 1]
    two_ref[...] = small[E + 1 : E + 2]


def finish(order, parts):
    return call(
        finish_kernel,
        "finish",
        [order, *parts],
        [SCALARS] + [None] * Z,
        [
            shape((ROWS, D), F32),
            shape((ROWS, KEY_VALUE_HEADS * HEAD_DIM), F32),
            shape((ROWS, KEY_VALUE_HEADS * HEAD_DIM), F32),
            shape((ROWS, D), F32),
            shape((E, ROWS), F32),
            shape((1, ROWS), F32),
            shape((1, ROWS), F32),
        ],
        scratch=[pltpu.VMEM((Z, ROWS, LANES), F32)],
        flops=ROWS * SLICE * Z,
        moved=3 << 20,
    )


def unpack_kernel(share_ref, *refs):
    parts, outs = refs[:LINE], refs[LINE:]

    def store(value):
        for at in range(3):
            outs[at][0] = value[:, at * H : (at + 1) * H]

    @pl.when(pl.program_id(0) < PLAIN)
    def _():
        store(share_ref[0].astype(F32))

    @pl.when(pl.program_id(0) >= PLAIN)
    def _():
        total = parts[0][0].astype(F32)
        for ref in parts[1:]:
            total = total + ref[0].astype(F32)
        store(total)


def unpack(share, parts):
    block = (1, ROWS, 3 * H)
    return pl.pallas_call(
        unpack_kernel,
        grid=(LOCAL,),
        in_specs=[pl.BlockSpec(block, lambda e: (jnp.minimum(e, PLAIN - 1), 0, 0))]
        + [pl.BlockSpec(block, lambda e: (jnp.maximum(e - PLAIN, 0), 0, 0))] * LINE,
        out_specs=[per_expert(ROWS, H)] * 3,
        out_shape=[shape((LOCAL, ROWS, H), F32)] * 3,
        compiler_params=params(),
        cost_estimate=cost(LOCAL * ROWS * 3 * H, 5 << 20),
        name="unpack",
    )(share, *parts)


def spread_tables(all_routes, me):
    lane = jnp.arange(LANES, dtype=jnp.int32)
    member = jnp.sum((all_routes[..., None] == lane).astype(F32), axis=2)
    mine = me * LOCAL + jnp.arange(LOCAL, dtype=jnp.int32)
    own = jnp.sum((all_routes[..., None] == mine).astype(F32), axis=2)
    earlier = (np.arange(T)[:, None] > np.arange(T)[None, :]).astype(np.float32)
    before = jnp.einsum(
        "ts,rse->rte", jnp.asarray(earlier, BF16), own.astype(BF16), preferred_element_type=F32
    )
    slots = jnp.where(own > 0.5, before.astype(jnp.int32), -1)
    slots = jnp.swapaxes(slots, 1, 2)[:, :, None, :]
    place = slots == jnp.arange(CAP, dtype=jnp.int32)[None, None, :, None]
    return member, place.astype(BF16).reshape(PEERS, SLOTS, T)


def body(
    tokens,
    cotangent,
    routes,
    norm_one,
    w_query,
    key_weight,
    value_weight,
    w_out,
    norm_two,
    w_router,
    w_gate,
    w_up,
    w_down,
):
    me = lax.axis_index("expert")
    place_in_group = lax.axis_index("fsdp")
    z = me % Z
    core = place_in_group % 2
    cosine, signed = (jnp.asarray(table) for table in rope_tables())

    first, second = pack(
        z.astype(jnp.int32)[None],
        w_out,
        w_query,
        key_weight,
        value_weight,
        w_router.T,
        norm_one[None, :],
        norm_two[None, :],
    )
    def spread_over_chips(value):
        pair = jnp.stack([value, send_chip(value, LINE)])
        own = [send_chip(pair, hop) for hop in range(LINE)]
        return own, [swap_core(value) for value in own]

    own, other = spread_over_chips(first)
    out_own, _ = spread_over_chips(after(second, own[1]))
    sources = jnp.stack([chip_at(place_in_group, hop, True) for hop in range(CHIPS)])
    order = jnp.concatenate([2 * sources + core, 2 * sources + 1 - core]).astype(jnp.int32)
    dests = jnp.stack([chip_at(place_in_group, hop) for hop in range(CHIPS)]).astype(jnp.int32)
    twins = jnp.concatenate([2 * dests + core, 2 * dests + 1 - core])
    expert_pack = lax.all_gather(
        jnp.concatenate([w_gate, w_up, jnp.swapaxes(w_down, 1, 2)], axis=2),
        "fsdp",
        axis=1,
        tiled=True,
    )

    behind = jnp.stack([(z + Z - hop) % Z for hop in range(Z)]).astype(jnp.int32)
    ahead = jnp.stack([(z + hop) % Z for hop in range(Z)]).astype(jnp.int32)

    marks = jnp.pad(routes, ((0, 0), (0, LANES - TOPK))).astype(BF16)
    early = jnp.concatenate([cotangent, marks], axis=1)
    whole_row = jnp.concatenate([tokens, early], axis=1)
    whole_row = after(whole_row, first)
    xs = [send(whole_row, hop) for hop in (0, 1, 3)]
    xs.insert(2, send(whole_row, 2))
    w, gains, h1, qkv, ob = project(order, cosine, signed, own, other, xs)
    obs = [send(ob, hop) for hop in range(Z)]
    out_other = [swap_core(after(value, ob)) for value in out_own]
    early_other = send(after(early, xs[3]), Z)
    w_out_slice, ob_full, *x1_columns = out_project(behind, order, out_own, out_other, obs)
    x1_pieces = [send(x1_columns[hop], hop, True) for hop in range(Z)]
    early_other = after(early_other, x1_pieces[1])
    early_other = [send(early_other, hop) for hop in range(Z)]
    x1, h2 = residual(ahead, tokens, gains, x1_pieces)
    h2_other = send(h2, Z)
    h2_line = [send(h2, hop) for hop in range(Z)]
    h2_other = [send(h2_other, hop) for hop in range(Z)]

    all_routes = jnp.stack(
        [r[:, 2 * D : 2 * D + TOPK].astype(jnp.int32) for r in xs]
        + [r[:, D : D + TOPK].astype(jnp.int32) for r in early_other]
    )
    member, place = spread_tables(all_routes, me)
    row_expert = me * LOCAL + jnp.arange(SLOTS, dtype=jnp.int32) // CAP
    chosen = (row_expert[:, None] == jnp.arange(LANES, dtype=jnp.int32)[None, :]).astype(F32)
    dyr = spread_rows(place, xs, early_other)

    gates, gate0, b0 = gate_rows(0, w, member, chosen, place, h2_line)
    _, gate1, b1 = gate_rows(1, w, member, chosen, place, h2_other)
    b, slot_gate = (b0, b1), (gate0, gate1)
    weights = after(cut_out(ahead, after(w_out_slice, x1)), b1)
    slot_gate = after(slot_gate, *weights)
    weights = [send(weights[hop], hop) for hop in range(Z)]
    number = me.astype(jnp.int32)[None]
    gy, db, grad_pack = experts(number, b, dyr, slot_gate, expert_pack)
    extra_gy, extra_db, keep_extra, give_extra = extra_experts(
        after(number, db), b, dyr, slot_gate, twins, expert_pack
    )
    db_parts = collect(place, after((db, extra_db), *weights[1:]), "collect_grads")
    grad_cross = [send(db_parts[Z + hop], hop, True) for hop in range(Z)]
    grad_line = after(db_parts[:Z], *grad_cross[1:])
    grad_line = [send(grad_line[hop], hop, True) for hop in range(Z)]
    got_extra = swap_core(give_extra)
    grad_other = send(add_all(grad_cross, "line_grads"), Z)
    expert_share = lax.psum_scatter(
        after(grad_pack, *weights[1:]), "fsdp", scatter_dimension=1, tiled=True
    )
    results = collect(place, (gy, extra_gy), "collect_results")
    grad_line = after(grad_line, results)
    dx1, dlogits, scaled, da = token_back(x1, cotangent, gates, w, gains, [*grad_line, grad_other])
    das = [send(da, hop) for hop in range(Z)]
    extra_line, extra_cross = extra_halves(keep_extra, after(got_extra, da))
    shadows = shadow(after(qkv, extra_cross), h2, dlogits, scaled, xs)
    results = after(results, shadows[1], *das[1:])
    results_cross = [send(results[Z + hop], hop, True) for hop in range(Z)]
    *returns, keep, give = head_back(
        behind,
        core.astype(jnp.int32)[None],
        qkv,
        h1,
        w,
        ob_full,
        shadows,
        cosine,
        signed,
        xs,
        das,
        weights,
        results[:Z],
    )
    parts = split(dests, keep, swap_core(after(give, *results_cross[1:])))
    extra_got = send_chip(extra_cross, LINE)
    parts = after(parts, expert_share)
    lines = [send_chip(parts[hop], hop) for hop in range(LINE)]
    results_other = send(add_all(results_cross, "line_results"), Z)
    first, third = send(returns[1], 1, True), send(returns[3], 3, True)
    lines[0] = after(lines[0], first, third)
    second = send(after(returns[2], first, third), 2, True)
    returns = [returns[0], first, second, third]
    share = sum_lines(lines)
    extra_parts = extra_lines(extra_line, after(extra_got, share[1]))
    share = add_all([share[0], send_chip(share[1], LINE)], "sum_chips")
    share = add_all([share, send(share, Z)], "sum_halves")
    extra_first, extra_third = (send_chip(extra_parts[hop], hop) for hop in (1, 3))
    share = after(share, second)
    extra_second = send_chip(extra_parts[2], 2)
    extra_parts = [extra_parts[0], extra_first, extra_second, extra_third]
    shares = [send(share, hop) for hop in range(Z)]
    grad_gate, grad_up, grad_down = unpack(expert_share, extra_parts)
    grad_tokens = token_grad(tokens, gains, dx1, returns)
    mixed_out = mix(x1, returns, results_other)
    shares = after(shares, grad_tokens, mixed_out, grad_gate)
    grad_query, grad_key, grad_value, grad_out, router, one, two = finish(behind, shares)

    return (
        mixed_out,
        grad_tokens,
        one.reshape(ROWS),
        grad_query,
        grad_key,
        grad_value,
        grad_out,
        two.reshape(ROWS),
        router.T,
        grad_gate,
        grad_up,
        jnp.swapaxes(grad_down, 1, 2),
    )


def solution(mesh):
    return jax.shard_map(
        body,
        mesh=mesh,
        in_specs=(
            P(("expert", "fsdp"), None),
            P(("expert", "fsdp"), None),
            P(("expert", "fsdp"), None),
            P("fsdp"),
            P("fsdp", None),
            P("fsdp", None),
            P("fsdp", None),
            P("fsdp", None),
            P("fsdp"),
            P("fsdp", None),
            P("expert", "fsdp", None),
            P("expert", "fsdp", None),
            P("expert", None, "fsdp"),
        ),
        out_specs=(
            P(("expert", "fsdp"), None),
            P(("expert", "fsdp"), None),
            P("fsdp"),
            P("fsdp", None),
            P("fsdp", None),
            P("fsdp", None),
            P("fsdp", None),
            P("fsdp"),
            P("fsdp", None),
            P("expert", "fsdp", None),
            P("expert", "fsdp", None),
            P("expert", None, "fsdp"),
        ),
        check_vma=False,
    )
```

```python
import jax
import jax.numpy as jnp
import numpy as np
from jax import lax
from jax.experimental import pallas as pl
from jax.experimental.pallas import tpu as pltpu
from jax.sharding import PartitionSpec as P

QUERY_HEADS = 24
KEY_VALUE_HEADS = 8
GROUP = QUERY_HEADS // KEY_VALUE_HEADS
HEAD_DIM = 64
HALF = HEAD_DIM // 2
E = 40
H = 512
D = 1536
T = 128
CAP = 32
NORM_EPSILON = 1e-05
SCALE = HEAD_DIM ** (-0.5)

Z = 4
PEERS = 8
LOCAL = E // PEERS
SLOTS = LOCAL * CAP
EXTRA = 1
PLAIN = LOCAL - EXTRA
LANES = 128
CHIPS = 8
LINE = 4
TOPK = 8
SHARDS = 2 * CHIPS
ROWS = D // SHARDS
QH = QUERY_HEADS // Z
KH = KEY_VALUE_HEADS // Z
QW = QH * HEAD_DIM
KW = KH * HEAD_DIM
QKV = QW + 2 * KW
MAIN = QW + QKV
SLICE = MAIN + LANES
VMEM_LIMIT = 60 * 1024 * 1024

F32 = jnp.float32
BF16 = jnp.bfloat16


def peer(index, hop, back=False):
    shift = hop % Z
    turned = (index % Z + (Z - shift if back else shift)) % Z
    return (index // Z + hop // Z) % 2 * Z + turned


def send(value, hop, back=False):
    if hop == 0:
        return value
    return lax.ppermute(value, "expert", [(i, peer(i, hop, back)) for i in range(PEERS)])


def chip_at(index, hop, back=False):
    shift = hop % 4
    turned = (index // 2 % 4 + (4 - shift if back else shift)) % 4
    return (index // 8 + hop // 4) % 2 * 4 + turned


def send_chip(value, hop):
    if hop == 0:
        return value
    pairs = [(i, 2 * chip_at(i, hop) + i % 2) for i in range(SHARDS)]
    return lax.ppermute(value, "fsdp", pairs)


def after(value, *others):
    return lax.optimization_barrier((value, others))[0]


def swap_core(value):
    return lax.ppermute(value, "fsdp", [(i, i ^ 1) for i in range(SHARDS)])


def mm(left, right):
    return jnp.dot(left, right, preferred_element_type=F32)


def mm_nt(left, right):
    return lax.dot_general(left, right, (((1,), (1,)), ((), ())), preferred_element_type=F32)


def mm_tn(left, right):
    return lax.dot_general(left, right, (((0,), (0,)), ((), ())), preferred_element_type=F32)


def rope_tables():
    frequency = np.exp(-np.log(10000.0) * np.arange(HALF, dtype=np.float64) * 2.0 / HEAD_DIM)
    angles = np.arange(T, dtype=np.float64)[:, None] * frequency[None, :]
    cosine = np.tile(np.cos(angles), (1, 4)).astype(np.float32)
    sine = np.sin(angles)
    signed = np.tile(np.concatenate([-sine, sine], axis=1), (1, 2)).astype(np.float32)
    return cosine, signed


def swap_halves(values):
    width = values.shape[1]
    lane = lax.broadcasted_iota(jnp.int32, values.shape, 1)
    up = pltpu.roll(values, width - HALF, 1)
    down = pltpu.roll(values, HALF, 1)
    return jnp.where(lane % HEAD_DIM < HALF, up, down)


def wide(table, width):
    return jnp.concatenate([table] * (width // LANES), axis=1)


def rotate(values, cosine, signed):
    width = values.shape[1]
    return values * wide(cosine, width) + swap_halves(values) * wide(signed, width)


def rotate_back(values, cosine, signed):
    width = values.shape[1]
    return values * wide(cosine, width) + swap_halves(values * wide(signed, width))


def gain_rows(small):
    pick = lax.broadcasted_iota(jnp.int32, (16, LANES), 1) == (
        lax.broadcasted_iota(jnp.int32, (16, LANES), 0) + E
    )
    return mm_nt(pick.astype(BF16), small)


def norm_of(values):
    inverse = lax.rsqrt(jnp.mean(values * values, axis=-1, keepdims=True) + NORM_EPSILON)
    return values * inverse, inverse


def head(ref, rows, index):
    return ref[rows, index * HEAD_DIM : (index + 1) * HEAD_DIM]


def stack_heads(ref, rows, first):
    return jnp.concatenate([head(ref, rows, first + index) for index in range(GROUP)], axis=0)


def probabilities(query, key):
    scores = mm_nt(query, key) * SCALE
    rows = lax.broadcasted_iota(jnp.int32, scores.shape, 0) % T
    cols = lax.broadcasted_iota(jnp.int32, scores.shape, 1)
    scores = jnp.where(rows >= cols, scores, -jnp.inf)
    exponent = jnp.exp(scores - jnp.max(scores, axis=-1, keepdims=True))
    return exponent / jnp.sum(exponent, axis=-1, keepdims=True)


def whole(shape):
    return pl.BlockSpec(shape, lambda *_: (0,) * len(shape))


SCALARS = pl.BlockSpec(memory_space=pltpu.SMEM)
ANYWHERE = pl.BlockSpec(memory_space=pl.ANY)


def params(**more):
    return pltpu.CompilerParams(vmem_limit_bytes=VMEM_LIMIT, **more)


WEIGHT = 60


def cost(flops, moved):
    return pl.CostEstimate(flops=flops * WEIGHT, bytes_accessed=moved * WEIGHT, transcendentals=0)


def shape(dims, kind):
    return jax.ShapeDtypeStruct(dims, kind)


def call(kernel, name, inputs, in_specs, outputs, out_specs=None, scratch=(), flops=0, moved=0):
    in_specs = [whole(v.shape) if spec is None else spec for v, spec in zip(inputs, in_specs)]
    if out_specs is None:
        out_specs = [whole(o.shape) for o in outputs]
    return pl.pallas_call(
        kernel,
        grid=(1,),
        in_specs=in_specs,
        out_specs=out_specs,
        out_shape=outputs,
        scratch_shapes=list(scratch),
        compiler_params=params(),
        cost_estimate=cost(flops, moved),
        name=name,
    )(*inputs)


SMALL_SPEC = pl.BlockSpec((SHARDS, ROWS, LANES), lambda *_: (0, 0, QKV // LANES))
X_SPEC = pl.BlockSpec((T, D), lambda *_: (0, 0))
DY_SPEC = pl.BlockSpec((T, D), lambda *_: (0, 1))


def small_of(ref):
    return ref[...].reshape(D, LANES)


def columns_of(index):
    return pl.ds(pl.multiple_of(index * QW, QW), QW)


def pack_kernel(
    z_ref, out_ref, query_ref, key_ref, value_ref, router_ref, one_ref, two_ref, first_ref, second_ref
):
    first_ref[:, 0:QW] = query_ref[...]
    first_ref[:, QW : QW + KW] = key_ref[...]
    first_ref[:, QW + KW : QKV] = value_ref[...]
    narrow = [router_ref[...], one_ref[...], two_ref[...], jnp.zeros((LANES - E - 2, ROWS), BF16)]
    first_ref[:, QKV:] = jnp.concatenate([v.astype(F32) for v in narrow], axis=0).T.astype(BF16)
    second_ref[...] = out_ref[...]


def pack(z, w_out, w_query, key_weight, value_weight, router, one, two):
    def slice_of(width):
        return pl.BlockSpec((ROWS, width), lambda i, z: (0, z[0]))

    return pl.pallas_call(
        pack_kernel,
        grid_spec=pltpu.PrefetchScalarGridSpec(
            num_scalar_prefetch=1,
            grid=(1,),
            in_specs=[
                slice_of(QW),
                slice_of(QW),
                slice_of(KW),
                slice_of(KW),
                whole((E, ROWS)),
                whole((1, ROWS)),
                whole((1, ROWS)),
            ],
            out_specs=[whole((ROWS, QKV + LANES)), whole((ROWS, QW))],
        ),
        out_shape=[shape((ROWS, QKV + LANES), BF16), shape((ROWS, QW), BF16)],
        compiler_params=params(),
        cost_estimate=cost(ROWS * SLICE, 1 << 20),
        name="pack",
    )(z, w_out, w_query, key_weight, value_weight, router, one, two)


def project_kernel(order_ref, cos_ref, sin_ref, *refs):
    own, other, xs = refs[:LINE], refs[LINE : 2 * LINE], refs[2 * LINE : 2 * LINE + Z]
    w_ref, gains_ref, h1_ref, qkv_ref, ob_ref = refs[2 * LINE + Z :]
    for chip in range(CHIPS):
        w_ref[order_ref[chip]] = own[chip % LINE][chip // LINE]
        w_ref[order_ref[CHIPS + chip]] = other[chip % LINE][chip // LINE]
    gains = gain_rows(w_ref[:, :, QKV:].reshape(D, LANES))
    gains_ref[...] = gains
    for hop in range(Z):
        normed, _ = norm_of(xs[hop][...].astype(F32))
        h1_ref[hop * T : (hop + 1) * T] = (normed * gains[0:1, :]).astype(BF16)
    pre = mm(h1_ref[...], w_ref[:, :, 0:QKV].reshape(D, QKV))
    cosine = jnp.concatenate([cos_ref[...]] * Z, axis=0)
    signed = jnp.concatenate([sin_ref[...]] * Z, axis=0)
    qkv_ref[:, 0:QW] = rotate(pre[:, 0:QW], cosine, signed).astype(BF16)
    qkv_ref[:, QW : QW + KW] = rotate(pre[:, QW : QW + KW], cosine, signed).astype(BF16)
    qkv_ref[:, QW + KW :] = pre[:, QW + KW :].astype(BF16)
    for hop in range(Z):
        rows = slice(hop * T, (hop + 1) * T)
        for group in range(KH):
            key, value = head(qkv_ref, rows, QH + group), head(qkv_ref, rows, QH + KH + group)
            query = stack_heads(qkv_ref, rows, group * GROUP)
            result = mm(probabilities(query, key).astype(BF16), value).astype(BF16)
            for index in range(GROUP):
                at = (group * GROUP + index) * HEAD_DIM
                ob_ref[rows, at : at + HEAD_DIM] = result[index * T : (index + 1) * T]


def project(order, cosine, signed, own, other, xs):
    return call(
        project_kernel,
        "project",
        [order, cosine, signed, *own, *other, *xs],
        [SCALARS] + [None] * (2 + 2 * LINE) + [X_SPEC] * Z,
        [
            shape((SHARDS, ROWS, QKV + LANES), BF16),
            shape((16, D), F32),
            shape((Z * T, D), BF16),
            shape((Z * T, QKV), BF16),
            shape((Z * T, QW), BF16),
        ],
        flops=2 * Z * T * D * QKV,
        moved=12 << 20,
    )


def out_project_kernel(peers_ref, order_ref, *refs):
    own, other, obs = refs[:LINE], refs[LINE : 2 * LINE], refs[2 * LINE : 2 * LINE + Z]
    w_ref, full_ref, *outs = refs[2 * LINE + Z :]
    for chip in range(CHIPS):
        w_ref[order_ref[chip]] = own[chip % LINE][chip // LINE]
        w_ref[order_ref[CHIPS + chip]] = other[chip % LINE][chip // LINE]
    total = jnp.zeros((Z * T, QW), F32)
    for hop in range(Z):
        peer_index = peers_ref[hop]
        blocks = [(row - hop) % Z for row in range(Z)]
        rows = jnp.concatenate([obs[hop][b * T : (b + 1) * T, :] for b in blocks], axis=0)
        full_ref[:, columns_of(peer_index)] = rows
        weight = w_ref[pl.ds(peer_index * Z, Z)].reshape(QW, QW)
        total = total + mm(rows, weight)
    for hop in range(Z):
        outs[hop][...] = total[hop * T : (hop + 1) * T].astype(BF16)


def out_project(peers, order, own, other, obs):
    return call(
        out_project_kernel,
        "out_project",
        [peers, order, *own, *other, *obs],
        [SCALARS] * 2 + [None] * (2 * LINE + Z),
        [shape((SHARDS, ROWS, QW), BF16), shape((Z * T, D), BF16)] + [shape((T, QW), BF16)] * Z,
        flops=2 * Z * T * D * QW,
        moved=6 << 20,
    )


def cut_out_kernel(peers_ref, w_ref, *outs):
    for hop in range(Z):
        outs[hop][...] = w_ref[pl.ds(peers_ref[hop] * Z, Z)].reshape(QW, QW)


def cut_out(peers, w):
    return call(
        cut_out_kernel,
        "cut_out",
        [peers, w],
        [SCALARS, None],
        [shape((QW, QW), BF16)] * Z,
        flops=D * QW,
        moved=2 << 20,
    )


def residual_kernel(peers_ref, x_ref, gains_ref, *refs):
    pieces, (x1_ref, h2_ref) = refs[:Z], refs[Z:]
    x1_ref[...] = x_ref[...].astype(F32)
    for hop in range(Z):
        x1_ref[:, columns_of(peers_ref[hop])] += pieces[hop][...].astype(F32)
    normed, _ = norm_of(x1_ref[...])
    h2_ref[...] = (normed * gains_ref[1:2, :]).astype(BF16)


def residual(peers, x, gains, pieces):
    return call(
        residual_kernel,
        "residual",
        [peers, x, gains, *pieces],
        [SCALARS] + [None] * (2 + Z),
        [shape((T, D), F32), shape((T, D), BF16)],
        flops=T * D * 8,
        moved=2 << 20,
    )


def gate_kernel(small_ref, member_ref, chosen_ref, place_ref, *refs):
    rows, (gates_ref, slot_gate_ref, b_ref) = refs[:Z], refs[Z:]
    small = small_of(small_ref)
    for hop in range(Z):
        h2 = rows[hop][...]
        member = member_ref[hop] > 0.5
        logits = jnp.where(member, mm(h2, small), -jnp.inf)
        exponent = jnp.exp(logits - jnp.max(logits, axis=-1, keepdims=True))
        gates = exponent / jnp.sum(exponent, axis=-1, keepdims=True)
        gates_ref[hop] = gates
        high = gates.astype(BF16)
        low = (gates - high.astype(F32)).astype(BF16)
        place = place_ref[hop]
        spread = mm(place, high) + mm(place, low)
        picked = jnp.sum(spread * chosen_ref[...], axis=-1, keepdims=True)
        slot_gate_ref[:, hop] = picked.reshape(LOCAL, CAP, 1)
        b_ref[:, hop] = mm(place, h2).astype(BF16).reshape(LOCAL, CAP, D)


def gate_rows(half, w, member, chosen, place, rows):
    gates, slot_gate, b = call(
        gate_kernel,
        "gate_rows",
        [w, member, chosen, place, *rows],
        [
            SMALL_SPEC,
            pl.BlockSpec((Z, T, LANES), lambda *_: (half, 0, 0)),
            None,
            pl.BlockSpec((Z, SLOTS, T), lambda *_: (half, 0, 0)),
        ]
        + [None] * Z,
        [
            shape((Z, T, LANES), F32),
            shape((LOCAL, Z, CAP, 1), F32),
            shape((LOCAL, Z, CAP, D), BF16),
        ],
        flops=2 * Z * SLOTS * T * D,
        moved=5 << 20,
    )
    return gates, slot_gate.reshape(LOCAL, Z * CAP, 1), b.reshape(LOCAL, Z * CAP, D)


def spread_kernel(place_ref, *refs):
    rows, out_ref = refs[:PEERS], refs[PEERS]
    for hop in range(PEERS):
        out_ref[:, hop] = mm(place_ref[hop], rows[hop][...]).astype(BF16).reshape(LOCAL, CAP, D)


def spread_rows(place, line, other):
    return call(
        spread_kernel,
        "spread_rows",
        [place, *line, *other],
        [None] + [DY_SPEC] * Z + [X_SPEC] * Z,
        [shape((LOCAL, PEERS, CAP, D), BF16)],
        flops=2 * PEERS * SLOTS * T * D,
        moved=8 << 20,
    )[0].reshape(LOCAL, PEERS * CAP, D)


def expert_step(expert, b_refs, dyr_ref, gate_refs, first, down, gy_ref, db_ref):
    rows = jnp.concatenate([ref[0] for ref in b_refs], axis=0)
    gate = jnp.concatenate([ref[0] for ref in gate_refs], axis=0)
    pre = mm(rows, first())
    gate_pre, up_pre = pre[:, :H], pre[:, H:]
    sigmoid = 1.0 / (1.0 + jnp.exp(-gate_pre))
    silu = gate_pre * sigmoid
    activated = (silu * up_pre).astype(BF16)
    result = mm_nt(activated, down()).astype(BF16).astype(F32)
    raw = dyr_ref[0].astype(F32)
    gy_ref[0] = (gate * result).astype(BF16)
    inner = jnp.sum(raw * result, axis=-1, keepdims=True)
    grad_rows = (gate * raw).astype(BF16)
    grad_act = mm(grad_rows, down())
    grad_gate = (grad_act * up_pre * sigmoid * (1.0 + gate_pre * (1.0 - sigmoid))).astype(BF16)
    grad_up = (grad_act * silu).astype(BF16)
    both = jnp.concatenate([grad_gate, grad_up], axis=1)
    db_ref[0, :, 0:D] = mm_nt(both, first()).astype(BF16)
    lane = lax.broadcasted_iota(jnp.int32, (PEERS * CAP, LANES), 1)
    high = inner.astype(BF16).astype(F32)
    low = inner - high
    tail = jnp.where(lane == expert, high, jnp.where(lane == expert + E, low, 0.0))
    db_ref[0, :, D : D + LANES] = tail.astype(BF16)
    return rows, both, grad_rows, activated


def expert_kernel(
    me_ref, b0_ref, b1_ref, dyr_ref, gate0_ref, gate1_ref, w_ref, gy_ref, db_ref, grad_ref
):
    rows, both, grad_rows, activated = expert_step(
        me_ref[0] * LOCAL + pl.program_id(0),
        (b0_ref, b1_ref),
        dyr_ref,
        (gate0_ref, gate1_ref),
        lambda: w_ref[0, :, 0 : 2 * H],
        lambda: w_ref[0, :, 2 * H : 3 * H],
        gy_ref,
        db_ref,
    )
    grad_ref[0, :, 0 : 2 * H] = mm_tn(rows, both).astype(BF16)
    grad_ref[0, :, 2 * H : 3 * H] = mm_tn(grad_rows, activated).astype(BF16)


def per_expert(*dims, first=0):
    return pl.BlockSpec((1,) + dims, lambda e: (e + first, 0, 0))


def row_specs(first):
    half = PEERS * CAP // 2
    return [
        SCALARS,
        per_expert(half, D, first=first),
        per_expert(half, D, first=first),
        per_expert(2 * half, D, first=first),
        per_expert(half, 1, first=first),
        per_expert(half, 1, first=first),
    ]


def experts(me, b, dyr, slot_gate, pack):
    rows = PEERS * CAP
    return pl.pallas_call(
        expert_kernel,
        grid=(PLAIN,),
        in_specs=row_specs(0) + [per_expert(D, 3 * H)],
        out_specs=[per_expert(rows, D), per_expert(rows, D + LANES), per_expert(D, 3 * H)],
        out_shape=[
            shape((PLAIN, rows, D), BF16),
            shape((PLAIN, rows, D + LANES), BF16),
            shape((PLAIN, D, 3 * H), BF16),
        ],
        compiler_params=params(),
        cost_estimate=cost(18 * PLAIN * rows * D * H, 12 * PLAIN << 20),
        name="experts",
    )(me, *b, dyr, *slot_gate, pack)


def extra_kernel(
    me_ref,
    b0_ref,
    b1_ref,
    dyr_ref,
    gate0_ref,
    gate1_ref,
    dests_ref,
    w_ref,
    gy_ref,
    db_ref,
    keep_ref,
    give_ref,
    grads,
):
    rows, both, grad_rows, activated = expert_step(
        me_ref[0] * LOCAL + PLAIN + pl.program_id(0),
        (b0_ref, b1_ref),
        dyr_ref,
        (gate0_ref, gate1_ref),
        lambda: w_ref[0, :, 0 : 2 * H],
        lambda: w_ref[0, :, 2 * H : 3 * H],
        gy_ref,
        db_ref,
    )
    grads[:, :, 0 : 2 * H] = mm_tn(rows, both).astype(BF16).reshape(SHARDS, ROWS, 2 * H)
    grads[:, :, 2 * H : 3 * H] = mm_tn(grad_rows, activated).astype(BF16).reshape(SHARDS, ROWS, H)
    for chip in range(CHIPS):
        keep_ref[chip, 0] = grads[dests_ref[chip]]
        give_ref[chip, 0] = grads[dests_ref[CHIPS + chip]]


def extra_experts(me, b, dyr, slot_gate, dests, pack):
    rows = PEERS * CAP
    blocks = pl.BlockSpec((CHIPS, 1, ROWS, 3 * H), lambda e: (0, e, 0, 0))
    return pl.pallas_call(
        extra_kernel,
        grid=(EXTRA,),
        in_specs=row_specs(PLAIN) + [SCALARS, per_expert(D, 3 * H, first=PLAIN)],
        out_specs=[per_expert(rows, D), per_expert(rows, D + LANES), blocks, blocks],
        out_shape=[
            shape((EXTRA, rows, D), BF16),
            shape((EXTRA, rows, D + LANES), BF16),
            shape((CHIPS, EXTRA, ROWS, 3 * H), BF16),
            shape((CHIPS, EXTRA, ROWS, 3 * H), BF16),
        ],
        scratch_shapes=[pltpu.VMEM((SHARDS, ROWS, 3 * H), BF16)],
        compiler_params=params(),
        cost_estimate=cost(18 * EXTRA * rows * D * H, 14 * EXTRA << 20),
        name="extra_experts",
    )(me, *b, dyr, *slot_gate, dests, pack)


def extra_halves_kernel(keep_ref, got_ref, line_ref, cross_ref):
    total = (keep_ref[0].astype(F32) + got_ref[0].astype(F32)).astype(BF16)

    @pl.when(pl.program_id(0) < LINE)
    def _():
        cross_ref[0] = total

    @pl.when(pl.program_id(0) >= LINE)
    def _():
        line_ref[0] = total


def extra_halves(keep, got):
    block = (1, EXTRA, ROWS, 3 * H)
    return pl.pallas_call(
        extra_halves_kernel,
        grid=(CHIPS,),
        in_specs=[pl.BlockSpec(block, lambda i: ((i + LINE) % CHIPS, 0, 0, 0))] * 2,
        out_specs=[
            pl.BlockSpec(block, lambda i: (jnp.maximum(i - LINE, 0), 0, 0, 0)),
            pl.BlockSpec(block, lambda i: (jnp.minimum(i, LINE - 1), 0, 0, 0)),
        ],
        out_shape=[shape((LINE, EXTRA, ROWS, 3 * H), BF16)] * 2,
        compiler_params=params(),
        cost_estimate=cost(keep.size, 6 * keep.size),
        name="extra_halves",
    )(keep, got)


def extra_lines_kernel(line_ref, got_ref, *outs):
    for hop in range(LINE):
        outs[hop][...] = (line_ref[hop].astype(F32) + got_ref[hop].astype(F32)).astype(BF16)


def extra_lines(line, got):
    return call(
        extra_lines_kernel,
        "extra_lines",
        [line, got],
        [None, None],
        [shape((EXTRA, ROWS, 3 * H), BF16)] * LINE,
        flops=line.size,
        moved=6 * line.size,
    )


def collect_kernel(place_ref, plain_ref, extra_ref, *out_refs):
    for hop in range(PEERS):
        rows = jnp.concatenate(
            [ref[:, hop].reshape(-1, ref.shape[-1]) for ref in (plain_ref, extra_ref)], axis=0
        )
        out_refs[hop][...] = mm_tn(place_ref[hop], rows).astype(BF16)


def collect(place, values, name):
    width = values[0].shape[-1]
    return call(
        collect_kernel,
        name,
        [place, *(v.reshape(-1, PEERS, CAP, width) for v in values)],
        [None] * 3,
        [shape((T, width), BF16)] * PEERS,
        flops=2 * PEERS * SLOTS * T * width,
        moved=8 << 20,
    )


def mix(x1, returns, other):
    return call(
        add_kernel,
        "mix",
        [x1, *returns, other],
        [None] + [DY_SPEC] * Z + [None],
        [shape((T, D), BF16)],
        flops=T * D * Z,
        moved=4 << 20,
    )[0]


def norm_back(grad, normed, inverse, gain):
    scaled = grad * gain
    return inverse * (scaled - normed * jnp.mean(scaled * normed, axis=-1, keepdims=True))


def token_back_kernel(
    x1_ref, dy_ref, gates_ref, small_ref, gains_ref, *refs
):
    parts, (dx1_ref, dlogits_ref, scaled_ref, da_ref) = refs[: Z + 1], refs[Z + 1 :]
    total = parts[0][...].astype(F32)
    for ref in parts[1:]:
        total = total + ref[...].astype(F32)
    grad, tail = total[:, :D], total[:, D:]
    lane = lax.broadcasted_iota(jnp.int32, (T, LANES), 1)
    inner = jnp.where(lane < E, tail + pltpu.roll(tail, LANES - E, 1), 0.0)
    gates = gates_ref[0]
    score = gates * (inner - jnp.sum(gates * inner, axis=-1, keepdims=True))
    dlogits_ref[...] = score.astype(BF16)
    grad = grad + mm_nt(dlogits_ref[...], small_of(small_ref))
    normed, inverse = norm_of(x1_ref[...])
    scaled_ref[...] = (grad * normed).astype(BF16)
    through = dy_ref[...].astype(F32) + norm_back(grad, normed, inverse, gains_ref[1:2, :])
    dx1_ref[...] = through
    da_ref[...] = through.astype(BF16)


def token_back(x1, dy, gates, w, gains, parts):
    return call(
        token_back_kernel,
        "token_back",
        [x1, dy, gates, w, gains, *parts],
        [None, None, pl.BlockSpec((1, T, LANES), lambda *_: (0, 0, 0)), SMALL_SPEC]
        + [None] * (1 + len(parts)),
        [
            shape((T, D), F32),
            shape((T, LANES), BF16),
            shape((T, D), BF16),
            shape((T, D), BF16),
        ],
        flops=T * D * 64,
        moved=6 << 20,
    )


def shadow_kernel(qkv_ref, h2_ref, dlogits_ref, scaled_ref, small_ref, prob_ref):
    lane = lax.broadcasted_iota(jnp.int32, (T, LANES), 1)
    small = mm_tn(h2_ref[...], dlogits_ref[...])
    small_ref[...] = small + mm_tn(scaled_ref[...], (lane == E + 1).astype(BF16))
    for hop in range(Z):
        rows = slice(hop * T, (hop + 1) * T)
        for group in range(KH):
            query = stack_heads(qkv_ref, rows, group * GROUP)
            prob_ref[hop * KH + group] = probabilities(query, head(qkv_ref, rows, QH + group))


def shadow(qkv, h2, dlogits, scaled):
    return call(
        shadow_kernel,
        "shadow",
        [qkv, h2, dlogits, scaled],
        [None] * 4,
        [shape((D, LANES), F32), shape((Z * KH, GROUP * T, T), F32)],
        flops=Z * T * D * QW,
        moved=6 << 20,
    )


def head_back_kernel(
    behind_ref,
    parity_ref,
    qkv_ref,
    h1_ref,
    w_ref,
    full_ref,
    partial_ref,
    prob_ref,
    cos_ref,
    sin_ref,
    *refs,
):
    das, weights, results, outs = (refs[at * Z : at * Z + Z] for at in range(4))
    keep_ref, give_ref, dob, dqk, dqkv, h1, w, full, sems = refs[4 * Z :]
    late = [(h1_ref, h1), (w_ref, w), (full_ref, full)]
    late += [(results[hop], outs[hop].at[:, pl.ds(D, D)]) for hop in range(Z)]
    late = [pltpu.make_async_copy(a, b, sems.at[at]) for at, (a, b) in enumerate(late)]
    for copy in late:
        copy.start()
    total = jnp.zeros((Z * T, QW), F32)
    for hop in range(Z):
        columns = columns_of(behind_ref[hop])
        rows = jnp.concatenate([ref[:, columns] for ref in das], axis=0)
        total = total + mm_nt(rows, weights[hop][...])
        if hop == 0:
            own_columns = rows
    dob[...] = total.astype(BF16)
    for hop in range(Z):
        rows = slice(hop * T, (hop + 1) * T)
        for group in range(KH):
            key, value = head(qkv_ref, rows, QH + group), head(qkv_ref, rows, QH + KH + group)
            query = stack_heads(qkv_ref, rows, group * GROUP)
            out_grad = stack_heads(dob, rows, group * GROUP)
            probability = prob_ref[hop * KH + group]
            grad_prob = mm_nt(out_grad, value)
            held = jnp.sum(probability * grad_prob, axis=-1, keepdims=True)
            grad_scores = (probability * (grad_prob - held)).astype(BF16)
            grad_query = mm(grad_scores, key) * SCALE
            for index in range(GROUP):
                at = (group * GROUP + index) * HEAD_DIM
                dqk[rows, at : at + HEAD_DIM] = grad_query[index * T : (index + 1) * T]
            at = QW + group * HEAD_DIM
            dqk[rows, at : at + HEAD_DIM] = mm_tn(grad_scores, query) * SCALE
            dqkv[rows, at + KW : at + KW + HEAD_DIM] = mm_tn(
                probability.astype(BF16), out_grad
            ).astype(BF16)
    cosine = jnp.concatenate([cos_ref[...]] * Z, axis=0)
    signed = jnp.concatenate([sin_ref[...]] * Z, axis=0)
    dqkv[:, 0 : QW + KW] = rotate_back(dqk[...], cosine, signed).astype(BF16)
    even = parity_ref[0] == 0

    def store(grads, columns):
        pair = grads.astype(BF16).reshape(CHIPS, 2, ROWS, grads.shape[1])
        keep_ref[:, :, columns] = jnp.where(even, pair[:, 0], pair[:, 1])
        give_ref[:, :, columns] = jnp.where(even, pair[:, 1], pair[:, 0])

    late[2].wait()
    store(mm_tn(full[...], own_columns), slice(0, QW))
    late[0].wait()
    store(mm_tn(h1[...], dqkv[...]), slice(QW, MAIN))
    late[1].wait()
    dh1 = mm_nt(dqkv[...], w[:, :, 0:QKV].reshape(D, QKV))
    for hop in range(Z):
        outs[hop][:, 0:D] = dh1[hop * T : (hop + 1) * T].astype(BF16)
        late[3 + hop].wait()
    store(partial_ref[...], slice(MAIN, SLICE))


def head_back(behind, parity, qkv, h1, w, full, shadows, cosine, signed, das, weights, results):
    return call(
        head_back_kernel,
        "head_back",
        [behind, parity, qkv, h1, w, full, *shadows, cosine, signed, *das, *weights, *results],
        [SCALARS] * 2
        + [None, ANYWHERE, ANYWHERE, ANYWHERE]
        + [None] * (4 + 2 * Z)
        + [ANYWHERE] * Z,
        [shape((T, 2 * D), BF16)] * Z + [shape((CHIPS, ROWS, SLICE), BF16)] * 2,
        scratch=[
            pltpu.VMEM((Z * T, QW), BF16),
            pltpu.VMEM((Z * T, QW + KW), F32),
            pltpu.VMEM((Z * T, QKV), BF16),
            pltpu.VMEM((Z * T, D), BF16),
            pltpu.VMEM((SHARDS, ROWS, QKV + LANES), BF16),
            pltpu.VMEM((Z * T, D), BF16),
            pltpu.SemaphoreType.DMA((3 + Z,)),
        ],
        flops=4 * Z * T * D * QKV,
        moved=16 << 20,
    )


def token_grad_kernel(x_ref, gains_ref, dx1_ref, *refs):
    grad = refs[0][...].astype(F32)
    for hop in range(1, Z):
        grad = grad + refs[hop][...].astype(F32)
    normed, inverse = norm_of(x_ref[...].astype(F32))
    refs[Z][...] = dx1_ref[...] + norm_back(grad, normed, inverse, gains_ref[0:1, :])


def token_grad(x, gains, dx1, pieces):
    return call(
        token_grad_kernel,
        "token_grad",
        [x, gains, dx1, *pieces],
        [None] * 3 + [X_SPEC] * Z,
        [shape((T, D), F32)],
        flops=T * D * 16,
        moved=4 << 20,
    )[0]


def split_kernel(order_ref, keep_ref, got_ref, *outs):
    for chip in range(CHIPS):
        at = order_ref[chip]
        total = (keep_ref[at].astype(F32) + got_ref[at].astype(F32)).astype(BF16)
        outs[chip % 4][chip // 4] = total


def split(order, keep, got):
    return call(
        split_kernel,
        "split",
        [order, keep, got],
        [SCALARS, None, None],
        [shape((2, ROWS, SLICE), BF16)] * 4,
        flops=CHIPS * ROWS * SLICE,
        moved=6 << 20,
    )


def add_kernel(*refs):
    total = refs[0][...].astype(F32)
    for ref in refs[1:-1]:
        total = total + ref[...].astype(F32)
    refs[-1][...] = total.astype(BF16)


def sum_lines_kernel(*refs):
    for at in range(2):
        total = refs[0][at].astype(F32)
        for ref in refs[1:LINE]:
            total = total + ref[at].astype(F32)
        refs[LINE + at][...] = total.astype(BF16)


def sum_lines(parts):
    return call(
        sum_lines_kernel,
        "sum_lines",
        list(parts),
        [None] * LINE,
        [shape((ROWS, SLICE), BF16)] * 2,
        flops=LINE * ROWS * SLICE,
        moved=12 * ROWS * SLICE,
    )


def add_all(parts, name):
    return call(
        add_kernel,
        name,
        list(parts),
        [None] * len(parts),
        [shape(parts[0].shape, BF16)],
        flops=parts[0].size * len(parts),
        moved=2 * parts[0].size * (len(parts) + 1),
    )[0]


def finish_kernel(order_ref, *refs):
    parts, (wq_ref, wk_ref, wv_ref, gain_ref) = refs[:Z], refs[Z : Z + 4]
    q_ref, k_ref, v_ref, o_ref, router_ref, one_ref, two_ref, narrow = refs[Z + 4 :]
    for hop in range(Z):
        at = order_ref[hop]
        part = parts[hop][...].astype(F32)
        o_ref[:, columns_of(at)] = part[:, 0:QW]
        q_ref[:, columns_of(at)] = part[:, QW : 2 * QW]
        heads = pl.ds(pl.multiple_of(at * KW, KW), KW)
        k_ref[:, heads] = part[:, 2 * QW : 2 * QW + KW]
        v_ref[:, heads] = part[:, 2 * QW + KW : MAIN]
        narrow[at] = part[:, MAIN:]
    scaled = jnp.zeros((ROWS, 1), F32)
    for weight, grad in ((wq_ref, q_ref), (wk_ref, k_ref), (wv_ref, v_ref)):
        scaled += jnp.sum(weight[...].astype(F32) * grad[...], axis=-1, keepdims=True)
    small = narrow[0] + narrow[1] + narrow[2] + narrow[3]
    lane = lax.broadcasted_iota(jnp.int32, small.shape, 1)
    small = jnp.where(lane == E, scaled, small).T
    router_ref[...] = small[0:E]
    one_ref[...] = small[E : E + 1] / gain_ref[...].astype(F32)
    two_ref[...] = small[E + 1 : E + 2]


def finish(order, parts, w_query, key_weight, value_weight, gain):
    return call(
        finish_kernel,
        "finish",
        [order, *parts, w_query, key_weight, value_weight, gain],
        [SCALARS] + [None] * (Z + 4),
        [
            shape((ROWS, D), F32),
            shape((ROWS, KEY_VALUE_HEADS * HEAD_DIM), F32),
            shape((ROWS, KEY_VALUE_HEADS * HEAD_DIM), F32),
            shape((ROWS, D), F32),
            shape((E, ROWS), F32),
            shape((1, ROWS), F32),
            shape((1, ROWS), F32),
        ],
        scratch=[pltpu.VMEM((Z, ROWS, LANES), F32)],
        flops=ROWS * SLICE * Z,
        moved=3 << 20,
    )


def unpack_kernel(share_ref, *refs):
    parts, outs = refs[:LINE], refs[LINE:]

    def store(value):
        for at in range(3):
            outs[at][0] = value[:, at * H : (at + 1) * H]

    @pl.when(pl.program_id(0) < PLAIN)
    def _():
        store(share_ref[0].astype(F32))

    @pl.when(pl.program_id(0) >= PLAIN)
    def _():
        total = parts[0][0].astype(F32)
        for ref in parts[1:]:
            total = total + ref[0].astype(F32)
        store(total)


def unpack(share, parts):
    block = (1, ROWS, 3 * H)
    return pl.pallas_call(
        unpack_kernel,
        grid=(LOCAL,),
        in_specs=[pl.BlockSpec(block, lambda e: (jnp.minimum(e, PLAIN - 1), 0, 0))]
        + [pl.BlockSpec(block, lambda e: (jnp.maximum(e - PLAIN, 0), 0, 0))] * LINE,
        out_specs=[per_expert(ROWS, H)] * 3,
        out_shape=[shape((LOCAL, ROWS, H), F32)] * 3,
        compiler_params=params(),
        cost_estimate=cost(LOCAL * ROWS * 3 * H, 5 << 20),
        name="unpack",
    )(share, *parts)


def spread_tables(all_routes, me):
    lane = jnp.arange(LANES, dtype=jnp.int32)
    member = jnp.sum((all_routes[..., None] == lane).astype(F32), axis=2)
    mine = me * LOCAL + jnp.arange(LOCAL, dtype=jnp.int32)
    own = jnp.sum((all_routes[..., None] == mine).astype(F32), axis=2)
    earlier = (np.arange(T)[:, None] > np.arange(T)[None, :]).astype(np.float32)
    before = jnp.einsum(
        "ts,rse->rte", jnp.asarray(earlier, BF16), own.astype(BF16), preferred_element_type=F32
    )
    slots = jnp.where(own > 0.5, before.astype(jnp.int32), -1)
    slots = jnp.swapaxes(slots, 1, 2)[:, :, None, :]
    place = slots == jnp.arange(CAP, dtype=jnp.int32)[None, None, :, None]
    return member, place.astype(BF16).reshape(PEERS, SLOTS, T)


def body(
    tokens,
    cotangent,
    routes,
    norm_one,
    w_query,
    key_weight,
    value_weight,
    w_out,
    norm_two,
    w_router,
    w_gate,
    w_up,
    w_down,
):
    me = lax.axis_index("expert")
    place_in_group = lax.axis_index("fsdp")
    z = me % Z
    core = place_in_group % 2
    cosine, signed = (jnp.asarray(table) for table in rope_tables())

    first, second = pack(
        z.astype(jnp.int32)[None],
        w_out,
        w_query,
        key_weight,
        value_weight,
        w_router.T,
        norm_one[None, :],
        norm_two[None, :],
    )
    def spread_over_chips(value):
        pair = jnp.stack([value, send_chip(value, LINE)])
        own = [send_chip(pair, hop) for hop in range(LINE)]
        return own, [swap_core(value) for value in own]

    own, other = spread_over_chips(first)
    out_own, _ = spread_over_chips(after(second, own[1]))
    sources = jnp.stack([chip_at(place_in_group, hop, True) for hop in range(CHIPS)])
    order = jnp.concatenate([2 * sources + core, 2 * sources + 1 - core]).astype(jnp.int32)
    dests = jnp.stack([chip_at(place_in_group, hop) for hop in range(CHIPS)]).astype(jnp.int32)
    twins = jnp.concatenate([2 * dests + core, 2 * dests + 1 - core])
    expert_pack = lax.all_gather(
        jnp.concatenate(after([w_gate, w_up, jnp.swapaxes(w_down, 1, 2)], first), axis=2),
        "fsdp",
        axis=1,
        tiled=True,
    )

    behind = jnp.stack([(z + Z - hop) % Z for hop in range(Z)]).astype(jnp.int32)
    ahead = jnp.stack([(z + hop) % Z for hop in range(Z)]).astype(jnp.int32)

    marks = jnp.pad(routes, ((0, 0), (0, LANES - TOPK))).astype(BF16)
    early = jnp.concatenate([cotangent, marks], axis=1)
    whole_row = jnp.concatenate([tokens, early], axis=1)
    whole_row = after(whole_row, first)
    xs = [send(whole_row, hop) for hop in (0, 1, 3)]
    xs.insert(2, send(whole_row, 2))
    w, gains, h1, qkv, ob = project(order, cosine, signed, own, other, xs)
    obs = [send(ob, hop) for hop in range(Z)]
    out_other = [swap_core(after(value, ob)) for value in out_own]
    early_other = send(after(early, xs[3]), Z)
    w_out_slice, ob_full, *x1_columns = out_project(behind, order, out_own, out_other, obs)
    x1_pieces = [send(x1_columns[hop], hop, True) for hop in range(Z)]
    early_other = after(early_other, x1_pieces[1])
    early_other = [send(early_other, hop) for hop in range(Z)]
    x1, h2 = residual(ahead, tokens, gains, x1_pieces)
    h2_other = send(h2, Z)
    h2_line = [send(h2, hop) for hop in range(Z)]
    h2_other = [send(h2_other, hop) for hop in range(Z)]

    all_routes = jnp.stack(
        [r[:, 2 * D : 2 * D + TOPK].astype(jnp.int32) for r in xs]
        + [r[:, D : D + TOPK].astype(jnp.int32) for r in early_other]
    )
    member, place = spread_tables(all_routes, me)
    row_expert = me * LOCAL + jnp.arange(SLOTS, dtype=jnp.int32) // CAP
    chosen = (row_expert[:, None] == jnp.arange(LANES, dtype=jnp.int32)[None, :]).astype(F32)
    dyr = spread_rows(after(place, h2_line[1]), xs, early_other)

    gates, gate0, b0 = gate_rows(0, w, member, chosen, place, h2_line)
    _, gate1, b1 = gate_rows(1, w, member, chosen, place, h2_other)
    b, slot_gate = (b0, b1), (gate0, gate1)
    weights = after(cut_out(ahead, after(w_out_slice, x1)), b1)
    slot_gate = after(slot_gate, *weights)
    weights = [send(weights[hop], hop) for hop in range(Z)]
    number = me.astype(jnp.int32)[None]
    gy, db, grad_pack = experts(number, b, dyr, slot_gate, expert_pack)
    extra_gy, extra_db, keep_extra, give_extra = extra_experts(
        after(number, db), b, dyr, slot_gate, twins, expert_pack
    )
    db_parts = collect(place, after((db, extra_db), *weights[1:]), "collect_grads")
    grad_cross = [send(db_parts[Z + hop], hop, True) for hop in range(Z)]
    grad_line = after(db_parts[:Z], *grad_cross[1:])
    grad_line = [send(grad_line[hop], hop, True) for hop in range(Z)]
    got_extra = swap_core(give_extra)
    grad_other = send(add_all(grad_cross, "line_grads"), Z)
    expert_share = lax.psum_scatter(
        after(grad_pack, *weights[1:]), "fsdp", scatter_dimension=1, tiled=True
    )
    results = collect(place, (gy, extra_gy), "collect_results")
    grad_line = after(grad_line, results)
    dx1, dlogits, scaled, da = token_back(x1, cotangent, gates, w, gains, [*grad_line, grad_other])
    das = [send(da, hop) for hop in range(Z)]
    extra_line, extra_cross = extra_halves(keep_extra, after(got_extra, da))
    shadows = shadow(after(qkv, extra_cross), h2, dlogits, scaled)
    results = after(results, shadows[1], *das[1:])
    results_cross = [send(results[Z + hop], hop, True) for hop in range(Z)]
    *returns, keep, give = head_back(
        behind,
        core.astype(jnp.int32)[None],
        qkv,
        h1,
        w,
        ob_full,
        shadows,
        cosine,
        signed,
        das,
        weights,
        results[:Z],
    )
    parts = split(dests, keep, swap_core(after(give, *results_cross[1:])))
    extra_got = send_chip(extra_cross, LINE)
    parts = after(parts, expert_share)
    lines = [send_chip(parts[hop], hop) for hop in range(LINE)]
    results_other = send(add_all(results_cross, "line_results"), Z)
    first, third = send(returns[1], 1, True), send(returns[3], 3, True)
    lines[0] = after(lines[0], first, third)
    second = send(after(returns[2], first, third), 2, True)
    returns = [returns[0], first, second, third]
    share = sum_lines(lines)
    extra_parts = extra_lines(extra_line, after(extra_got, share[1]))
    share = add_all([share[0], send_chip(share[1], LINE)], "sum_chips")
    share = add_all([share, send(share, Z)], "sum_halves")
    extra_first, extra_third = (send_chip(extra_parts[hop], hop) for hop in (1, 3))
    share = after(share, second)
    extra_second = send_chip(extra_parts[2], 2)
    extra_parts = [extra_parts[0], extra_first, extra_second, extra_third]
    shares = [send(share, hop) for hop in range(Z)]
    grad_gate, grad_up, grad_down = unpack(expert_share, extra_parts)
    grad_tokens = token_grad(tokens, gains, dx1, returns)
    mixed_out = mix(x1, returns, results_other)
    shares = after(shares, grad_tokens, mixed_out, grad_gate)
    grad_query, grad_key, grad_value, grad_out, router, one, two = finish(
        behind, shares, w_query, key_weight, value_weight, norm_one[None, :]
    )

    return (
        mixed_out,
        grad_tokens,
        one.reshape(ROWS),
        grad_query,
        grad_key,
        grad_value,
        grad_out,
        two.reshape(ROWS),
        router.T,
        grad_gate,
        grad_up,
        jnp.swapaxes(grad_down, 1, 2),
    )


def solution(mesh):
    return jax.shard_map(
        body,
        mesh=mesh,
        in_specs=(
            P(("expert", "fsdp"), None),
            P(("expert", "fsdp"), None),
            P(("expert", "fsdp"), None),
            P("fsdp"),
            P("fsdp", None),
            P("fsdp", None),
            P("fsdp", None),
            P("fsdp", None),
            P("fsdp"),
            P("fsdp", None),
            P("expert", "fsdp", None),
            P("expert", "fsdp", None),
            P("expert", None, "fsdp"),
        ),
        out_specs=(
            P(("expert", "fsdp"), None),
            P(("expert", "fsdp"), None),
            P("fsdp"),
            P("fsdp", None),
            P("fsdp", None),
            P("fsdp", None),
            P("fsdp", None),
            P("fsdp"),
            P("fsdp", None),
            P("expert", "fsdp", None),
            P("expert", "fsdp", None),
            P("expert", None, "fsdp"),
        ),
        check_vma=False,
    )
```

```python
import jax
import jax.numpy as jnp
import numpy as np
from jax import lax
from jax.experimental import pallas as pl
from jax.experimental.pallas import tpu as pltpu
from jax.sharding import PartitionSpec as P

QUERY_HEADS = 24
KEY_VALUE_HEADS = 8
GROUP = QUERY_HEADS // KEY_VALUE_HEADS
HEAD_DIM = 64
HALF = HEAD_DIM // 2
E = 40
H = 512
D = 1536
T = 128
CAP = 32
NORM_EPSILON = 1e-05
SCALE = HEAD_DIM ** (-0.5)

Z = 4
PEERS = 8
LOCAL = E // PEERS
SLOTS = LOCAL * CAP
EXTRA = 1
PLAIN = LOCAL - EXTRA
LANES = 128
CHIPS = 8
LINE = 4
TOPK = 8
SHARDS = 2 * CHIPS
ROWS = D // SHARDS
QH = QUERY_HEADS // Z
KH = KEY_VALUE_HEADS // Z
QW = QH * HEAD_DIM
KW = KH * HEAD_DIM
QKV = QW + 2 * KW
MAIN = QW + QKV
SLICE = MAIN + LANES
VMEM_LIMIT = 60 * 1024 * 1024

F32 = jnp.float32
BF16 = jnp.bfloat16


def peer(index, hop, back=False):
    shift = hop % Z
    turned = (index % Z + (Z - shift if back else shift)) % Z
    return (index // Z + hop // Z) % 2 * Z + turned


def send(value, hop, back=False):
    if hop == 0:
        return value
    return lax.ppermute(value, "expert", [(i, peer(i, hop, back)) for i in range(PEERS)])


def chip_at(index, hop, back=False):
    shift = hop % 4
    turned = (index // 2 % 4 + (4 - shift if back else shift)) % 4
    return (index // 8 + hop // 4) % 2 * 4 + turned


def send_chip(value, hop):
    if hop == 0:
        return value
    pairs = [(i, 2 * chip_at(i, hop) + i % 2) for i in range(SHARDS)]
    return lax.ppermute(value, "fsdp", pairs)


def after(value, *others):
    return lax.optimization_barrier((value, others))[0]


def swap_core(value):
    return lax.ppermute(value, "fsdp", [(i, i ^ 1) for i in range(SHARDS)])


def mm(left, right):
    return jnp.dot(left, right, preferred_element_type=F32)


def mm_nt(left, right):
    return lax.dot_general(left, right, (((1,), (1,)), ((), ())), preferred_element_type=F32)


def mm_tn(left, right):
    return lax.dot_general(left, right, (((0,), (0,)), ((), ())), preferred_element_type=F32)


def rope_tables():
    frequency = np.exp(-np.log(10000.0) * np.arange(HALF, dtype=np.float64) * 2.0 / HEAD_DIM)
    angles = np.arange(T, dtype=np.float64)[:, None] * frequency[None, :]
    cosine = np.tile(np.cos(angles), (1, 4)).astype(np.float32)
    sine = np.sin(angles)
    signed = np.tile(np.concatenate([-sine, sine], axis=1), (1, 2)).astype(np.float32)
    return cosine, signed


def swap_halves(values):
    width = values.shape[1]
    lane = lax.broadcasted_iota(jnp.int32, values.shape, 1)
    up = pltpu.roll(values, width - HALF, 1)
    down = pltpu.roll(values, HALF, 1)
    return jnp.where(lane % HEAD_DIM < HALF, up, down)


def wide(table, width):
    return jnp.concatenate([table] * (width // LANES), axis=1)


def rotate(values, cosine, signed):
    width = values.shape[1]
    return values * wide(cosine, width) + swap_halves(values) * wide(signed, width)


def rotate_back(values, cosine, signed):
    width = values.shape[1]
    return values * wide(cosine, width) + swap_halves(values * wide(signed, width))


def gain_rows(small):
    pick = lax.broadcasted_iota(jnp.int32, (16, LANES), 1) == (
        lax.broadcasted_iota(jnp.int32, (16, LANES), 0) + E
    )
    return mm_nt(pick.astype(BF16), small)


def norm_of(values):
    inverse = lax.rsqrt(jnp.mean(values * values, axis=-1, keepdims=True) + NORM_EPSILON)
    return values * inverse, inverse


def head(ref, rows, index):
    return ref[rows, index * HEAD_DIM : (index + 1) * HEAD_DIM]


def stack_heads(ref, rows, first):
    return jnp.concatenate([head(ref, rows, first + index) for index in range(GROUP)], axis=0)


def probabilities(query, key):
    scores = mm_nt(query, key) * SCALE
    rows = lax.broadcasted_iota(jnp.int32, scores.shape, 0) % T
    cols = lax.broadcasted_iota(jnp.int32, scores.shape, 1)
    scores = jnp.where(rows >= cols, scores, -jnp.inf)
    exponent = jnp.exp(scores - jnp.max(scores, axis=-1, keepdims=True))
    return exponent / jnp.sum(exponent, axis=-1, keepdims=True)


def whole(shape):
    return pl.BlockSpec(shape, lambda *_: (0,) * len(shape))


SCALARS = pl.BlockSpec(memory_space=pltpu.SMEM)
ANYWHERE = pl.BlockSpec(memory_space=pl.ANY)


def params(**more):
    return pltpu.CompilerParams(vmem_limit_bytes=VMEM_LIMIT, **more)


WEIGHT = 60


def cost(flops, moved):
    return pl.CostEstimate(flops=flops * WEIGHT, bytes_accessed=moved * WEIGHT, transcendentals=0)


def shape(dims, kind):
    return jax.ShapeDtypeStruct(dims, kind)


def call(kernel, name, inputs, in_specs, outputs, out_specs=None, scratch=(), flops=0, moved=0):
    in_specs = [whole(v.shape) if spec is None else spec for v, spec in zip(inputs, in_specs)]
    if out_specs is None:
        out_specs = [whole(o.shape) for o in outputs]
    return pl.pallas_call(
        kernel,
        grid=(1,),
        in_specs=in_specs,
        out_specs=out_specs,
        out_shape=outputs,
        scratch_shapes=list(scratch),
        compiler_params=params(),
        cost_estimate=cost(flops, moved),
        name=name,
    )(*inputs)


SMALL_SPEC = pl.BlockSpec((SHARDS, ROWS, LANES), lambda *_: (0, 0, QKV // LANES))
X_SPEC = pl.BlockSpec((T, D), lambda *_: (0, 0))
DY_SPEC = pl.BlockSpec((T, D), lambda *_: (0, 1))


def small_of(ref):
    return ref[...].reshape(D, LANES)


def columns_of(index):
    return pl.ds(pl.multiple_of(index * QW, QW), QW)


def pack_kernel(
    z_ref, out_ref, query_ref, key_ref, value_ref, router_ref, one_ref, two_ref, first_ref, second_ref
):
    first_ref[:, 0:QW] = query_ref[...]
    first_ref[:, QW : QW + KW] = key_ref[...]
    first_ref[:, QW + KW : QKV] = value_ref[...]
    narrow = [router_ref[...], one_ref[...], two_ref[...], jnp.zeros((LANES - E - 2, ROWS), BF16)]
    first_ref[:, QKV:] = jnp.concatenate([v.astype(F32) for v in narrow], axis=0).T.astype(BF16)
    second_ref[...] = out_ref[...]


def pack(z, w_out, w_query, key_weight, value_weight, router, one, two):
    def slice_of(width):
        return pl.BlockSpec((ROWS, width), lambda i, z: (0, z[0]))

    return pl.pallas_call(
        pack_kernel,
        grid_spec=pltpu.PrefetchScalarGridSpec(
            num_scalar_prefetch=1,
            grid=(1,),
            in_specs=[
                slice_of(QW),
                slice_of(QW),
                slice_of(KW),
                slice_of(KW),
                whole((E, ROWS)),
                whole((1, ROWS)),
                whole((1, ROWS)),
            ],
            out_specs=[whole((ROWS, QKV + LANES)), whole((ROWS, QW))],
        ),
        out_shape=[shape((ROWS, QKV + LANES), BF16), shape((ROWS, QW), BF16)],
        compiler_params=params(),
        cost_estimate=cost(ROWS * SLICE, 1 << 20),
        name="pack",
    )(z, w_out, w_query, key_weight, value_weight, router, one, two)


def project_kernel(order_ref, cos_ref, sin_ref, *refs):
    own, other, xs = refs[:LINE], refs[LINE : 2 * LINE], refs[2 * LINE : 2 * LINE + Z]
    w_ref, gains_ref, h1_ref, qkv_ref, ob_ref = refs[2 * LINE + Z :]
    for chip in range(CHIPS):
        w_ref[order_ref[chip]] = own[chip % LINE][chip // LINE]
        w_ref[order_ref[CHIPS + chip]] = other[chip % LINE][chip // LINE]
    gains = gain_rows(w_ref[:, :, QKV:].reshape(D, LANES))
    gains_ref[...] = gains
    for hop in range(Z):
        normed, _ = norm_of(xs[hop][...].astype(F32))
        h1_ref[hop * T : (hop + 1) * T] = (normed * gains[0:1, :]).astype(BF16)
    pre = mm(h1_ref[...], w_ref[:, :, 0:QKV].reshape(D, QKV))
    cosine = jnp.concatenate([cos_ref[...]] * Z, axis=0)
    signed = jnp.concatenate([sin_ref[...]] * Z, axis=0)
    qkv_ref[:, 0:QW] = rotate(pre[:, 0:QW], cosine, signed).astype(BF16)
    qkv_ref[:, QW : QW + KW] = rotate(pre[:, QW : QW + KW], cosine, signed).astype(BF16)
    qkv_ref[:, QW + KW :] = pre[:, QW + KW :].astype(BF16)
    for hop in range(Z):
        rows = slice(hop * T, (hop + 1) * T)
        for group in range(KH):
            key, value = head(qkv_ref, rows, QH + group), head(qkv_ref, rows, QH + KH + group)
            query = stack_heads(qkv_ref, rows, group * GROUP)
            result = mm(probabilities(query, key).astype(BF16), value).astype(BF16)
            for index in range(GROUP):
                at = (group * GROUP + index) * HEAD_DIM
                ob_ref[rows, at : at + HEAD_DIM] = result[index * T : (index + 1) * T]


def project(order, cosine, signed, own, other, xs):
    return call(
        project_kernel,
        "project",
        [order, cosine, signed, *own, *other, *xs],
        [SCALARS] + [None] * (2 + 2 * LINE) + [X_SPEC] * Z,
        [
            shape((SHARDS, ROWS, QKV + LANES), BF16),
            shape((16, D), F32),
            shape((Z * T, D), BF16),
            shape((Z * T, QKV), BF16),
            shape((Z * T, QW), BF16),
        ],
        flops=2 * Z * T * D * QKV,
        moved=12 << 20,
    )


def out_project_kernel(peers_ref, order_ref, *refs):
    own, other, obs = refs[:LINE], refs[LINE : 2 * LINE], refs[2 * LINE : 2 * LINE + Z]
    w_ref, full_ref, *outs = refs[2 * LINE + Z :]
    for chip in range(CHIPS):
        w_ref[order_ref[chip]] = own[chip % LINE][chip // LINE]
        w_ref[order_ref[CHIPS + chip]] = other[chip % LINE][chip // LINE]
    total = jnp.zeros((Z * T, QW), F32)
    for hop in range(Z):
        peer_index = peers_ref[hop]
        blocks = [(row - hop) % Z for row in range(Z)]
        rows = jnp.concatenate([obs[hop][b * T : (b + 1) * T, :] for b in blocks], axis=0)
        full_ref[:, columns_of(peer_index)] = rows
        weight = w_ref[pl.ds(peer_index * Z, Z)].reshape(QW, QW)
        total = total + mm(rows, weight)
    for hop in range(Z):
        outs[hop][...] = total[hop * T : (hop + 1) * T].astype(BF16)


def out_project(peers, order, own, other, obs):
    return call(
        out_project_kernel,
        "out_project",
        [peers, order, *own, *other, *obs],
        [SCALARS] * 2 + [None] * (2 * LINE + Z),
        [shape((SHARDS, ROWS, QW), BF16), shape((Z * T, D), BF16)] + [shape((T, QW), BF16)] * Z,
        flops=2 * Z * T * D * QW,
        moved=6 << 20,
    )


def cut_out_kernel(peers_ref, w_ref, *outs):
    for hop in range(Z):
        outs[hop][...] = w_ref[pl.ds(peers_ref[hop] * Z, Z)].reshape(QW, QW)


def cut_out(peers, w):
    return call(
        cut_out_kernel,
        "cut_out",
        [peers, w],
        [SCALARS, None],
        [shape((QW, QW), BF16)] * Z,
        flops=D * QW,
        moved=2 << 20,
    )


def residual_kernel(peers_ref, x_ref, gains_ref, *refs):
    pieces, (x1_ref, h2_ref) = refs[:Z], refs[Z:]
    x1_ref[...] = x_ref[...].astype(F32)
    for hop in range(Z):
        x1_ref[:, columns_of(peers_ref[hop])] += pieces[hop][...].astype(F32)
    normed, _ = norm_of(x1_ref[...])
    h2_ref[...] = (normed * gains_ref[1:2, :]).astype(BF16)


def residual(peers, x, gains, pieces):
    return call(
        residual_kernel,
        "residual",
        [peers, x, gains, *pieces],
        [SCALARS] + [None] * (2 + Z),
        [shape((T, D), F32), shape((T, D), BF16)],
        flops=T * D * 8,
        moved=2 << 20,
    )


def gate_kernel(small_ref, member_ref, chosen_ref, place_ref, *refs):
    rows, (gates_ref, slot_gate_ref, b_ref) = refs[:Z], refs[Z:]
    small = small_of(small_ref)
    for hop in range(Z):
        h2 = rows[hop][...]
        member = member_ref[hop] > 0.5
        logits = jnp.where(member, mm(h2, small), -jnp.inf)
        exponent = jnp.exp(logits - jnp.max(logits, axis=-1, keepdims=True))
        gates = exponent / jnp.sum(exponent, axis=-1, keepdims=True)
        gates_ref[hop] = gates
        high = gates.astype(BF16)
        low = (gates - high.astype(F32)).astype(BF16)
        place = place_ref[hop]
        spread = mm(place, high) + mm(place, low)
        picked = jnp.sum(spread * chosen_ref[...], axis=-1, keepdims=True)
        slot_gate_ref[:, hop] = picked.reshape(LOCAL, CAP, 1)
        b_ref[:, hop] = mm(place, h2).astype(BF16).reshape(LOCAL, CAP, D)


def gate_rows(half, w, member, chosen, place, rows):
    gates, slot_gate, b = call(
        gate_kernel,
        "gate_rows",
        [w, member, chosen, place, *rows],
        [
            SMALL_SPEC,
            pl.BlockSpec((Z, T, LANES), lambda *_: (half, 0, 0)),
            None,
            pl.BlockSpec((Z, SLOTS, T), lambda *_: (half, 0, 0)),
        ]
        + [None] * Z,
        [
            shape((Z, T, LANES), F32),
            shape((LOCAL, Z, CAP, 1), F32),
            shape((LOCAL, Z, CAP, D), BF16),
        ],
        flops=2 * Z * SLOTS * T * D,
        moved=5 << 20,
    )
    return gates, slot_gate.reshape(LOCAL, Z * CAP, 1), b.reshape(LOCAL, Z * CAP, D)


def spread_kernel(place_ref, *refs):
    rows, out_ref = refs[:PEERS], refs[PEERS]
    for hop in range(PEERS):
        out_ref[:, hop] = mm(place_ref[hop], rows[hop][...]).astype(BF16).reshape(LOCAL, CAP, D)


def spread_rows(place, line, other):
    return call(
        spread_kernel,
        "spread_rows",
        [place, *line, *other],
        [None] + [DY_SPEC] * Z + [X_SPEC] * Z,
        [shape((LOCAL, PEERS, CAP, D), BF16)],
        flops=2 * PEERS * SLOTS * T * D,
        moved=8 << 20,
    )[0].reshape(LOCAL, PEERS * CAP, D)


def expert_step(expert, b_refs, dyr_ref, gate_refs, first, down, gy_ref, db_ref):
    rows = jnp.concatenate([ref[0] for ref in b_refs], axis=0)
    gate = jnp.concatenate([ref[0] for ref in gate_refs], axis=0)
    pre = mm(rows, first())
    gate_pre, up_pre = pre[:, :H], pre[:, H:]
    sigmoid = 1.0 / (1.0 + jnp.exp(-gate_pre))
    silu = gate_pre * sigmoid
    activated = (silu * up_pre).astype(BF16)
    result = mm_nt(activated, down()).astype(BF16).astype(F32)
    raw = dyr_ref[0].astype(F32)
    gy_ref[0] = (gate * result).astype(BF16)
    inner = jnp.sum(raw * result, axis=-1, keepdims=True)
    grad_rows = (gate * raw).astype(BF16)
    grad_act = mm(grad_rows, down())
    grad_gate = (grad_act * up_pre * sigmoid * (1.0 + gate_pre * (1.0 - sigmoid))).astype(BF16)
    grad_up = (grad_act * silu).astype(BF16)
    both = jnp.concatenate([grad_gate, grad_up], axis=1)
    db_ref[0, :, 0:D] = mm_nt(both, first()).astype(BF16)
    lane = lax.broadcasted_iota(jnp.int32, (PEERS * CAP, LANES), 1)
    high = inner.astype(BF16).astype(F32)
    low = inner - high
    tail = jnp.where(lane == expert, high, jnp.where(lane == expert + E, low, 0.0))
    db_ref[0, :, D : D + LANES] = tail.astype(BF16)
    return rows, both, grad_rows, activated


def expert_kernel(
    me_ref, b0_ref, b1_ref, dyr_ref, gate0_ref, gate1_ref, w_ref, gy_ref, db_ref, grad_ref
):
    rows, both, grad_rows, activated = expert_step(
        me_ref[0] * LOCAL + pl.program_id(0),
        (b0_ref, b1_ref),
        dyr_ref,
        (gate0_ref, gate1_ref),
        lambda: w_ref[0, :, 0 : 2 * H],
        lambda: w_ref[0, :, 2 * H : 3 * H],
        gy_ref,
        db_ref,
    )
    grad_ref[0, :, 0 : 2 * H] = mm_tn(rows, both).astype(BF16)
    grad_ref[0, :, 2 * H : 3 * H] = mm_tn(grad_rows, activated).astype(BF16)


def per_expert(*dims, first=0):
    return pl.BlockSpec((1,) + dims, lambda e: (e + first, 0, 0))


def row_specs(first):
    half = PEERS * CAP // 2
    return [
        SCALARS,
        per_expert(half, D, first=first),
        per_expert(half, D, first=first),
        per_expert(2 * half, D, first=first),
        per_expert(half, 1, first=first),
        per_expert(half, 1, first=first),
    ]


def experts(me, b, dyr, slot_gate, pack):
    rows = PEERS * CAP
    return pl.pallas_call(
        expert_kernel,
        grid=(PLAIN,),
        in_specs=row_specs(0) + [per_expert(D, 3 * H)],
        out_specs=[per_expert(rows, D), per_expert(rows, D + LANES), per_expert(D, 3 * H)],
        out_shape=[
            shape((PLAIN, rows, D), BF16),
            shape((PLAIN, rows, D + LANES), BF16),
            shape((PLAIN, D, 3 * H), BF16),
        ],
        compiler_params=params(),
        cost_estimate=cost(18 * PLAIN * rows * D * H, 12 * PLAIN << 20),
        name="experts",
    )(me, *b, dyr, *slot_gate, pack)


def extra_kernel(
    me_ref,
    b0_ref,
    b1_ref,
    dyr_ref,
    gate0_ref,
    gate1_ref,
    dests_ref,
    w_ref,
    gy_ref,
    db_ref,
    keep_ref,
    give_ref,
    grads,
):
    rows, both, grad_rows, activated = expert_step(
        me_ref[0] * LOCAL + PLAIN + pl.program_id(0),
        (b0_ref, b1_ref),
        dyr_ref,
        (gate0_ref, gate1_ref),
        lambda: w_ref[0, :, 0 : 2 * H],
        lambda: w_ref[0, :, 2 * H : 3 * H],
        gy_ref,
        db_ref,
    )
    grads[:, :, 0 : 2 * H] = mm_tn(rows, both).astype(BF16).reshape(SHARDS, ROWS, 2 * H)
    grads[:, :, 2 * H : 3 * H] = mm_tn(grad_rows, activated).astype(BF16).reshape(SHARDS, ROWS, H)
    for chip in range(CHIPS):
        keep_ref[chip, 0] = grads[dests_ref[chip]]
        give_ref[chip, 0] = grads[dests_ref[CHIPS + chip]]


def extra_experts(me, b, dyr, slot_gate, dests, pack):
    rows = PEERS * CAP
    blocks = pl.BlockSpec((CHIPS, 1, ROWS, 3 * H), lambda e: (0, e, 0, 0))
    return pl.pallas_call(
        extra_kernel,
        grid=(EXTRA,),
        in_specs=row_specs(PLAIN) + [SCALARS, per_expert(D, 3 * H, first=PLAIN)],
        out_specs=[per_expert(rows, D), per_expert(rows, D + LANES), blocks, blocks],
        out_shape=[
            shape((EXTRA, rows, D), BF16),
            shape((EXTRA, rows, D + LANES), BF16),
            shape((CHIPS, EXTRA, ROWS, 3 * H), BF16),
            shape((CHIPS, EXTRA, ROWS, 3 * H), BF16),
        ],
        scratch_shapes=[pltpu.VMEM((SHARDS, ROWS, 3 * H), BF16)],
        compiler_params=params(),
        cost_estimate=cost(18 * EXTRA * rows * D * H, 14 * EXTRA << 20),
        name="extra_experts",
    )(me, *b, dyr, *slot_gate, dests, pack)


def extra_halves_kernel(keep_ref, got_ref, line_ref, cross_ref):
    total = (keep_ref[0].astype(F32) + got_ref[0].astype(F32)).astype(BF16)

    @pl.when(pl.program_id(0) < LINE)
    def _():
        cross_ref[0] = total

    @pl.when(pl.program_id(0) >= LINE)
    def _():
        line_ref[0] = total


def extra_halves(keep, got):
    block = (1, EXTRA, ROWS, 3 * H)
    return pl.pallas_call(
        extra_halves_kernel,
        grid=(CHIPS,),
        in_specs=[pl.BlockSpec(block, lambda i: ((i + LINE) % CHIPS, 0, 0, 0))] * 2,
        out_specs=[
            pl.BlockSpec(block, lambda i: (jnp.maximum(i - LINE, 0), 0, 0, 0)),
            pl.BlockSpec(block, lambda i: (jnp.minimum(i, LINE - 1), 0, 0, 0)),
        ],
        out_shape=[shape((LINE, EXTRA, ROWS, 3 * H), BF16)] * 2,
        compiler_params=params(),
        cost_estimate=cost(keep.size, 6 * keep.size),
        name="extra_halves",
    )(keep, got)


def extra_lines_kernel(line_ref, got_ref, *outs):
    for hop in range(LINE):
        outs[hop][...] = (line_ref[hop].astype(F32) + got_ref[hop].astype(F32)).astype(BF16)


def extra_lines(line, got):
    return call(
        extra_lines_kernel,
        "extra_lines",
        [line, got],
        [None, None],
        [shape((EXTRA, ROWS, 3 * H), BF16)] * LINE,
        flops=line.size,
        moved=6 * line.size,
    )


def collect_kernel(place_ref, plain_ref, extra_ref, *out_refs):
    for hop in range(PEERS):
        rows = jnp.concatenate(
            [ref[:, hop].reshape(-1, ref.shape[-1]) for ref in (plain_ref, extra_ref)], axis=0
        )
        out_refs[hop][...] = mm_tn(place_ref[hop], rows).astype(BF16)


def collect(place, values, name):
    width = values[0].shape[-1]
    return call(
        collect_kernel,
        name,
        [place, *(v.reshape(-1, PEERS, CAP, width) for v in values)],
        [None] * 3,
        [shape((T, width), BF16)] * PEERS,
        flops=2 * PEERS * SLOTS * T * width,
        moved=8 << 20,
    )


def mix(x1, returns, other):
    return call(
        add_kernel,
        "mix",
        [x1, *returns, other],
        [None] + [DY_SPEC] * Z + [None],
        [shape((T, D), BF16)],
        flops=T * D * Z,
        moved=4 << 20,
    )[0]


def norm_back(grad, normed, inverse, gain):
    scaled = grad * gain
    return inverse * (scaled - normed * jnp.mean(scaled * normed, axis=-1, keepdims=True))


def token_back_kernel(
    x1_ref, dy_ref, gates_ref, small_ref, gains_ref, *refs
):
    parts, (dx1_ref, dlogits_ref, scaled_ref, da_ref) = refs[: Z + 1], refs[Z + 1 :]
    total = parts[0][...].astype(F32)
    for ref in parts[1:]:
        total = total + ref[...].astype(F32)
    grad, tail = total[:, :D], total[:, D:]
    lane = lax.broadcasted_iota(jnp.int32, (T, LANES), 1)
    inner = jnp.where(lane < E, tail + pltpu.roll(tail, LANES - E, 1), 0.0)
    gates = gates_ref[0]
    score = gates * (inner - jnp.sum(gates * inner, axis=-1, keepdims=True))
    dlogits_ref[...] = score.astype(BF16)
    grad = grad + mm_nt(dlogits_ref[...], small_of(small_ref))
    normed, inverse = norm_of(x1_ref[...])
    scaled_ref[...] = (grad * normed).astype(BF16)
    through = dy_ref[...].astype(F32) + norm_back(grad, normed, inverse, gains_ref[1:2, :])
    dx1_ref[...] = through
    da_ref[...] = through.astype(BF16)


def token_back(x1, dy, gates, w, gains, parts):
    return call(
        token_back_kernel,
        "token_back",
        [x1, dy, gates, w, gains, *parts],
        [None, None, pl.BlockSpec((1, T, LANES), lambda *_: (0, 0, 0)), SMALL_SPEC]
        + [None] * (1 + len(parts)),
        [
            shape((T, D), F32),
            shape((T, LANES), BF16),
            shape((T, D), BF16),
            shape((T, D), BF16),
        ],
        flops=T * D * 64,
        moved=6 << 20,
    )


def shadow_kernel(qkv_ref, h2_ref, dlogits_ref, scaled_ref, small_ref, prob_ref):
    lane = lax.broadcasted_iota(jnp.int32, (T, LANES), 1)
    small = mm_tn(h2_ref[...], dlogits_ref[...])
    small_ref[...] = small + mm_tn(scaled_ref[...], (lane == E + 1).astype(BF16))
    for hop in range(Z):
        rows = slice(hop * T, (hop + 1) * T)
        for group in range(KH):
            query = stack_heads(qkv_ref, rows, group * GROUP)
            prob_ref[hop * KH + group] = probabilities(query, head(qkv_ref, rows, QH + group))


def shadow(qkv, h2, dlogits, scaled):
    return call(
        shadow_kernel,
        "shadow",
        [qkv, h2, dlogits, scaled],
        [None] * 4,
        [shape((D, LANES), F32), shape((Z * KH, GROUP * T, T), F32)],
        flops=Z * T * D * QW,
        moved=6 << 20,
    )


def head_back_kernel(
    behind_ref,
    parity_ref,
    qkv_ref,
    h1_ref,
    w_ref,
    full_ref,
    partial_ref,
    prob_ref,
    cos_ref,
    sin_ref,
    *refs,
):
    das, weights, results, outs = (refs[at * Z : at * Z + Z] for at in range(4))
    keep_ref, give_ref, dob, dqk, dqkv, h1, w, full, sems = refs[4 * Z :]
    late = [(h1_ref, h1), (w_ref, w), (full_ref, full)]
    late += [(results[hop], outs[hop].at[:, pl.ds(D, D)]) for hop in range(Z)]
    late = [pltpu.make_async_copy(a, b, sems.at[at]) for at, (a, b) in enumerate(late)]
    for copy in late:
        copy.start()
    total = jnp.zeros((Z * T, QW), F32)
    for hop in range(Z):
        columns = columns_of(behind_ref[hop])
        rows = jnp.concatenate([ref[:, columns] for ref in das], axis=0)
        total = total + mm_nt(rows, weights[hop][...])
        if hop == 0:
            own_columns = rows
    dob[...] = total.astype(BF16)
    for hop in range(Z):
        rows = slice(hop * T, (hop + 1) * T)
        for group in range(KH):
            key, value = head(qkv_ref, rows, QH + group), head(qkv_ref, rows, QH + KH + group)
            query = stack_heads(qkv_ref, rows, group * GROUP)
            out_grad = stack_heads(dob, rows, group * GROUP)
            probability = prob_ref[hop * KH + group]
            grad_prob = mm_nt(out_grad, value)
            held = jnp.sum(probability * grad_prob, axis=-1, keepdims=True)
            grad_scores = (probability * (grad_prob - held)).astype(BF16)
            grad_query = mm(grad_scores, key) * SCALE
            for index in range(GROUP):
                at = (group * GROUP + index) * HEAD_DIM
                dqk[rows, at : at + HEAD_DIM] = grad_query[index * T : (index + 1) * T]
            at = QW + group * HEAD_DIM
            dqk[rows, at : at + HEAD_DIM] = mm_tn(grad_scores, query) * SCALE
            dqkv[rows, at + KW : at + KW + HEAD_DIM] = mm_tn(
                probability.astype(BF16), out_grad
            ).astype(BF16)
    cosine = jnp.concatenate([cos_ref[...]] * Z, axis=0)
    signed = jnp.concatenate([sin_ref[...]] * Z, axis=0)
    dqkv[:, 0 : QW + KW] = rotate_back(dqk[...], cosine, signed).astype(BF16)
    even = parity_ref[0] == 0

    def store(grads, columns):
        pair = grads.astype(BF16).reshape(CHIPS, 2, ROWS, grads.shape[1])
        keep_ref[:, :, columns] = jnp.where(even, pair[:, 0], pair[:, 1])
        give_ref[:, :, columns] = jnp.where(even, pair[:, 1], pair[:, 0])

    late[2].wait()
    store(mm_tn(full[...], own_columns), slice(0, QW))
    late[0].wait()
    store(mm_tn(h1[...], dqkv[...]), slice(QW, MAIN))
    late[1].wait()
    dh1 = mm_nt(dqkv[...], w[:, :, 0:QKV].reshape(D, QKV))
    for hop in range(Z):
        outs[hop][:, 0:D] = dh1[hop * T : (hop + 1) * T].astype(BF16)
        late[3 + hop].wait()
    store(partial_ref[...], slice(MAIN, SLICE))


def head_back(behind, parity, qkv, h1, w, full, shadows, cosine, signed, das, weights, results):
    return call(
        head_back_kernel,
        "head_back",
        [behind, parity, qkv, h1, w, full, *shadows, cosine, signed, *das, *weights, *results],
        [SCALARS] * 2
        + [None, ANYWHERE, ANYWHERE, ANYWHERE]
        + [None] * (4 + 2 * Z)
        + [ANYWHERE] * Z,
        [shape((T, 2 * D), BF16)] * Z + [shape((CHIPS, ROWS, SLICE), BF16)] * 2,
        scratch=[
            pltpu.VMEM((Z * T, QW), BF16),
            pltpu.VMEM((Z * T, QW + KW), F32),
            pltpu.VMEM((Z * T, QKV), BF16),
            pltpu.VMEM((Z * T, D), BF16),
            pltpu.VMEM((SHARDS, ROWS, QKV + LANES), BF16),
            pltpu.VMEM((Z * T, D), BF16),
            pltpu.SemaphoreType.DMA((3 + Z,)),
        ],
        flops=4 * Z * T * D * QKV,
        moved=16 << 20,
    )


def token_grad_kernel(x_ref, gains_ref, dx1_ref, *refs):
    grad = refs[0][...].astype(F32)
    for hop in range(1, Z):
        grad = grad + refs[hop][...].astype(F32)
    normed, inverse = norm_of(x_ref[...].astype(F32))
    refs[Z][...] = dx1_ref[...] + norm_back(grad, normed, inverse, gains_ref[0:1, :])


def token_grad(x, gains, dx1, pieces):
    return call(
        token_grad_kernel,
        "token_grad",
        [x, gains, dx1, *pieces],
        [None] * 3 + [X_SPEC] * Z,
        [shape((T, D), F32)],
        flops=T * D * 16,
        moved=4 << 20,
    )[0]


def split_kernel(order_ref, keep_ref, got_ref, *outs):
    for chip in range(CHIPS):
        at = order_ref[chip]
        total = (keep_ref[at].astype(F32) + got_ref[at].astype(F32)).astype(BF16)
        outs[chip % 4][chip // 4] = total


def split(order, keep, got):
    return call(
        split_kernel,
        "split",
        [order, keep, got],
        [SCALARS, None, None],
        [shape((2, ROWS, SLICE), BF16)] * 4,
        flops=CHIPS * ROWS * SLICE,
        moved=6 << 20,
    )


def add_kernel(*refs):
    total = refs[0][...].astype(F32)
    for ref in refs[1:-1]:
        total = total + ref[...].astype(F32)
    refs[-1][...] = total.astype(BF16)


def sum_lines_kernel(*refs):
    for at in range(2):
        total = refs[0][at].astype(F32)
        for ref in refs[1:LINE]:
            total = total + ref[at].astype(F32)
        refs[LINE + at][...] = total.astype(BF16)


def sum_lines(parts):
    return call(
        sum_lines_kernel,
        "sum_lines",
        list(parts),
        [None] * LINE,
        [shape((ROWS, SLICE), BF16)] * 2,
        flops=LINE * ROWS * SLICE,
        moved=12 * ROWS * SLICE,
    )


def add_all(parts, name):
    return call(
        add_kernel,
        name,
        list(parts),
        [None] * len(parts),
        [shape(parts[0].shape, BF16)],
        flops=parts[0].size * len(parts),
        moved=2 * parts[0].size * (len(parts) + 1),
    )[0]


def finish_kernel(order_ref, *refs):
    parts, (wq_ref, wk_ref, wv_ref, gain_ref) = refs[:Z], refs[Z : Z + 4]
    q_ref, k_ref, v_ref, o_ref, router_ref, one_ref, two_ref, narrow = refs[Z + 4 :]
    for hop in range(Z):
        at = order_ref[hop]
        part = parts[hop][...].astype(F32)
        o_ref[:, columns_of(at)] = part[:, 0:QW]
        q_ref[:, columns_of(at)] = part[:, QW : 2 * QW]
        heads = pl.ds(pl.multiple_of(at * KW, KW), KW)
        k_ref[:, heads] = part[:, 2 * QW : 2 * QW + KW]
        v_ref[:, heads] = part[:, 2 * QW + KW : MAIN]
        narrow[at] = part[:, MAIN:]
    scaled = jnp.zeros((ROWS, 1), F32)
    for weight, grad in ((wq_ref, q_ref), (wk_ref, k_ref), (wv_ref, v_ref)):
        scaled += jnp.sum(weight[...].astype(F32) * grad[...], axis=-1, keepdims=True)
    small = narrow[0] + narrow[1] + narrow[2] + narrow[3]
    lane = lax.broadcasted_iota(jnp.int32, small.shape, 1)
    small = jnp.where(lane == E, scaled, small).T
    router_ref[...] = small[0:E]
    one_ref[...] = small[E : E + 1] / gain_ref[...].astype(F32)
    two_ref[...] = small[E + 1 : E + 2]


def finish(order, parts, w_query, key_weight, value_weight, gain):
    return call(
        finish_kernel,
        "finish",
        [order, *parts, w_query, key_weight, value_weight, gain],
        [SCALARS] + [None] * (Z + 4),
        [
            shape((ROWS, D), F32),
            shape((ROWS, KEY_VALUE_HEADS * HEAD_DIM), F32),
            shape((ROWS, KEY_VALUE_HEADS * HEAD_DIM), F32),
            shape((ROWS, D), F32),
            shape((E, ROWS), F32),
            shape((1, ROWS), F32),
            shape((1, ROWS), F32),
        ],
        scratch=[pltpu.VMEM((Z, ROWS, LANES), F32)],
        flops=ROWS * SLICE * Z,
        moved=3 << 20,
    )


def unpack_kernel(share_ref, *refs):
    parts, outs = refs[:LINE], refs[LINE:]

    def store(value):
        for at in range(3):
            outs[at][0] = value[:, at * H : (at + 1) * H]

    @pl.when(pl.program_id(0) < PLAIN)
    def _():
        store(share_ref[0].astype(F32))

    @pl.when(pl.program_id(0) >= PLAIN)
    def _():
        total = parts[0][0].astype(F32)
        for ref in parts[1:]:
            total = total + ref[0].astype(F32)
        store(total)


def unpack(share, parts):
    block = (1, ROWS, 3 * H)
    return pl.pallas_call(
        unpack_kernel,
        grid=(LOCAL,),
        in_specs=[pl.BlockSpec(block, lambda e: (jnp.minimum(e, PLAIN - 1), 0, 0))]
        + [pl.BlockSpec(block, lambda e: (jnp.maximum(e - PLAIN, 0), 0, 0))] * LINE,
        out_specs=[per_expert(ROWS, H)] * 3,
        out_shape=[shape((LOCAL, ROWS, H), F32)] * 3,
        compiler_params=params(),
        cost_estimate=cost(LOCAL * ROWS * 3 * H, 5 << 20),
        name="unpack",
    )(share, *parts)


def spread_tables(all_routes, me):
    lane = jnp.arange(LANES, dtype=jnp.int32)
    member = jnp.sum((all_routes[..., None] == lane).astype(F32), axis=2)
    mine = me * LOCAL + jnp.arange(LOCAL, dtype=jnp.int32)
    own = jnp.sum((all_routes[..., None] == mine).astype(F32), axis=2)
    earlier = (np.arange(T)[:, None] > np.arange(T)[None, :]).astype(np.float32)
    before = jnp.einsum(
        "ts,rse->rte", jnp.asarray(earlier, BF16), own.astype(BF16), preferred_element_type=F32
    )
    slots = jnp.where(own > 0.5, before.astype(jnp.int32), -1)
    slots = jnp.swapaxes(slots, 1, 2)[:, :, None, :]
    place = slots == jnp.arange(CAP, dtype=jnp.int32)[None, None, :, None]
    return member, place.astype(BF16).reshape(PEERS, SLOTS, T)


def body(
    tokens,
    cotangent,
    routes,
    norm_one,
    w_query,
    key_weight,
    value_weight,
    w_out,
    norm_two,
    w_router,
    w_gate,
    w_up,
    w_down,
):
    me = lax.axis_index("expert")
    place_in_group = lax.axis_index("fsdp")
    z = me % Z
    core = place_in_group % 2
    cosine, signed = (jnp.asarray(table) for table in rope_tables())

    first, second = pack(
        z.astype(jnp.int32)[None],
        w_out,
        w_query,
        key_weight,
        value_weight,
        w_router.T,
        norm_one[None, :],
        norm_two[None, :],
    )
    def spread_over_chips(value):
        pair = jnp.stack([value, send_chip(value, LINE)])
        own = [send_chip(pair, hop) for hop in range(LINE)]
        return own, [swap_core(value) for value in own]

    own, other = spread_over_chips(first)
    out_own, _ = spread_over_chips(after(second, own[1]))
    sources = jnp.stack([chip_at(place_in_group, hop, True) for hop in range(CHIPS)])
    order = jnp.concatenate([2 * sources + core, 2 * sources + 1 - core]).astype(jnp.int32)
    dests = jnp.stack([chip_at(place_in_group, hop) for hop in range(CHIPS)]).astype(jnp.int32)
    twins = jnp.concatenate([2 * dests + core, 2 * dests + 1 - core])
    expert_pack = lax.all_gather(
        jnp.concatenate(after([w_gate, w_up, jnp.swapaxes(w_down, 1, 2)], first), axis=2),
        "fsdp",
        axis=1,
        tiled=True,
    )

    behind = jnp.stack([(z + Z - hop) % Z for hop in range(Z)]).astype(jnp.int32)
    ahead = jnp.stack([(z + hop) % Z for hop in range(Z)]).astype(jnp.int32)

    marks = jnp.pad(routes, ((0, 0), (0, LANES - TOPK))).astype(BF16)
    early = jnp.concatenate([cotangent, marks], axis=1)
    whole_row = jnp.concatenate([tokens, early], axis=1)
    whole_row = after(whole_row, first)
    xs = [send(whole_row, hop) for hop in (0, 1, 3)]
    xs.insert(2, send(whole_row, 2))
    w, gains, h1, qkv, ob = project(order, cosine, signed, own, other, xs)
    obs = [send(ob, hop) for hop in range(Z)]
    out_other = [swap_core(after(value, ob)) for value in out_own]
    early_other = send(after(early, xs[3]), Z)
    w_out_slice, ob_full, *x1_columns = out_project(behind, order, out_own, out_other, obs)
    x1_pieces = [send(x1_columns[hop], hop, True) for hop in range(Z)]
    early_other = after(early_other, x1_pieces[1])
    early_other = [send(early_other, hop) for hop in range(Z)]
    x1, h2 = residual(ahead, tokens, gains, x1_pieces)
    h2_other = send(h2, Z)
    h2_line = [send(h2, hop) for hop in range(Z)]
    h2_other = [send(h2_other, hop) for hop in range(Z)]

    all_routes = jnp.stack(
        [r[:, 2 * D : 2 * D + TOPK].astype(jnp.int32) for r in xs]
        + [r[:, D : D + TOPK].astype(jnp.int32) for r in early_other]
    )
    member, place = spread_tables(all_routes, me)
    row_expert = me * LOCAL + jnp.arange(SLOTS, dtype=jnp.int32) // CAP
    chosen = (row_expert[:, None] == jnp.arange(LANES, dtype=jnp.int32)[None, :]).astype(F32)
    dyr = spread_rows(after(place, h2_line[1]), xs, early_other)

    gates, gate0, b0 = gate_rows(0, w, member, chosen, place, h2_line)
    _, gate1, b1 = gate_rows(1, w, member, chosen, place, h2_other)
    b, slot_gate = (b0, b1), (gate0, gate1)
    weights = after(cut_out(ahead, after(w_out_slice, x1)), b1)
    slot_gate = after(slot_gate, *weights)
    weights = [send(weights[hop], hop) for hop in range(Z)]
    number = me.astype(jnp.int32)[None]
    gy, db, grad_pack = experts(number, b, dyr, slot_gate, expert_pack)
    extra_gy, extra_db, keep_extra, give_extra = extra_experts(
        after(number, db), b, dyr, slot_gate, twins, expert_pack
    )
    db_parts = collect(place, after((db, extra_db), *weights[1:]), "collect_grads")
    grad_cross = [send(db_parts[Z + hop], hop, True) for hop in range(Z)]
    grad_line = after(db_parts[:Z], grad_cross[1], grad_cross[3])
    grad_line = [send(grad_line[hop], hop, True) for hop in range(Z)]
    got_extra = swap_core(give_extra)
    grad_other = send(add_all(after(grad_cross, grad_line[1]), "line_grads"), Z)
    expert_share = lax.psum_scatter(
        after(grad_pack, *weights[1:]), "fsdp", scatter_dimension=1, tiled=True
    )
    results = collect(place, (gy, extra_gy), "collect_results")
    grad_line = after(grad_line, results)
    dx1, dlogits, scaled, da = token_back(x1, cotangent, gates, w, gains, [*grad_line, grad_other])
    das = [send(da, hop) for hop in range(Z)]
    extra_line, extra_cross = extra_halves(keep_extra, after(got_extra, da))
    shadows = shadow(after(qkv, extra_cross), h2, dlogits, scaled)
    results = after(results, shadows[1], *das[1:])
    results_cross = [send(results[Z + hop], hop, True) for hop in range(Z)]
    *returns, keep, give = head_back(
        behind,
        core.astype(jnp.int32)[None],
        qkv,
        h1,
        w,
        ob_full,
        shadows,
        cosine,
        signed,
        das,
        weights,
        results[:Z],
    )
    parts = split(dests, keep, swap_core(after(give, *results_cross[1:])))
    extra_got = send_chip(extra_cross, LINE)
    parts = after(parts, expert_share)
    lines = [send_chip(parts[hop], hop) for hop in range(LINE)]
    results_other = send(add_all(results_cross, "line_results"), Z)
    first, third = send(returns[1], 1, True), send(returns[3], 3, True)
    lines[0] = after(lines[0], first, third)
    second = send(after(returns[2], first, third), 2, True)
    returns = [returns[0], first, second, third]
    share = sum_lines(lines)
    extra_parts = extra_lines(extra_line, after(extra_got, share[1]))
    share = add_all([share[0], send_chip(share[1], LINE)], "sum_chips")
    share = add_all([share, send(share, Z)], "sum_halves")
    extra_first, extra_third = (send_chip(extra_parts[hop], hop) for hop in (1, 3))
    share = after(share, second)
    extra_second = send_chip(extra_parts[2], 2)
    extra_parts = [extra_parts[0], extra_first, extra_second, extra_third]
    shares = [send(share, hop) for hop in range(Z)]
    grad_gate, grad_up, grad_down = unpack(expert_share, extra_parts)
    grad_tokens = token_grad(tokens, gains, dx1, returns)
    mixed_out = mix(x1, returns, results_other)
    shares = after(shares, grad_tokens, mixed_out, grad_gate)
    grad_query, grad_key, grad_value, grad_out, router, one, two = finish(
        behind, shares, w_query, key_weight, value_weight, norm_one[None, :]
    )

    return (
        mixed_out,
        grad_tokens,
        one.reshape(ROWS),
        grad_query,
        grad_key,
        grad_value,
        grad_out,
        two.reshape(ROWS),
        router.T,
        grad_gate,
        grad_up,
        jnp.swapaxes(grad_down, 1, 2),
    )


def solution(mesh):
    return jax.shard_map(
        body,
        mesh=mesh,
        in_specs=(
            P(("expert", "fsdp"), None),
            P(("expert", "fsdp"), None),
            P(("expert", "fsdp"), None),
            P("fsdp"),
            P("fsdp", None),
            P("fsdp", None),
            P("fsdp", None),
            P("fsdp", None),
            P("fsdp"),
            P("fsdp", None),
            P("expert", "fsdp", None),
            P("expert", "fsdp", None),
            P("expert", None, "fsdp"),
        ),
        out_specs=(
            P(("expert", "fsdp"), None),
            P(("expert", "fsdp"), None),
            P("fsdp"),
            P("fsdp", None),
            P("fsdp", None),
            P("fsdp", None),
            P("fsdp", None),
            P("fsdp"),
            P("fsdp", None),
            P("expert", "fsdp", None),
            P("expert", "fsdp", None),
            P("expert", None, "fsdp"),
        ),
        check_vma=False,
    )
```

```python
import jax
import jax.numpy as jnp
import numpy as np
from jax import lax
from jax.experimental import pallas as pl
from jax.experimental.pallas import tpu as pltpu
from jax.sharding import PartitionSpec as P

QUERY_HEADS = 24
KEY_VALUE_HEADS = 8
GROUP = QUERY_HEADS // KEY_VALUE_HEADS
HEAD_DIM = 64
HALF = HEAD_DIM // 2
E = 40
H = 512
D = 1536
T = 128
CAP = 32
NORM_EPSILON = 1e-05
SCALE = HEAD_DIM ** (-0.5)

Z = 4
PEERS = 8
LOCAL = E // PEERS
SLOTS = LOCAL * CAP
EXTRA = 1
PLAIN = LOCAL - EXTRA
LANES = 128
CHIPS = 8
LINE = 4
TOPK = 8
SHARDS = 2 * CHIPS
ROWS = D // SHARDS
QH = QUERY_HEADS // Z
KH = KEY_VALUE_HEADS // Z
QW = QH * HEAD_DIM
KW = KH * HEAD_DIM
QKV = QW + 2 * KW
MAIN = QW + QKV
SLICE = MAIN + LANES
VMEM_LIMIT = 60 * 1024 * 1024

F32 = jnp.float32
BF16 = jnp.bfloat16


def peer(index, hop, back=False):
    shift = hop % Z
    turned = (index % Z + (Z - shift if back else shift)) % Z
    return (index // Z + hop // Z) % 2 * Z + turned


def send(value, hop, back=False):
    if hop == 0:
        return value
    return lax.ppermute(value, "expert", [(i, peer(i, hop, back)) for i in range(PEERS)])


def chip_at(index, hop, back=False):
    shift = hop % 4
    turned = (index // 2 % 4 + (4 - shift if back else shift)) % 4
    return (index // 8 + hop // 4) % 2 * 4 + turned


def send_chip(value, hop):
    if hop == 0:
        return value
    pairs = [(i, 2 * chip_at(i, hop) + i % 2) for i in range(SHARDS)]
    return lax.ppermute(value, "fsdp", pairs)


def after(value, *others):
    return lax.optimization_barrier((value, others))[0]


def swap_core(value):
    return lax.ppermute(value, "fsdp", [(i, i ^ 1) for i in range(SHARDS)])


def mm(left, right):
    return jnp.dot(left, right, preferred_element_type=F32)


def mm_nt(left, right):
    return lax.dot_general(left, right, (((1,), (1,)), ((), ())), preferred_element_type=F32)


def mm_tn(left, right):
    return lax.dot_general(left, right, (((0,), (0,)), ((), ())), preferred_element_type=F32)


def rope_tables():
    frequency = np.exp(-np.log(10000.0) * np.arange(HALF, dtype=np.float64) * 2.0 / HEAD_DIM)
    angles = np.arange(T, dtype=np.float64)[:, None] * frequency[None, :]
    cosine = np.tile(np.cos(angles), (1, 4)).astype(np.float32)
    sine = np.sin(angles)
    signed = np.tile(np.concatenate([-sine, sine], axis=1), (1, 2)).astype(np.float32)
    return cosine, signed


def swap_halves(values):
    width = values.shape[1]
    lane = lax.broadcasted_iota(jnp.int32, values.shape, 1)
    up = pltpu.roll(values, width - HALF, 1)
    down = pltpu.roll(values, HALF, 1)
    return jnp.where(lane % HEAD_DIM < HALF, up, down)


def wide(table, width):
    return jnp.concatenate([table] * (width // LANES), axis=1)


def rotate(values, cosine, signed):
    width = values.shape[1]
    return values * wide(cosine, width) + swap_halves(values) * wide(signed, width)


def rotate_back(values, cosine, signed):
    width = values.shape[1]
    return values * wide(cosine, width) + swap_halves(values * wide(signed, width))


def gain_rows(small):
    pick = lax.broadcasted_iota(jnp.int32, (16, LANES), 1) == (
        lax.broadcasted_iota(jnp.int32, (16, LANES), 0) + E
    )
    return mm_nt(pick.astype(BF16), small)


def norm_of(values):
    inverse = lax.rsqrt(jnp.mean(values * values, axis=-1, keepdims=True) + NORM_EPSILON)
    return values * inverse, inverse


def head(ref, rows, index):
    return ref[rows, index * HEAD_DIM : (index + 1) * HEAD_DIM]


def stack_heads(ref, rows, first):
    return jnp.concatenate([head(ref, rows, first + index) for index in range(GROUP)], axis=0)


def probabilities(query, key):
    scores = mm_nt(query, key) * SCALE
    rows = lax.broadcasted_iota(jnp.int32, scores.shape, 0) % T
    cols = lax.broadcasted_iota(jnp.int32, scores.shape, 1)
    scores = jnp.where(rows >= cols, scores, -jnp.inf)
    exponent = jnp.exp(scores - jnp.max(scores, axis=-1, keepdims=True))
    return exponent / jnp.sum(exponent, axis=-1, keepdims=True)


def whole(shape):
    return pl.BlockSpec(shape, lambda *_: (0,) * len(shape))


SCALARS = pl.BlockSpec(memory_space=pltpu.SMEM)
ANYWHERE = pl.BlockSpec(memory_space=pl.ANY)


def params(**more):
    return pltpu.CompilerParams(vmem_limit_bytes=VMEM_LIMIT, **more)


WEIGHT = 60


def cost(flops, moved):
    return pl.CostEstimate(flops=flops * WEIGHT, bytes_accessed=moved * WEIGHT, transcendentals=0)


def shape(dims, kind):
    return jax.ShapeDtypeStruct(dims, kind)


def call(kernel, name, inputs, in_specs, outputs, out_specs=None, scratch=(), flops=0, moved=0):
    in_specs = [whole(v.shape) if spec is None else spec for v, spec in zip(inputs, in_specs)]
    if out_specs is None:
        out_specs = [whole(o.shape) for o in outputs]
    return pl.pallas_call(
        kernel,
        grid=(1,),
        in_specs=in_specs,
        out_specs=out_specs,
        out_shape=outputs,
        scratch_shapes=list(scratch),
        compiler_params=params(),
        cost_estimate=cost(flops, moved),
        name=name,
    )(*inputs)


SMALL_SPEC = pl.BlockSpec((SHARDS, ROWS, LANES), lambda *_: (0, 0, QKV // LANES))
X_SPEC = pl.BlockSpec((T, D), lambda *_: (0, 0))
DY_SPEC = pl.BlockSpec((T, D), lambda *_: (0, 1))


def small_of(ref):
    return ref[...].reshape(D, LANES)


def columns_of(index):
    return pl.ds(pl.multiple_of(index * QW, QW), QW)


def pack_kernel(
    z_ref, out_ref, query_ref, key_ref, value_ref, router_ref, one_ref, two_ref, first_ref, second_ref
):
    first_ref[:, 0:QW] = query_ref[...]
    first_ref[:, QW : QW + KW] = key_ref[...]
    first_ref[:, QW + KW : QKV] = value_ref[...]
    narrow = [router_ref[...], one_ref[...], two_ref[...], jnp.zeros((LANES - E - 2, ROWS), BF16)]
    first_ref[:, QKV:] = jnp.concatenate([v.astype(F32) for v in narrow], axis=0).T.astype(BF16)
    second_ref[...] = out_ref[...]


def pack(z, w_out, w_query, key_weight, value_weight, router, one, two):
    def slice_of(width):
        return pl.BlockSpec((ROWS, width), lambda i, z: (0, z[0]))

    return pl.pallas_call(
        pack_kernel,
        grid_spec=pltpu.PrefetchScalarGridSpec(
            num_scalar_prefetch=1,
            grid=(1,),
            in_specs=[
                slice_of(QW),
                slice_of(QW),
                slice_of(KW),
                slice_of(KW),
                whole((E, ROWS)),
                whole((1, ROWS)),
                whole((1, ROWS)),
            ],
            out_specs=[whole((ROWS, QKV + LANES)), whole((ROWS, QW))],
        ),
        out_shape=[shape((ROWS, QKV + LANES), BF16), shape((ROWS, QW), BF16)],
        compiler_params=params(),
        cost_estimate=cost(ROWS * SLICE, 1 << 20),
        name="pack",
    )(z, w_out, w_query, key_weight, value_weight, router, one, two)


def project_kernel(order_ref, cos_ref, sin_ref, *refs):
    own, other, xs = refs[:LINE], refs[LINE : 2 * LINE], refs[2 * LINE : 2 * LINE + Z]
    w_ref, gains_ref, h1_ref, qkv_ref, ob_ref = refs[2 * LINE + Z :]
    for chip in range(CHIPS):
        w_ref[order_ref[chip]] = own[chip % LINE][chip // LINE]
        w_ref[order_ref[CHIPS + chip]] = other[chip % LINE][chip // LINE]
    gains = gain_rows(w_ref[:, :, QKV:].reshape(D, LANES))
    gains_ref[...] = gains
    for hop in range(Z):
        normed, _ = norm_of(xs[hop][...].astype(F32))
        h1_ref[hop * T : (hop + 1) * T] = (normed * gains[0:1, :]).astype(BF16)
    pre = mm(h1_ref[...], w_ref[:, :, 0:QKV].reshape(D, QKV))
    cosine = jnp.concatenate([cos_ref[...]] * Z, axis=0)
    signed = jnp.concatenate([sin_ref[...]] * Z, axis=0)
    qkv_ref[:, 0:QW] = rotate(pre[:, 0:QW], cosine, signed).astype(BF16)
    qkv_ref[:, QW : QW + KW] = rotate(pre[:, QW : QW + KW], cosine, signed).astype(BF16)
    qkv_ref[:, QW + KW :] = pre[:, QW + KW :].astype(BF16)
    for hop in range(Z):
        rows = slice(hop * T, (hop + 1) * T)
        for group in range(KH):
            key, value = head(qkv_ref, rows, QH + group), head(qkv_ref, rows, QH + KH + group)
            query = stack_heads(qkv_ref, rows, group * GROUP)
            result = mm(probabilities(query, key).astype(BF16), value).astype(BF16)
            for index in range(GROUP):
                at = (group * GROUP + index) * HEAD_DIM
                ob_ref[rows, at : at + HEAD_DIM] = result[index * T : (index + 1) * T]


def project(order, cosine, signed, own, other, xs):
    return call(
        project_kernel,
        "project",
        [order, cosine, signed, *own, *other, *xs],
        [SCALARS] + [None] * (2 + 2 * LINE) + [X_SPEC] * Z,
        [
            shape((SHARDS, ROWS, QKV + LANES), BF16),
            shape((16, D), F32),
            shape((Z * T, D), BF16),
            shape((Z * T, QKV), BF16),
            shape((Z * T, QW), BF16),
        ],
        flops=2 * Z * T * D * QKV,
        moved=12 << 20,
    )


def out_project_kernel(peers_ref, order_ref, *refs):
    own, other, obs = refs[:LINE], refs[LINE : 2 * LINE], refs[2 * LINE : 2 * LINE + Z]
    w_ref, full_ref, *outs = refs[2 * LINE + Z :]
    for chip in range(CHIPS):
        w_ref[order_ref[chip]] = own[chip % LINE][chip // LINE]
        w_ref[order_ref[CHIPS + chip]] = other[chip % LINE][chip // LINE]
    total = jnp.zeros((Z * T, QW), F32)
    for hop in range(Z):
        peer_index = peers_ref[hop]
        blocks = [(row - hop) % Z for row in range(Z)]
        rows = jnp.concatenate([obs[hop][b * T : (b + 1) * T, :] for b in blocks], axis=0)
        full_ref[:, columns_of(peer_index)] = rows
        weight = w_ref[pl.ds(peer_index * Z, Z)].reshape(QW, QW)
        total = total + mm(rows, weight)
    for hop in range(Z):
        outs[hop][...] = total[hop * T : (hop + 1) * T].astype(BF16)


def out_project(peers, order, own, other, obs):
    return call(
        out_project_kernel,
        "out_project",
        [peers, order, *own, *other, *obs],
        [SCALARS] * 2 + [None] * (2 * LINE + Z),
        [shape((SHARDS, ROWS, QW), BF16), shape((Z * T, D), BF16)] + [shape((T, QW), BF16)] * Z,
        flops=2 * Z * T * D * QW,
        moved=6 << 20,
    )


def cut_out_kernel(peers_ref, w_ref, *outs):
    for hop in range(Z):
        outs[hop][...] = w_ref[pl.ds(peers_ref[hop] * Z, Z)].reshape(QW, QW)


def cut_out(peers, w):
    return call(
        cut_out_kernel,
        "cut_out",
        [peers, w],
        [SCALARS, None],
        [shape((QW, QW), BF16)] * Z,
        flops=D * QW,
        moved=2 << 20,
    )


def residual_kernel(peers_ref, x_ref, gains_ref, *refs):
    pieces, (x1_ref, h2_ref) = refs[:Z], refs[Z:]
    x1_ref[...] = x_ref[...].astype(F32)
    for hop in range(Z):
        x1_ref[:, columns_of(peers_ref[hop])] += pieces[hop][...].astype(F32)
    normed, _ = norm_of(x1_ref[...])
    h2_ref[...] = (normed * gains_ref[1:2, :]).astype(BF16)


def residual(peers, x, gains, pieces):
    return call(
        residual_kernel,
        "residual",
        [peers, x, gains, *pieces],
        [SCALARS] + [None] * (2 + Z),
        [shape((T, D), F32), shape((T, D), BF16)],
        flops=T * D * 8,
        moved=2 << 20,
    )


def gate_kernel(small_ref, member_ref, chosen_ref, place_ref, *refs):
    rows, (gates_ref, slot_gate_ref, b_ref) = refs[:Z], refs[Z:]
    small = small_of(small_ref)
    for hop in range(Z):
        h2 = rows[hop][...]
        member = member_ref[hop] > 0.5
        logits = jnp.where(member, mm(h2, small), -jnp.inf)
        exponent = jnp.exp(logits - jnp.max(logits, axis=-1, keepdims=True))
        gates = exponent / jnp.sum(exponent, axis=-1, keepdims=True)
        gates_ref[hop] = gates
        high = gates.astype(BF16)
        low = (gates - high.astype(F32)).astype(BF16)
        place = place_ref[hop]
        spread = mm(place, high) + mm(place, low)
        picked = jnp.sum(spread * chosen_ref[...], axis=-1, keepdims=True)
        slot_gate_ref[:, hop] = picked.reshape(LOCAL, CAP, 1)
        b_ref[:, hop] = mm(place, h2).astype(BF16).reshape(LOCAL, CAP, D)


def gate_rows(half, w, member, chosen, place, rows):
    gates, slot_gate, b = call(
        gate_kernel,
        "gate_rows",
        [w, member, chosen, place, *rows],
        [
            SMALL_SPEC,
            pl.BlockSpec((Z, T, LANES), lambda *_: (half, 0, 0)),
            None,
            pl.BlockSpec((Z, SLOTS, T), lambda *_: (half, 0, 0)),
        ]
        + [None] * Z,
        [
            shape((Z, T, LANES), F32),
            shape((LOCAL, Z, CAP, 1), F32),
            shape((LOCAL, Z, CAP, D), BF16),
        ],
        flops=2 * Z * SLOTS * T * D,
        moved=5 << 20,
    )
    return gates, slot_gate.reshape(LOCAL, Z * CAP, 1), b.reshape(LOCAL, Z * CAP, D)


def spread_kernel(place_ref, *refs):
    rows, out_ref = refs[:PEERS], refs[PEERS]
    for hop in range(PEERS):
        out_ref[:, hop] = mm(place_ref[hop], rows[hop][...]).astype(BF16).reshape(LOCAL, CAP, D)


def spread_rows(place, line, other):
    return call(
        spread_kernel,
        "spread_rows",
        [place, *line, *other],
        [None] + [DY_SPEC] * Z + [X_SPEC] * Z,
        [shape((LOCAL, PEERS, CAP, D), BF16)],
        flops=2 * PEERS * SLOTS * T * D,
        moved=8 << 20,
    )[0].reshape(LOCAL, PEERS * CAP, D)


def expert_step(expert, b_refs, dyr_ref, gate_refs, first, down, gy_ref, db_ref):
    rows = jnp.concatenate([ref[0] for ref in b_refs], axis=0)
    gate = jnp.concatenate([ref[0] for ref in gate_refs], axis=0)
    pre = mm(rows, first())
    gate_pre, up_pre = pre[:, :H], pre[:, H:]
    sigmoid = 1.0 / (1.0 + jnp.exp(-gate_pre))
    silu = gate_pre * sigmoid
    activated = (silu * up_pre).astype(BF16)
    result = mm_nt(activated, down()).astype(BF16).astype(F32)
    raw = dyr_ref[0].astype(F32)
    gy_ref[0] = (gate * result).astype(BF16)
    inner = jnp.sum(raw * result, axis=-1, keepdims=True)
    grad_rows = (gate * raw).astype(BF16)
    grad_act = mm(grad_rows, down())
    grad_gate = (grad_act * up_pre * sigmoid * (1.0 + gate_pre * (1.0 - sigmoid))).astype(BF16)
    grad_up = (grad_act * silu).astype(BF16)
    both = jnp.concatenate([grad_gate, grad_up], axis=1)
    db_ref[0, :, 0:D] = mm_nt(both, first()).astype(BF16)
    lane = lax.broadcasted_iota(jnp.int32, (PEERS * CAP, LANES), 1)
    high = inner.astype(BF16).astype(F32)
    low = inner - high
    tail = jnp.where(lane == expert, high, jnp.where(lane == expert + E, low, 0.0))
    db_ref[0, :, D : D + LANES] = tail.astype(BF16)
    return rows, both, grad_rows, activated


def expert_kernel(
    me_ref, b0_ref, b1_ref, dyr_ref, gate0_ref, gate1_ref, w_ref, gy_ref, db_ref, grad_ref
):
    rows, both, grad_rows, activated = expert_step(
        me_ref[0] * LOCAL + pl.program_id(0),
        (b0_ref, b1_ref),
        dyr_ref,
        (gate0_ref, gate1_ref),
        lambda: w_ref[0, :, 0 : 2 * H],
        lambda: w_ref[0, :, 2 * H : 3 * H],
        gy_ref,
        db_ref,
    )
    grad_ref[0, :, 0 : 2 * H] = mm_tn(rows, both).astype(BF16)
    grad_ref[0, :, 2 * H : 3 * H] = mm_tn(grad_rows, activated).astype(BF16)


def per_expert(*dims, first=0):
    return pl.BlockSpec((1,) + dims, lambda e: (e + first, 0, 0))


def row_specs(first):
    half = PEERS * CAP // 2
    return [
        SCALARS,
        per_expert(half, D, first=first),
        per_expert(half, D, first=first),
        per_expert(2 * half, D, first=first),
        per_expert(half, 1, first=first),
        per_expert(half, 1, first=first),
    ]


def experts(me, b, dyr, slot_gate, pack):
    rows = PEERS * CAP
    return pl.pallas_call(
        expert_kernel,
        grid=(PLAIN,),
        in_specs=row_specs(0) + [per_expert(D, 3 * H)],
        out_specs=[per_expert(rows, D), per_expert(rows, D + LANES), per_expert(D, 3 * H)],
        out_shape=[
            shape((PLAIN, rows, D), BF16),
            shape((PLAIN, rows, D + LANES), BF16),
            shape((PLAIN, D, 3 * H), BF16),
        ],
        compiler_params=params(),
        cost_estimate=cost(18 * PLAIN * rows * D * H, 12 * PLAIN << 20),
        name="experts",
    )(me, *b, dyr, *slot_gate, pack)


def extra_kernel(
    me_ref,
    b0_ref,
    b1_ref,
    dyr_ref,
    gate0_ref,
    gate1_ref,
    dests_ref,
    w_ref,
    gy_ref,
    db_ref,
    keep_ref,
    give_ref,
    grads,
):
    rows, both, grad_rows, activated = expert_step(
        me_ref[0] * LOCAL + PLAIN + pl.program_id(0),
        (b0_ref, b1_ref),
        dyr_ref,
        (gate0_ref, gate1_ref),
        lambda: w_ref[0, :, 0 : 2 * H],
        lambda: w_ref[0, :, 2 * H : 3 * H],
        gy_ref,
        db_ref,
    )
    grads[:, :, 0 : 2 * H] = mm_tn(rows, both).astype(BF16).reshape(SHARDS, ROWS, 2 * H)
    grads[:, :, 2 * H : 3 * H] = mm_tn(grad_rows, activated).astype(BF16).reshape(SHARDS, ROWS, H)
    for chip in range(CHIPS):
        keep_ref[chip, 0] = grads[dests_ref[chip]]
        give_ref[chip, 0] = grads[dests_ref[CHIPS + chip]]


def extra_experts(me, b, dyr, slot_gate, dests, pack):
    rows = PEERS * CAP
    blocks = pl.BlockSpec((CHIPS, 1, ROWS, 3 * H), lambda e: (0, e, 0, 0))
    return pl.pallas_call(
        extra_kernel,
        grid=(EXTRA,),
        in_specs=row_specs(PLAIN) + [SCALARS, per_expert(D, 3 * H, first=PLAIN)],
        out_specs=[per_expert(rows, D), per_expert(rows, D + LANES), blocks, blocks],
        out_shape=[
            shape((EXTRA, rows, D), BF16),
            shape((EXTRA, rows, D + LANES), BF16),
            shape((CHIPS, EXTRA, ROWS, 3 * H), BF16),
            shape((CHIPS, EXTRA, ROWS, 3 * H), BF16),
        ],
        scratch_shapes=[pltpu.VMEM((SHARDS, ROWS, 3 * H), BF16)],
        compiler_params=params(),
        cost_estimate=cost(18 * EXTRA * rows * D * H, 14 * EXTRA << 20),
        name="extra_experts",
    )(me, *b, dyr, *slot_gate, dests, pack)


def extra_halves_kernel(keep_ref, got_ref, line_ref, cross_ref):
    total = (keep_ref[0].astype(F32) + got_ref[0].astype(F32)).astype(BF16)

    @pl.when(pl.program_id(0) < LINE)
    def _():
        cross_ref[0] = total

    @pl.when(pl.program_id(0) >= LINE)
    def _():
        line_ref[0] = total


def extra_halves(keep, got):
    block = (1, EXTRA, ROWS, 3 * H)
    return pl.pallas_call(
        extra_halves_kernel,
        grid=(CHIPS,),
        in_specs=[pl.BlockSpec(block, lambda i: ((i + LINE) % CHIPS, 0, 0, 0))] * 2,
        out_specs=[
            pl.BlockSpec(block, lambda i: (jnp.maximum(i - LINE, 0), 0, 0, 0)),
            pl.BlockSpec(block, lambda i: (jnp.minimum(i, LINE - 1), 0, 0, 0)),
        ],
        out_shape=[shape((LINE, EXTRA, ROWS, 3 * H), BF16)] * 2,
        compiler_params=params(),
        cost_estimate=cost(keep.size, 6 * keep.size),
        name="extra_halves",
    )(keep, got)


def extra_lines_kernel(line_ref, got_ref, *outs):
    for hop in range(LINE):
        outs[hop][...] = (line_ref[hop].astype(F32) + got_ref[hop].astype(F32)).astype(BF16)


def extra_lines(line, got):
    return call(
        extra_lines_kernel,
        "extra_lines",
        [line, got],
        [None, None],
        [shape((EXTRA, ROWS, 3 * H), BF16)] * LINE,
        flops=line.size,
        moved=6 * line.size,
    )


def collect_kernel(place_ref, plain_ref, extra_ref, *out_refs):
    for hop in range(PEERS):
        rows = jnp.concatenate(
            [ref[:, hop].reshape(-1, ref.shape[-1]) for ref in (plain_ref, extra_ref)], axis=0
        )
        out_refs[hop][...] = mm_tn(place_ref[hop], rows).astype(BF16)


def collect(place, values, name):
    width = values[0].shape[-1]
    return call(
        collect_kernel,
        name,
        [place, *(v.reshape(-1, PEERS, CAP, width) for v in values)],
        [None] * 3,
        [shape((T, width), BF16)] * PEERS,
        flops=2 * PEERS * SLOTS * T * width,
        moved=8 << 20,
    )


def mix(x1, returns, other):
    return call(
        add_kernel,
        "mix",
        [x1, *returns, other],
        [None] + [DY_SPEC] * Z + [None],
        [shape((T, D), BF16)],
        flops=T * D * Z,
        moved=4 << 20,
    )[0]


def norm_back(grad, normed, inverse, gain):
    scaled = grad * gain
    return inverse * (scaled - normed * jnp.mean(scaled * normed, axis=-1, keepdims=True))


def token_back_kernel(
    x1_ref, dy_ref, gates_ref, small_ref, gains_ref, *refs
):
    parts, (dx1_ref, dlogits_ref, scaled_ref, da_ref) = refs[: Z + 1], refs[Z + 1 :]
    total = parts[0][...].astype(F32)
    for ref in parts[1:]:
        total = total + ref[...].astype(F32)
    grad, tail = total[:, :D], total[:, D:]
    lane = lax.broadcasted_iota(jnp.int32, (T, LANES), 1)
    inner = jnp.where(lane < E, tail + pltpu.roll(tail, LANES - E, 1), 0.0)
    gates = gates_ref[0]
    score = gates * (inner - jnp.sum(gates * inner, axis=-1, keepdims=True))
    dlogits_ref[...] = score.astype(BF16)
    grad = grad + mm_nt(dlogits_ref[...], small_of(small_ref))
    normed, inverse = norm_of(x1_ref[...])
    scaled_ref[...] = (grad * normed).astype(BF16)
    through = dy_ref[...].astype(F32) + norm_back(grad, normed, inverse, gains_ref[1:2, :])
    dx1_ref[...] = through
    da_ref[...] = through.astype(BF16)


def token_back(x1, dy, gates, w, gains, parts):
    return call(
        token_back_kernel,
        "token_back",
        [x1, dy, gates, w, gains, *parts],
        [None, None, pl.BlockSpec((1, T, LANES), lambda *_: (0, 0, 0)), SMALL_SPEC]
        + [None] * (1 + len(parts)),
        [
            shape((T, D), F32),
            shape((T, LANES), BF16),
            shape((T, D), BF16),
            shape((T, D), BF16),
        ],
        flops=T * D * 64,
        moved=6 << 20,
    )


def shadow_kernel(qkv_ref, h2_ref, dlogits_ref, scaled_ref, small_ref, prob_ref):
    lane = lax.broadcasted_iota(jnp.int32, (T, LANES), 1)
    small = mm_tn(h2_ref[...], dlogits_ref[...])
    small_ref[...] = small + mm_tn(scaled_ref[...], (lane == E + 1).astype(BF16))
    for hop in range(Z):
        rows = slice(hop * T, (hop + 1) * T)
        for group in range(KH):
            query = stack_heads(qkv_ref, rows, group * GROUP)
            prob_ref[hop * KH + group] = probabilities(query, head(qkv_ref, rows, QH + group))


def shadow(qkv, h2, dlogits, scaled):
    return call(
        shadow_kernel,
        "shadow",
        [qkv, h2, dlogits, scaled],
        [None] * 4,
        [shape((D, LANES), F32), shape((Z * KH, GROUP * T, T), F32)],
        flops=Z * T * D * QW,
        moved=6 << 20,
    )


def head_back_kernel(
    behind_ref,
    parity_ref,
    qkv_ref,
    h1_ref,
    w_ref,
    full_ref,
    partial_ref,
    prob_ref,
    cos_ref,
    sin_ref,
    *refs,
):
    das, weights, results, outs = (refs[at * Z : at * Z + Z] for at in range(4))
    keep_ref, give_ref, dob, dqk, dqkv, h1, w, full, sems = refs[4 * Z :]
    late = [(h1_ref, h1), (w_ref, w), (full_ref, full)]
    late += [(results[hop], outs[hop].at[:, pl.ds(D, D)]) for hop in range(Z)]
    late = [pltpu.make_async_copy(a, b, sems.at[at]) for at, (a, b) in enumerate(late)]
    for copy in late:
        copy.start()
    total = jnp.zeros((Z * T, QW), F32)
    for hop in range(Z):
        columns = columns_of(behind_ref[hop])
        rows = jnp.concatenate([ref[:, columns] for ref in das], axis=0)
        total = total + mm_nt(rows, weights[hop][...])
        if hop == 0:
            own_columns = rows
    dob[...] = total.astype(BF16)
    for hop in range(Z):
        rows = slice(hop * T, (hop + 1) * T)
        for group in range(KH):
            key, value = head(qkv_ref, rows, QH + group), head(qkv_ref, rows, QH + KH + group)
            query = stack_heads(qkv_ref, rows, group * GROUP)
            out_grad = stack_heads(dob, rows, group * GROUP)
            probability = prob_ref[hop * KH + group]
            grad_prob = mm_nt(out_grad, value)
            held = jnp.sum(probability * grad_prob, axis=-1, keepdims=True)
            grad_scores = (probability * (grad_prob - held)).astype(BF16)
            grad_query = mm(grad_scores, key) * SCALE
            for index in range(GROUP):
                at = (group * GROUP + index) * HEAD_DIM
                dqk[rows, at : at + HEAD_DIM] = grad_query[index * T : (index + 1) * T]
            at = QW + group * HEAD_DIM
            dqk[rows, at : at + HEAD_DIM] = mm_tn(grad_scores, query) * SCALE
            dqkv[rows, at + KW : at + KW + HEAD_DIM] = mm_tn(
                probability.astype(BF16), out_grad
            ).astype(BF16)
    cosine = jnp.concatenate([cos_ref[...]] * Z, axis=0)
    signed = jnp.concatenate([sin_ref[...]] * Z, axis=0)
    dqkv[:, 0 : QW + KW] = rotate_back(dqk[...], cosine, signed).astype(BF16)
    even = parity_ref[0] == 0

    def store(grads, columns):
        pair = grads.astype(BF16).reshape(CHIPS, 2, ROWS, grads.shape[1])
        keep_ref[:, :, columns] = jnp.where(even, pair[:, 0], pair[:, 1])
        give_ref[:, :, columns] = jnp.where(even, pair[:, 1], pair[:, 0])

    late[2].wait()
    store(mm_tn(full[...], own_columns), slice(0, QW))
    late[0].wait()
    store(mm_tn(h1[...], dqkv[...]), slice(QW, MAIN))
    late[1].wait()
    dh1 = mm_nt(dqkv[...], w[:, :, 0:QKV].reshape(D, QKV))
    for hop in range(Z):
        outs[hop][:, 0:D] = dh1[hop * T : (hop + 1) * T].astype(BF16)
        late[3 + hop].wait()
    store(partial_ref[...], slice(MAIN, SLICE))


def head_back(behind, parity, qkv, h1, w, full, shadows, cosine, signed, das, weights, results):
    return call(
        head_back_kernel,
        "head_back",
        [behind, parity, qkv, h1, w, full, *shadows, cosine, signed, *das, *weights, *results],
        [SCALARS] * 2
        + [None, ANYWHERE, ANYWHERE, ANYWHERE]
        + [None] * (4 + 2 * Z)
        + [ANYWHERE] * Z,
        [shape((T, 2 * D), BF16)] * Z + [shape((CHIPS, ROWS, SLICE), BF16)] * 2,
        scratch=[
            pltpu.VMEM((Z * T, QW), BF16),
            pltpu.VMEM((Z * T, QW + KW), F32),
            pltpu.VMEM((Z * T, QKV), BF16),
            pltpu.VMEM((Z * T, D), BF16),
            pltpu.VMEM((SHARDS, ROWS, QKV + LANES), BF16),
            pltpu.VMEM((Z * T, D), BF16),
            pltpu.SemaphoreType.DMA((3 + Z,)),
        ],
        flops=4 * Z * T * D * QKV,
        moved=16 << 20,
    )


def token_grad_kernel(x_ref, gains_ref, dx1_ref, *refs):
    grad = refs[0][...].astype(F32)
    for hop in range(1, Z):
        grad = grad + refs[hop][...].astype(F32)
    normed, inverse = norm_of(x_ref[...].astype(F32))
    refs[Z][...] = dx1_ref[...] + norm_back(grad, normed, inverse, gains_ref[0:1, :])


def token_grad(x, gains, dx1, pieces):
    return call(
        token_grad_kernel,
        "token_grad",
        [x, gains, dx1, *pieces],
        [None] * 3 + [X_SPEC] * Z,
        [shape((T, D), F32)],
        flops=T * D * 16,
        moved=4 << 20,
    )[0]


def split_kernel(order_ref, keep_ref, got_ref, *outs):
    for chip in range(CHIPS):
        at = order_ref[chip]
        total = (keep_ref[at].astype(F32) + got_ref[at].astype(F32)).astype(BF16)
        outs[chip % 4][chip // 4] = total


def split(order, keep, got):
    return call(
        split_kernel,
        "split",
        [order, keep, got],
        [SCALARS, None, None],
        [shape((2, ROWS, SLICE), BF16)] * 4,
        flops=CHIPS * ROWS * SLICE,
        moved=6 << 20,
    )


def add_kernel(*refs):
    total = refs[0][...].astype(F32)
    for ref in refs[1:-1]:
        total = total + ref[...].astype(F32)
    refs[-1][...] = total.astype(BF16)


def sum_lines_kernel(*refs):
    for at in range(2):
        total = refs[0][at].astype(F32)
        for ref in refs[1:LINE]:
            total = total + ref[at].astype(F32)
        refs[LINE + at][...] = total.astype(BF16)


def sum_lines(parts):
    return call(
        sum_lines_kernel,
        "sum_lines",
        list(parts),
        [None] * LINE,
        [shape((ROWS, SLICE), BF16)] * 2,
        flops=LINE * ROWS * SLICE,
        moved=12 * ROWS * SLICE,
    )


def add_all(parts, name):
    return call(
        add_kernel,
        name,
        list(parts),
        [None] * len(parts),
        [shape(parts[0].shape, BF16)],
        flops=parts[0].size * len(parts),
        moved=2 * parts[0].size * (len(parts) + 1),
    )[0]


def finish_kernel(order_ref, *refs):
    parts, (wq_ref, wk_ref, wv_ref, gain_ref) = refs[:Z], refs[Z : Z + 4]
    q_ref, k_ref, v_ref, o_ref, router_ref, one_ref, two_ref, narrow = refs[Z + 4 :]
    for hop in range(Z):
        at = order_ref[hop]
        part = parts[hop][...].astype(F32)
        o_ref[:, columns_of(at)] = part[:, 0:QW]
        q_ref[:, columns_of(at)] = part[:, QW : 2 * QW]
        heads = pl.ds(pl.multiple_of(at * KW, KW), KW)
        k_ref[:, heads] = part[:, 2 * QW : 2 * QW + KW]
        v_ref[:, heads] = part[:, 2 * QW + KW : MAIN]
        narrow[at] = part[:, MAIN:]
    scaled = jnp.zeros((ROWS, 1), F32)
    for weight, grad in ((wq_ref, q_ref), (wk_ref, k_ref), (wv_ref, v_ref)):
        scaled += jnp.sum(weight[...].astype(F32) * grad[...], axis=-1, keepdims=True)
    small = narrow[0] + narrow[1] + narrow[2] + narrow[3]
    lane = lax.broadcasted_iota(jnp.int32, small.shape, 1)
    small = jnp.where(lane == E, scaled, small).T
    router_ref[...] = small[0:E]
    one_ref[...] = small[E : E + 1] / gain_ref[...].astype(F32)
    two_ref[...] = small[E + 1 : E + 2]


def finish(order, parts, w_query, key_weight, value_weight, gain):
    return call(
        finish_kernel,
        "finish",
        [order, *parts, w_query, key_weight, value_weight, gain],
        [SCALARS] + [None] * (Z + 4),
        [
            shape((ROWS, D), F32),
            shape((ROWS, KEY_VALUE_HEADS * HEAD_DIM), F32),
            shape((ROWS, KEY_VALUE_HEADS * HEAD_DIM), F32),
            shape((ROWS, D), F32),
            shape((E, ROWS), F32),
            shape((1, ROWS), F32),
            shape((1, ROWS), F32),
        ],
        scratch=[pltpu.VMEM((Z, ROWS, LANES), F32)],
        flops=ROWS * SLICE * Z,
        moved=3 << 20,
    )


def unpack_kernel(share_ref, *refs):
    parts, outs = refs[:LINE], refs[LINE:]

    def store(value):
        for at in range(3):
            outs[at][0] = value[:, at * H : (at + 1) * H]

    @pl.when(pl.program_id(0) < PLAIN)
    def _():
        store(share_ref[0].astype(F32))

    @pl.when(pl.program_id(0) >= PLAIN)
    def _():
        total = parts[0][0].astype(F32)
        for ref in parts[1:]:
            total = total + ref[0].astype(F32)
        store(total)


def unpack(share, parts):
    block = (1, ROWS, 3 * H)
    return pl.pallas_call(
        unpack_kernel,
        grid=(LOCAL,),
        in_specs=[pl.BlockSpec(block, lambda e: (jnp.minimum(e, PLAIN - 1), 0, 0))]
        + [pl.BlockSpec(block, lambda e: (jnp.maximum(e - PLAIN, 0), 0, 0))] * LINE,
        out_specs=[per_expert(ROWS, H)] * 3,
        out_shape=[shape((LOCAL, ROWS, H), F32)] * 3,
        compiler_params=params(),
        cost_estimate=cost(LOCAL * ROWS * 3 * H, 5 << 20),
        name="unpack",
    )(share, *parts)


def spread_tables(all_routes, me):
    lane = jnp.arange(LANES, dtype=jnp.int32)
    member = jnp.sum((all_routes[..., None] == lane).astype(F32), axis=2)
    mine = me * LOCAL + jnp.arange(LOCAL, dtype=jnp.int32)
    own = jnp.sum((all_routes[..., None] == mine).astype(F32), axis=2)
    earlier = (np.arange(T)[:, None] > np.arange(T)[None, :]).astype(np.float32)
    before = jnp.einsum(
        "ts,rse->rte", jnp.asarray(earlier, BF16), own.astype(BF16), preferred_element_type=F32
    )
    slots = jnp.where(own > 0.5, before.astype(jnp.int32), -1)
    slots = jnp.swapaxes(slots, 1, 2)[:, :, None, :]
    place = slots == jnp.arange(CAP, dtype=jnp.int32)[None, None, :, None]
    return member, place.astype(BF16).reshape(PEERS, SLOTS, T)


def body(
    tokens,
    cotangent,
    routes,
    norm_one,
    w_query,
    key_weight,
    value_weight,
    w_out,
    norm_two,
    w_router,
    w_gate,
    w_up,
    w_down,
):
    me = lax.axis_index("expert")
    place_in_group = lax.axis_index("fsdp")
    z = me % Z
    core = place_in_group % 2
    cosine, signed = (jnp.asarray(table) for table in rope_tables())

    first, second = pack(
        z.astype(jnp.int32)[None],
        w_out,
        w_query,
        key_weight,
        value_weight,
        w_router.T,
        norm_one[None, :],
        norm_two[None, :],
    )
    def spread_over_chips(value):
        pair = jnp.stack([value, send_chip(value, LINE)])
        own = [send_chip(pair, hop) for hop in range(LINE)]
        return own, [swap_core(value) for value in own]

    own, other = spread_over_chips(first)
    out_own, _ = spread_over_chips(after(second, own[1]))
    sources = jnp.stack([chip_at(place_in_group, hop, True) for hop in range(CHIPS)])
    order = jnp.concatenate([2 * sources + core, 2 * sources + 1 - core]).astype(jnp.int32)
    dests = jnp.stack([chip_at(place_in_group, hop) for hop in range(CHIPS)]).astype(jnp.int32)
    twins = jnp.concatenate([2 * dests + core, 2 * dests + 1 - core])
    expert_pack = lax.all_gather(
        jnp.concatenate(after([w_gate, w_up, jnp.swapaxes(w_down, 1, 2)], first), axis=2),
        "fsdp",
        axis=1,
        tiled=True,
    )

    behind = jnp.stack([(z + Z - hop) % Z for hop in range(Z)]).astype(jnp.int32)
    ahead = jnp.stack([(z + hop) % Z for hop in range(Z)]).astype(jnp.int32)

    marks = jnp.pad(routes, ((0, 0), (0, LANES - TOPK))).astype(BF16)
    early = jnp.concatenate([cotangent, marks], axis=1)
    whole_row = jnp.concatenate([tokens, early], axis=1)
    whole_row = after(whole_row, first)
    xs = [send(whole_row, hop) for hop in (0, 1, 3)]
    xs.insert(2, send(whole_row, 2))
    w, gains, h1, qkv, ob = project(order, cosine, signed, own, other, xs)
    obs = [send(ob, hop) for hop in range(Z)]
    out_other = [swap_core(after(value, ob)) for value in out_own]
    early_other = send(after(early, xs[3]), Z)
    w_out_slice, ob_full, *x1_columns = out_project(behind, order, out_own, out_other, obs)
    x1_pieces = [send(x1_columns[hop], hop, True) for hop in range(Z)]
    early_other = after(early_other, x1_pieces[1])
    early_other = [send(early_other, hop) for hop in range(Z)]
    x1, h2 = residual(ahead, tokens, gains, x1_pieces)
    h2_other = send(h2, Z)
    h2_line = [send(h2, hop) for hop in range(Z)]
    h2_other = [send(h2_other, hop) for hop in range(Z)]

    all_routes = jnp.stack(
        [r[:, 2 * D : 2 * D + TOPK].astype(jnp.int32) for r in xs]
        + [r[:, D : D + TOPK].astype(jnp.int32) for r in early_other]
    )
    member, place = spread_tables(all_routes, me)
    row_expert = me * LOCAL + jnp.arange(SLOTS, dtype=jnp.int32) // CAP
    chosen = (row_expert[:, None] == jnp.arange(LANES, dtype=jnp.int32)[None, :]).astype(F32)
    dyr = spread_rows(after(place, h2_line[1]), xs, early_other)

    gates, gate0, b0 = gate_rows(0, w, member, chosen, place, h2_line)
    _, gate1, b1 = gate_rows(1, w, member, chosen, place, h2_other)
    b, slot_gate = (b0, b1), (gate0, gate1)
    weights = cut_out(ahead, after(w_out_slice, x1))
    slot_gate = after(slot_gate, *weights)
    number = me.astype(jnp.int32)[None]
    gy, db, grad_pack = experts(number, b, dyr, slot_gate, expert_pack)
    weights = after(weights, db)
    weights = [send(weights[hop], hop) for hop in range(Z)]
    extra_gy, extra_db, keep_extra, give_extra = extra_experts(
        after(number, db), b, dyr, slot_gate, twins, expert_pack
    )
    db_parts = collect(place, after((db, extra_db), *weights[1:]), "collect_grads")
    grad_cross = [send(db_parts[Z + hop], hop, True) for hop in range(Z)]
    grad_line = after(db_parts[:Z], *grad_cross[1:])
    grad_line = [send(grad_line[hop], hop, True) for hop in range(Z)]
    got_extra = swap_core(give_extra)
    grad_other = send(add_all(grad_cross, "line_grads"), Z)
    expert_share = lax.psum_scatter(grad_pack, "fsdp", scatter_dimension=1, tiled=True)
    results = collect(place, (gy, extra_gy), "collect_results")
    grad_line = after(grad_line, results)
    dx1, dlogits, scaled, da = token_back(x1, cotangent, gates, w, gains, [*grad_line, grad_other])
    das = [send(da, hop) for hop in range(Z)]
    extra_line, extra_cross = extra_halves(keep_extra, after(got_extra, da))
    shadows = shadow(after(qkv, extra_cross), h2, dlogits, scaled)
    results = after(results, shadows[1], *das[1:])
    results_cross = [send(results[Z + hop], hop, True) for hop in range(Z)]
    *returns, keep, give = head_back(
        behind,
        core.astype(jnp.int32)[None],
        qkv,
        h1,
        w,
        ob_full,
        shadows,
        cosine,
        signed,
        das,
        weights,
        results[:Z],
    )
    parts = split(dests, keep, swap_core(after(give, *results_cross[1:])))
    extra_got = send_chip(extra_cross, LINE)
    parts = after(parts, expert_share)
    lines = [send_chip(parts[hop], hop) for hop in range(LINE)]
    results_other = send(add_all(results_cross, "line_results"), Z)
    first, third = send(returns[1], 1, True), send(returns[3], 3, True)
    lines[0] = after(lines[0], first, third)
    second = send(after(returns[2], first, third), 2, True)
    returns = [returns[0], first, second, third]
    share = sum_lines(lines)
    extra_parts = extra_lines(extra_line, after(extra_got, share[1]))
    share = add_all([share[0], send_chip(share[1], LINE)], "sum_chips")
    share = add_all([share, send(share, Z)], "sum_halves")
    extra_first, extra_third = (send_chip(extra_parts[hop], hop) for hop in (1, 3))
    share = after(share, second)
    extra_second = send_chip(extra_parts[2], 2)
    extra_parts = [extra_parts[0], extra_first, extra_second, extra_third]
    shares = [send(share, hop) for hop in range(Z)]
    grad_gate, grad_up, grad_down = unpack(expert_share, extra_parts)
    grad_tokens = token_grad(tokens, gains, dx1, returns)
    mixed_out = mix(x1, returns, results_other)
    shares = after(shares, grad_tokens, mixed_out, grad_gate)
    grad_query, grad_key, grad_value, grad_out, router, one, two = finish(
        behind, shares, w_query, key_weight, value_weight, norm_one[None, :]
    )

    return (
        mixed_out,
        grad_tokens,
        one.reshape(ROWS),
        grad_query,
        grad_key,
        grad_value,
        grad_out,
        two.reshape(ROWS),
        router.T,
        grad_gate,
        grad_up,
        jnp.swapaxes(grad_down, 1, 2),
    )


def solution(mesh):
    return jax.shard_map(
        body,
        mesh=mesh,
        in_specs=(
            P(("expert", "fsdp"), None),
            P(("expert", "fsdp"), None),
            P(("expert", "fsdp"), None),
            P("fsdp"),
            P("fsdp", None),
            P("fsdp", None),
            P("fsdp", None),
            P("fsdp", None),
            P("fsdp"),
            P("fsdp", None),
            P("expert", "fsdp", None),
            P("expert", "fsdp", None),
            P("expert", None, "fsdp"),
        ),
        out_specs=(
            P(("expert", "fsdp"), None),
            P(("expert", "fsdp"), None),
            P("fsdp"),
            P("fsdp", None),
            P("fsdp", None),
            P("fsdp", None),
            P("fsdp", None),
            P("fsdp"),
            P("fsdp", None),
            P("expert", "fsdp", None),
            P("expert", "fsdp", None),
            P("expert", None, "fsdp"),
        ),
        check_vma=False,
    )
```

```python
import jax
import jax.numpy as jnp
import numpy as np
from jax import lax
from jax.experimental import pallas as pl
from jax.experimental.pallas import tpu as pltpu
from jax.sharding import PartitionSpec as P

QUERY_HEADS = 24
KEY_VALUE_HEADS = 8
GROUP = QUERY_HEADS // KEY_VALUE_HEADS
HEAD_DIM = 64
HALF = HEAD_DIM // 2
E = 40
H = 512
D = 1536
T = 128
CAP = 32
NORM_EPSILON = 1e-05
SCALE = HEAD_DIM ** (-0.5)

Z = 4
PEERS = 8
LOCAL = E // PEERS
SLOTS = LOCAL * CAP
EXTRA = 1
PLAIN = LOCAL - EXTRA
LANES = 128
CHIPS = 8
LINE = 4
TOPK = 8
SHARDS = 2 * CHIPS
ROWS = D // SHARDS
QH = QUERY_HEADS // Z
KH = KEY_VALUE_HEADS // Z
QW = QH * HEAD_DIM
KW = KH * HEAD_DIM
QKV = QW + 2 * KW
MAIN = QW + QKV
SLICE = MAIN + LANES
VMEM_LIMIT = 60 * 1024 * 1024

F32 = jnp.float32
BF16 = jnp.bfloat16


def peer(index, hop, back=False):
    shift = hop % Z
    turned = (index % Z + (Z - shift if back else shift)) % Z
    return (index // Z + hop // Z) % 2 * Z + turned


def send(value, hop, back=False):
    if hop == 0:
        return value
    return lax.ppermute(value, "expert", [(i, peer(i, hop, back)) for i in range(PEERS)])


def chip_at(index, hop, back=False):
    shift = hop % 4
    turned = (index // 2 % 4 + (4 - shift if back else shift)) % 4
    return (index // 8 + hop // 4) % 2 * 4 + turned


def send_chip(value, hop):
    if hop == 0:
        return value
    pairs = [(i, 2 * chip_at(i, hop) + i % 2) for i in range(SHARDS)]
    return lax.ppermute(value, "fsdp", pairs)


def after(value, *others):
    return lax.optimization_barrier((value, others))[0]


def swap_core(value):
    return lax.ppermute(value, "fsdp", [(i, i ^ 1) for i in range(SHARDS)])


def mm(left, right):
    return jnp.dot(left, right, preferred_element_type=F32)


def mm_nt(left, right):
    return lax.dot_general(left, right, (((1,), (1,)), ((), ())), preferred_element_type=F32)


def mm_tn(left, right):
    return lax.dot_general(left, right, (((0,), (0,)), ((), ())), preferred_element_type=F32)


def rope_tables():
    frequency = np.exp(-np.log(10000.0) * np.arange(HALF, dtype=np.float64) * 2.0 / HEAD_DIM)
    angles = np.arange(T, dtype=np.float64)[:, None] * frequency[None, :]
    cosine = np.tile(np.cos(angles), (1, 4)).astype(np.float32)
    sine = np.sin(angles)
    signed = np.tile(np.concatenate([-sine, sine], axis=1), (1, 2)).astype(np.float32)
    return cosine, signed


def swap_halves(values):
    width = values.shape[1]
    lane = lax.broadcasted_iota(jnp.int32, values.shape, 1)
    up = pltpu.roll(values, width - HALF, 1)
    down = pltpu.roll(values, HALF, 1)
    return jnp.where(lane % HEAD_DIM < HALF, up, down)


def wide(table, width):
    return jnp.concatenate([table] * (width // LANES), axis=1)


def rotate(values, cosine, signed):
    width = values.shape[1]
    return values * wide(cosine, width) + swap_halves(values) * wide(signed, width)


def rotate_back(values, cosine, signed):
    width = values.shape[1]
    return values * wide(cosine, width) + swap_halves(values * wide(signed, width))


def gain_rows(small):
    pick = lax.broadcasted_iota(jnp.int32, (16, LANES), 1) == (
        lax.broadcasted_iota(jnp.int32, (16, LANES), 0) + E
    )
    return mm_nt(pick.astype(BF16), small)


def norm_of(values):
    inverse = lax.rsqrt(jnp.mean(values * values, axis=-1, keepdims=True) + NORM_EPSILON)
    return values * inverse, inverse


def head(ref, rows, index):
    return ref[rows, index * HEAD_DIM : (index + 1) * HEAD_DIM]


def stack_heads(ref, rows, first):
    return jnp.concatenate([head(ref, rows, first + index) for index in range(GROUP)], axis=0)


def probabilities(query, key):
    scores = mm_nt(query, key) * SCALE
    rows = lax.broadcasted_iota(jnp.int32, scores.shape, 0) % T
    cols = lax.broadcasted_iota(jnp.int32, scores.shape, 1)
    scores = jnp.where(rows >= cols, scores, -jnp.inf)
    exponent = jnp.exp(scores - jnp.max(scores, axis=-1, keepdims=True))
    return exponent / jnp.sum(exponent, axis=-1, keepdims=True)


def whole(shape):
    return pl.BlockSpec(shape, lambda *_: (0,) * len(shape))


SCALARS = pl.BlockSpec(memory_space=pltpu.SMEM)
ANYWHERE = pl.BlockSpec(memory_space=pl.ANY)


def params(**more):
    return pltpu.CompilerParams(vmem_limit_bytes=VMEM_LIMIT, **more)


WEIGHT = 60


def cost(flops, moved):
    return pl.CostEstimate(flops=flops * WEIGHT, bytes_accessed=moved * WEIGHT, transcendentals=0)


def shape(dims, kind):
    return jax.ShapeDtypeStruct(dims, kind)


def call(kernel, name, inputs, in_specs, outputs, out_specs=None, scratch=(), flops=0, moved=0):
    in_specs = [whole(v.shape) if spec is None else spec for v, spec in zip(inputs, in_specs)]
    if out_specs is None:
        out_specs = [whole(o.shape) for o in outputs]
    return pl.pallas_call(
        kernel,
        grid=(1,),
        in_specs=in_specs,
        out_specs=out_specs,
        out_shape=outputs,
        scratch_shapes=list(scratch),
        compiler_params=params(),
        cost_estimate=cost(flops, moved),
        name=name,
    )(*inputs)


SMALL_SPEC = pl.BlockSpec((SHARDS, ROWS, LANES), lambda *_: (0, 0, QKV // LANES))
X_SPEC = pl.BlockSpec((T, D), lambda *_: (0, 0))
DY_SPEC = pl.BlockSpec((T, D), lambda *_: (0, 1))


def small_of(ref):
    return ref[...].reshape(D, LANES)


def columns_of(index):
    return pl.ds(pl.multiple_of(index * QW, QW), QW)


def pack_kernel(
    z_ref, out_ref, query_ref, key_ref, value_ref, router_ref, one_ref, two_ref, first_ref, second_ref
):
    first_ref[:, 0:QW] = query_ref[...]
    first_ref[:, QW : QW + KW] = key_ref[...]
    first_ref[:, QW + KW : QKV] = value_ref[...]
    narrow = [router_ref[...], one_ref[...], two_ref[...], jnp.zeros((LANES - E - 2, ROWS), BF16)]
    first_ref[:, QKV:] = jnp.concatenate([v.astype(F32) for v in narrow], axis=0).T.astype(BF16)
    second_ref[...] = out_ref[...]


def pack(z, w_out, w_query, key_weight, value_weight, router, one, two):
    def slice_of(width):
        return pl.BlockSpec((ROWS, width), lambda i, z: (0, z[0]))

    return pl.pallas_call(
        pack_kernel,
        grid_spec=pltpu.PrefetchScalarGridSpec(
            num_scalar_prefetch=1,
            grid=(1,),
            in_specs=[
                slice_of(QW),
                slice_of(QW),
                slice_of(KW),
                slice_of(KW),
                whole((E, ROWS)),
                whole((1, ROWS)),
                whole((1, ROWS)),
            ],
            out_specs=[whole((ROWS, QKV + LANES)), whole((ROWS, QW))],
        ),
        out_shape=[shape((ROWS, QKV + LANES), BF16), shape((ROWS, QW), BF16)],
        compiler_params=params(),
        cost_estimate=cost(ROWS * SLICE, 1 << 20),
        name="pack",
    )(z, w_out, w_query, key_weight, value_weight, router, one, two)


def project_kernel(order_ref, cos_ref, sin_ref, *refs):
    own, other, xs = refs[:LINE], refs[LINE : 2 * LINE], refs[2 * LINE : 2 * LINE + Z]
    w_ref, gains_ref, h1_ref, qkv_ref, ob_ref = refs[2 * LINE + Z :]
    for chip in range(CHIPS):
        w_ref[order_ref[chip]] = own[chip % LINE][chip // LINE]
        w_ref[order_ref[CHIPS + chip]] = other[chip % LINE][chip // LINE]
    gains = gain_rows(w_ref[:, :, QKV:].reshape(D, LANES))
    gains_ref[...] = gains
    for hop in range(Z):
        normed, _ = norm_of(xs[hop][...].astype(F32))
        h1_ref[hop * T : (hop + 1) * T] = (normed * gains[0:1, :]).astype(BF16)
    pre = mm(h1_ref[...], w_ref[:, :, 0:QKV].reshape(D, QKV))
    cosine = jnp.concatenate([cos_ref[...]] * Z, axis=0)
    signed = jnp.concatenate([sin_ref[...]] * Z, axis=0)
    qkv_ref[:, 0:QW] = rotate(pre[:, 0:QW], cosine, signed).astype(BF16)
    qkv_ref[:, QW : QW + KW] = rotate(pre[:, QW : QW + KW], cosine, signed).astype(BF16)
    qkv_ref[:, QW + KW :] = pre[:, QW + KW :].astype(BF16)
    for hop in range(Z):
        rows = slice(hop * T, (hop + 1) * T)
        for group in range(KH):
            key, value = head(qkv_ref, rows, QH + group), head(qkv_ref, rows, QH + KH + group)
            query = stack_heads(qkv_ref, rows, group * GROUP)
            result = mm(probabilities(query, key).astype(BF16), value).astype(BF16)
            for index in range(GROUP):
                at = (group * GROUP + index) * HEAD_DIM
                ob_ref[rows, at : at + HEAD_DIM] = result[index * T : (index + 1) * T]


def project(order, cosine, signed, own, other, xs):
    return call(
        project_kernel,
        "project",
        [order, cosine, signed, *own, *other, *xs],
        [SCALARS] + [None] * (2 + 2 * LINE) + [X_SPEC] * Z,
        [
            shape((SHARDS, ROWS, QKV + LANES), BF16),
            shape((16, D), F32),
            shape((Z * T, D), BF16),
            shape((Z * T, QKV), BF16),
            shape((Z * T, QW), BF16),
        ],
        flops=2 * Z * T * D * QKV,
        moved=12 << 20,
    )


def out_project_kernel(peers_ref, order_ref, *refs):
    own, other, obs = refs[:LINE], refs[LINE : 2 * LINE], refs[2 * LINE : 2 * LINE + Z]
    w_ref, full_ref, *outs = refs[2 * LINE + Z :]
    for chip in range(CHIPS):
        w_ref[order_ref[chip]] = own[chip % LINE][chip // LINE]
        w_ref[order_ref[CHIPS + chip]] = other[chip % LINE][chip // LINE]
    total = jnp.zeros((Z * T, QW), F32)
    for hop in range(Z):
        peer_index = peers_ref[hop]
        blocks = [(row - hop) % Z for row in range(Z)]
        rows = jnp.concatenate([obs[hop][b * T : (b + 1) * T, :] for b in blocks], axis=0)
        full_ref[:, columns_of(peer_index)] = rows
        weight = w_ref[pl.ds(peer_index * Z, Z)].reshape(QW, QW)
        total = total + mm(rows, weight)
    for hop in range(Z):
        outs[hop][...] = total[hop * T : (hop + 1) * T].astype(BF16)


def out_project(peers, order, own, other, obs):
    return call(
        out_project_kernel,
        "out_project",
        [peers, order, *own, *other, *obs],
        [SCALARS] * 2 + [None] * (2 * LINE + Z),
        [shape((SHARDS, ROWS, QW), BF16), shape((Z * T, D), BF16)] + [shape((T, QW), BF16)] * Z,
        flops=2 * Z * T * D * QW,
        moved=6 << 20,
    )


def cut_out_kernel(peers_ref, w_ref, *outs):
    for hop in range(Z):
        outs[hop][...] = w_ref[pl.ds(peers_ref[hop] * Z, Z)].reshape(QW, QW)


def cut_out(peers, w):
    return call(
        cut_out_kernel,
        "cut_out",
        [peers, w],
        [SCALARS, None],
        [shape((QW, QW), BF16)] * Z,
        flops=D * QW,
        moved=2 << 20,
    )


def residual_kernel(peers_ref, x_ref, gains_ref, *refs):
    pieces, (x1_ref, h2_ref) = refs[:Z], refs[Z:]
    x1_ref[...] = x_ref[...].astype(F32)
    for hop in range(Z):
        x1_ref[:, columns_of(peers_ref[hop])] += pieces[hop][...].astype(F32)
    normed, _ = norm_of(x1_ref[...])
    h2_ref[...] = (normed * gains_ref[1:2, :]).astype(BF16)


def residual(peers, x, gains, pieces):
    return call(
        residual_kernel,
        "residual",
        [peers, x, gains, *pieces],
        [SCALARS] + [None] * (2 + Z),
        [shape((T, D), F32), shape((T, D), BF16)],
        flops=T * D * 8,
        moved=2 << 20,
    )


def gate_kernel(small_ref, member_ref, chosen_ref, place_ref, *refs):
    rows, (gates_ref, slot_gate_ref, b_ref) = refs[:Z], refs[Z:]
    small = small_of(small_ref)
    for hop in range(Z):
        h2 = rows[hop][...]
        member = member_ref[hop] > 0.5
        logits = jnp.where(member, mm(h2, small), -jnp.inf)
        exponent = jnp.exp(logits - jnp.max(logits, axis=-1, keepdims=True))
        gates = exponent / jnp.sum(exponent, axis=-1, keepdims=True)
        gates_ref[hop] = gates
        high = gates.astype(BF16)
        low = (gates - high.astype(F32)).astype(BF16)
        place = place_ref[hop]
        spread = mm(place, high) + mm(place, low)
        picked = jnp.sum(spread * chosen_ref[...], axis=-1, keepdims=True)
        slot_gate_ref[:, hop] = picked.reshape(LOCAL, CAP, 1)
        b_ref[:, hop] = mm(place, h2).astype(BF16).reshape(LOCAL, CAP, D)


def gate_rows(half, w, member, chosen, place, rows):
    gates, slot_gate, b = call(
        gate_kernel,
        "gate_rows",
        [w, member, chosen, place, *rows],
        [
            SMALL_SPEC,
            pl.BlockSpec((Z, T, LANES), lambda *_: (half, 0, 0)),
            None,
            pl.BlockSpec((Z, SLOTS, T), lambda *_: (half, 0, 0)),
        ]
        + [None] * Z,
        [
            shape((Z, T, LANES), F32),
            shape((LOCAL, Z, CAP, 1), F32),
            shape((LOCAL, Z, CAP, D), BF16),
        ],
        flops=2 * Z * SLOTS * T * D,
        moved=5 << 20,
    )
    return gates, slot_gate.reshape(LOCAL, Z * CAP, 1), b.reshape(LOCAL, Z * CAP, D)


def spread_kernel(place_ref, *refs):
    rows, out_ref = refs[:PEERS], refs[PEERS]
    for hop in range(PEERS):
        out_ref[:, hop] = mm(place_ref[hop], rows[hop][...]).astype(BF16).reshape(LOCAL, CAP, D)


def spread_rows(place, line, other):
    return call(
        spread_kernel,
        "spread_rows",
        [place, *line, *other],
        [None] + [DY_SPEC] * Z + [X_SPEC] * Z,
        [shape((LOCAL, PEERS, CAP, D), BF16)],
        flops=2 * PEERS * SLOTS * T * D,
        moved=8 << 20,
    )[0].reshape(LOCAL, PEERS * CAP, D)


def expert_step(expert, b_refs, dyr_ref, gate_refs, first, down, gy_ref, db_ref):
    rows = jnp.concatenate([ref[0] for ref in b_refs], axis=0)
    gate = jnp.concatenate([ref[0] for ref in gate_refs], axis=0)
    pre = mm(rows, first())
    gate_pre, up_pre = pre[:, :H], pre[:, H:]
    sigmoid = 1.0 / (1.0 + jnp.exp(-gate_pre))
    silu = gate_pre * sigmoid
    activated = (silu * up_pre).astype(BF16)
    result = mm_nt(activated, down()).astype(BF16).astype(F32)
    raw = dyr_ref[0].astype(F32)
    gy_ref[0] = (gate * result).astype(BF16)
    inner = jnp.sum(raw * result, axis=-1, keepdims=True)
    grad_rows = (gate * raw).astype(BF16)
    grad_act = mm(grad_rows, down())
    grad_gate = (grad_act * up_pre * sigmoid * (1.0 + gate_pre * (1.0 - sigmoid))).astype(BF16)
    grad_up = (grad_act * silu).astype(BF16)
    both = jnp.concatenate([grad_gate, grad_up], axis=1)
    db_ref[0, :, 0:D] = mm_nt(both, first()).astype(BF16)
    lane = lax.broadcasted_iota(jnp.int32, (PEERS * CAP, LANES), 1)
    high = inner.astype(BF16).astype(F32)
    low = inner - high
    tail = jnp.where(lane == expert, high, jnp.where(lane == expert + E, low, 0.0))
    db_ref[0, :, D : D + LANES] = tail.astype(BF16)
    return rows, both, grad_rows, activated


def expert_kernel(
    me_ref, b0_ref, b1_ref, dyr_ref, gate0_ref, gate1_ref, w_ref, gy_ref, db_ref, grad_ref
):
    rows, both, grad_rows, activated = expert_step(
        me_ref[0] * LOCAL + pl.program_id(0),
        (b0_ref, b1_ref),
        dyr_ref,
        (gate0_ref, gate1_ref),
        lambda: w_ref[0, :, 0 : 2 * H],
        lambda: w_ref[0, :, 2 * H : 3 * H],
        gy_ref,
        db_ref,
    )
    grad_ref[0, :, 0 : 2 * H] = mm_tn(rows, both).astype(BF16)
    grad_ref[0, :, 2 * H : 3 * H] = mm_tn(grad_rows, activated).astype(BF16)


def per_expert(*dims, first=0):
    return pl.BlockSpec((1,) + dims, lambda e: (e + first, 0, 0))


def row_specs(first):
    half = PEERS * CAP // 2
    return [
        SCALARS,
        per_expert(half, D, first=first),
        per_expert(half, D, first=first),
        per_expert(2 * half, D, first=first),
        per_expert(half, 1, first=first),
        per_expert(half, 1, first=first),
    ]


def experts(me, b, dyr, slot_gate, pack):
    rows = PEERS * CAP
    return pl.pallas_call(
        expert_kernel,
        grid=(PLAIN,),
        in_specs=row_specs(0) + [per_expert(D, 3 * H)],
        out_specs=[per_expert(rows, D), per_expert(rows, D + LANES), per_expert(D, 3 * H)],
        out_shape=[
            shape((PLAIN, rows, D), BF16),
            shape((PLAIN, rows, D + LANES), BF16),
            shape((PLAIN, D, 3 * H), BF16),
        ],
        compiler_params=params(),
        cost_estimate=cost(18 * PLAIN * rows * D * H, 12 * PLAIN << 20),
        name="experts",
    )(me, *b, dyr, *slot_gate, pack)


def extra_kernel(
    me_ref,
    b0_ref,
    b1_ref,
    dyr_ref,
    gate0_ref,
    gate1_ref,
    dests_ref,
    w_ref,
    gy_ref,
    db_ref,
    keep_ref,
    give_ref,
    grads,
):
    rows, both, grad_rows, activated = expert_step(
        me_ref[0] * LOCAL + PLAIN + pl.program_id(0),
        (b0_ref, b1_ref),
        dyr_ref,
        (gate0_ref, gate1_ref),
        lambda: w_ref[0, :, 0 : 2 * H],
        lambda: w_ref[0, :, 2 * H : 3 * H],
        gy_ref,
        db_ref,
    )
    grads[:, :, 0 : 2 * H] = mm_tn(rows, both).astype(BF16).reshape(SHARDS, ROWS, 2 * H)
    grads[:, :, 2 * H : 3 * H] = mm_tn(grad_rows, activated).astype(BF16).reshape(SHARDS, ROWS, H)
    for chip in range(CHIPS):
        keep_ref[chip, 0] = grads[dests_ref[chip]]
        give_ref[chip, 0] = grads[dests_ref[CHIPS + chip]]


def extra_experts(me, b, dyr, slot_gate, dests, pack):
    rows = PEERS * CAP
    blocks = pl.BlockSpec((CHIPS, 1, ROWS, 3 * H), lambda e: (0, e, 0, 0))
    return pl.pallas_call(
        extra_kernel,
        grid=(EXTRA,),
        in_specs=row_specs(PLAIN) + [SCALARS, per_expert(D, 3 * H, first=PLAIN)],
        out_specs=[per_expert(rows, D), per_expert(rows, D + LANES), blocks, blocks],
        out_shape=[
            shape((EXTRA, rows, D), BF16),
            shape((EXTRA, rows, D + LANES), BF16),
            shape((CHIPS, EXTRA, ROWS, 3 * H), BF16),
            shape((CHIPS, EXTRA, ROWS, 3 * H), BF16),
        ],
        scratch_shapes=[pltpu.VMEM((SHARDS, ROWS, 3 * H), BF16)],
        compiler_params=params(),
        cost_estimate=cost(18 * EXTRA * rows * D * H, 14 * EXTRA << 20),
        name="extra_experts",
    )(me, *b, dyr, *slot_gate, dests, pack)


def extra_halves_kernel(keep_ref, got_ref, line_ref, cross_ref):
    total = (keep_ref[0].astype(F32) + got_ref[0].astype(F32)).astype(BF16)

    @pl.when(pl.program_id(0) < LINE)
    def _():
        cross_ref[0] = total

    @pl.when(pl.program_id(0) >= LINE)
    def _():
        line_ref[0] = total


def extra_halves(keep, got):
    block = (1, EXTRA, ROWS, 3 * H)
    return pl.pallas_call(
        extra_halves_kernel,
        grid=(CHIPS,),
        in_specs=[pl.BlockSpec(block, lambda i: ((i + LINE) % CHIPS, 0, 0, 0))] * 2,
        out_specs=[
            pl.BlockSpec(block, lambda i: (jnp.maximum(i - LINE, 0), 0, 0, 0)),
            pl.BlockSpec(block, lambda i: (jnp.minimum(i, LINE - 1), 0, 0, 0)),
        ],
        out_shape=[shape((LINE, EXTRA, ROWS, 3 * H), BF16)] * 2,
        compiler_params=params(),
        cost_estimate=cost(keep.size, 6 * keep.size),
        name="extra_halves",
    )(keep, got)


def extra_lines_kernel(line_ref, got_ref, *outs):
    for hop in range(LINE):
        outs[hop][...] = (line_ref[hop].astype(F32) + got_ref[hop].astype(F32)).astype(BF16)


def extra_lines(line, got):
    return call(
        extra_lines_kernel,
        "extra_lines",
        [line, got],
        [None, None],
        [shape((EXTRA, ROWS, 3 * H), BF16)] * LINE,
        flops=line.size,
        moved=6 * line.size,
    )


def collect_kernel(place_ref, plain_ref, extra_ref, *out_refs):
    for hop in range(PEERS):
        rows = jnp.concatenate(
            [ref[:, hop].reshape(-1, ref.shape[-1]) for ref in (plain_ref, extra_ref)], axis=0
        )
        out_refs[hop][...] = mm_tn(place_ref[hop], rows).astype(BF16)


def collect(place, values, name):
    width = values[0].shape[-1]
    return call(
        collect_kernel,
        name,
        [place, *(v.reshape(-1, PEERS, CAP, width) for v in values)],
        [None] * 3,
        [shape((T, width), BF16)] * PEERS,
        flops=2 * PEERS * SLOTS * T * width,
        moved=8 << 20,
    )


def mix(x1, returns, other):
    return call(
        add_kernel,
        "mix",
        [x1, *returns, other],
        [None] + [DY_SPEC] * Z + [None],
        [shape((T, D), BF16)],
        flops=T * D * Z,
        moved=4 << 20,
    )[0]


def norm_back(grad, normed, inverse, gain):
    scaled = grad * gain
    return inverse * (scaled - normed * jnp.mean(scaled * normed, axis=-1, keepdims=True))


def token_back_kernel(
    x1_ref, dy_ref, gates_ref, small_ref, gains_ref, *refs
):
    parts, (dx1_ref, dlogits_ref, scaled_ref, da_ref) = refs[: Z + 1], refs[Z + 1 :]
    total = parts[0][...].astype(F32)
    for ref in parts[1:]:
        total = total + ref[...].astype(F32)
    grad, tail = total[:, :D], total[:, D:]
    lane = lax.broadcasted_iota(jnp.int32, (T, LANES), 1)
    inner = jnp.where(lane < E, tail + pltpu.roll(tail, LANES - E, 1), 0.0)
    gates = gates_ref[0]
    score = gates * (inner - jnp.sum(gates * inner, axis=-1, keepdims=True))
    dlogits_ref[...] = score.astype(BF16)
    grad = grad + mm_nt(dlogits_ref[...], small_of(small_ref))
    normed, inverse = norm_of(x1_ref[...])
    scaled_ref[...] = (grad * normed).astype(BF16)
    through = dy_ref[...].astype(F32) + norm_back(grad, normed, inverse, gains_ref[1:2, :])
    dx1_ref[...] = through
    da_ref[...] = through.astype(BF16)


def token_back(x1, dy, gates, w, gains, parts):
    return call(
        token_back_kernel,
        "token_back",
        [x1, dy, gates, w, gains, *parts],
        [None, None, pl.BlockSpec((1, T, LANES), lambda *_: (0, 0, 0)), SMALL_SPEC]
        + [None] * (1 + len(parts)),
        [
            shape((T, D), F32),
            shape((T, LANES), BF16),
            shape((T, D), BF16),
            shape((T, D), BF16),
        ],
        flops=T * D * 64,
        moved=6 << 20,
    )


def shadow_kernel(qkv_ref, h2_ref, dlogits_ref, scaled_ref, small_ref, prob_ref):
    lane = lax.broadcasted_iota(jnp.int32, (T, LANES), 1)
    small = mm_tn(h2_ref[...], dlogits_ref[...])
    small_ref[...] = small + mm_tn(scaled_ref[...], (lane == E + 1).astype(BF16))
    for hop in range(Z):
        rows = slice(hop * T, (hop + 1) * T)
        for group in range(KH):
            query = stack_heads(qkv_ref, rows, group * GROUP)
            prob_ref[hop * KH + group] = probabilities(query, head(qkv_ref, rows, QH + group))


def shadow(qkv, h2, dlogits, scaled):
    return call(
        shadow_kernel,
        "shadow",
        [qkv, h2, dlogits, scaled],
        [None] * 4,
        [shape((D, LANES), F32), shape((Z * KH, GROUP * T, T), F32)],
        flops=Z * T * D * QW,
        moved=6 << 20,
    )


def head_back_kernel(
    behind_ref,
    parity_ref,
    qkv_ref,
    h1_ref,
    w_ref,
    full_ref,
    partial_ref,
    prob_ref,
    cos_ref,
    sin_ref,
    *refs,
):
    das, weights, results, outs = (refs[at * Z : at * Z + Z] for at in range(4))
    keep_ref, give_ref, dob, dqk, dqkv, h1, w, full, sems = refs[4 * Z :]
    late = [(h1_ref, h1), (w_ref, w), (full_ref, full)]
    late += [(results[hop], outs[hop].at[:, pl.ds(D, D)]) for hop in range(Z)]
    late = [pltpu.make_async_copy(a, b, sems.at[at]) for at, (a, b) in enumerate(late)]
    for copy in late:
        copy.start()
    total = jnp.zeros((Z * T, QW), F32)
    for hop in range(Z):
        columns = columns_of(behind_ref[hop])
        rows = jnp.concatenate([ref[:, columns] for ref in das], axis=0)
        total = total + mm_nt(rows, weights[hop][...])
        if hop == 0:
            own_columns = rows
    dob[...] = total.astype(BF16)
    for hop in range(Z):
        rows = slice(hop * T, (hop + 1) * T)
        for group in range(KH):
            key, value = head(qkv_ref, rows, QH + group), head(qkv_ref, rows, QH + KH + group)
            query = stack_heads(qkv_ref, rows, group * GROUP)
            out_grad = stack_heads(dob, rows, group * GROUP)
            probability = prob_ref[hop * KH + group]
            grad_prob = mm_nt(out_grad, value)
            held = jnp.sum(probability * grad_prob, axis=-1, keepdims=True)
            grad_scores = (probability * (grad_prob - held)).astype(BF16)
            grad_query = mm(grad_scores, key) * SCALE
            for index in range(GROUP):
                at = (group * GROUP + index) * HEAD_DIM
                dqk[rows, at : at + HEAD_DIM] = grad_query[index * T : (index + 1) * T]
            at = QW + group * HEAD_DIM
            dqk[rows, at : at + HEAD_DIM] = mm_tn(grad_scores, query) * SCALE
            dqkv[rows, at + KW : at + KW + HEAD_DIM] = mm_tn(
                probability.astype(BF16), out_grad
            ).astype(BF16)
    cosine = jnp.concatenate([cos_ref[...]] * Z, axis=0)
    signed = jnp.concatenate([sin_ref[...]] * Z, axis=0)
    dqkv[:, 0 : QW + KW] = rotate_back(dqk[...], cosine, signed).astype(BF16)
    even = parity_ref[0] == 0

    def store(grads, columns):
        pair = grads.astype(BF16).reshape(CHIPS, 2, ROWS, grads.shape[1])
        keep_ref[:, :, columns] = jnp.where(even, pair[:, 0], pair[:, 1])
        give_ref[:, :, columns] = jnp.where(even, pair[:, 1], pair[:, 0])

    late[2].wait()
    store(mm_tn(full[...], own_columns), slice(0, QW))
    late[0].wait()
    store(mm_tn(h1[...], dqkv[...]), slice(QW, MAIN))
    late[1].wait()
    dh1 = mm_nt(dqkv[...], w[:, :, 0:QKV].reshape(D, QKV))
    for hop in range(Z):
        outs[hop][:, 0:D] = dh1[hop * T : (hop + 1) * T].astype(BF16)
        late[3 + hop].wait()
    store(partial_ref[...], slice(MAIN, SLICE))


def head_back(behind, parity, qkv, h1, w, full, shadows, cosine, signed, das, weights, results):
    return call(
        head_back_kernel,
        "head_back",
        [behind, parity, qkv, h1, w, full, *shadows, cosine, signed, *das, *weights, *results],
        [SCALARS] * 2
        + [None, ANYWHERE, ANYWHERE, ANYWHERE]
        + [None] * (4 + 2 * Z)
        + [ANYWHERE] * Z,
        [shape((T, 2 * D), BF16)] * Z + [shape((CHIPS, ROWS, SLICE), BF16)] * 2,
        scratch=[
            pltpu.VMEM((Z * T, QW), BF16),
            pltpu.VMEM((Z * T, QW + KW), F32),
            pltpu.VMEM((Z * T, QKV), BF16),
            pltpu.VMEM((Z * T, D), BF16),
            pltpu.VMEM((SHARDS, ROWS, QKV + LANES), BF16),
            pltpu.VMEM((Z * T, D), BF16),
            pltpu.SemaphoreType.DMA((3 + Z,)),
        ],
        flops=4 * Z * T * D * QKV,
        moved=16 << 20,
    )


def token_grad_kernel(x_ref, gains_ref, dx1_ref, *refs):
    grad = refs[0][...].astype(F32)
    for hop in range(1, Z):
        grad = grad + refs[hop][...].astype(F32)
    normed, inverse = norm_of(x_ref[...].astype(F32))
    refs[Z][...] = dx1_ref[...] + norm_back(grad, normed, inverse, gains_ref[0:1, :])


def token_grad(x, gains, dx1, pieces):
    return call(
        token_grad_kernel,
        "token_grad",
        [x, gains, dx1, *pieces],
        [None] * 3 + [X_SPEC] * Z,
        [shape((T, D), F32)],
        flops=T * D * 16,
        moved=4 << 20,
    )[0]


def split_kernel(order_ref, keep_ref, got_ref, *outs):
    for chip in range(CHIPS):
        at = order_ref[chip]
        total = (keep_ref[at].astype(F32) + got_ref[at].astype(F32)).astype(BF16)
        outs[chip % 4][chip // 4] = total


def split(order, keep, got):
    return call(
        split_kernel,
        "split",
        [order, keep, got],
        [SCALARS, None, None],
        [shape((2, ROWS, SLICE), BF16)] * 4,
        flops=CHIPS * ROWS * SLICE,
        moved=6 << 20,
    )


def add_kernel(*refs):
    total = refs[0][...].astype(F32)
    for ref in refs[1:-1]:
        total = total + ref[...].astype(F32)
    refs[-1][...] = total.astype(BF16)


def sum_lines_kernel(*refs):
    for at in range(2):
        total = refs[0][at].astype(F32)
        for ref in refs[1:LINE]:
            total = total + ref[at].astype(F32)
        refs[LINE + at][...] = total.astype(BF16)


def sum_lines(parts):
    return call(
        sum_lines_kernel,
        "sum_lines",
        list(parts),
        [None] * LINE,
        [shape((ROWS, SLICE), BF16)] * 2,
        flops=LINE * ROWS * SLICE,
        moved=12 * ROWS * SLICE,
    )


def add_all(parts, name):
    return call(
        add_kernel,
        name,
        list(parts),
        [None] * len(parts),
        [shape(parts[0].shape, BF16)],
        flops=parts[0].size * len(parts),
        moved=2 * parts[0].size * (len(parts) + 1),
    )[0]


def finish_kernel(order_ref, *refs):
    parts, (wq_ref, wk_ref, wv_ref, gain_ref) = refs[:Z], refs[Z : Z + 4]
    q_ref, k_ref, v_ref, o_ref, router_ref, one_ref, two_ref, narrow = refs[Z + 4 :]
    for hop in range(Z):
        at = order_ref[hop]
        part = parts[hop][...].astype(F32)
        o_ref[:, columns_of(at)] = part[:, 0:QW]
        q_ref[:, columns_of(at)] = part[:, QW : 2 * QW]
        heads = pl.ds(pl.multiple_of(at * KW, KW), KW)
        k_ref[:, heads] = part[:, 2 * QW : 2 * QW + KW]
        v_ref[:, heads] = part[:, 2 * QW + KW : MAIN]
        narrow[at] = part[:, MAIN:]
    scaled = jnp.zeros((ROWS, 1), F32)
    for weight, grad in ((wq_ref, q_ref), (wk_ref, k_ref), (wv_ref, v_ref)):
        scaled += jnp.sum(weight[...].astype(F32) * grad[...], axis=-1, keepdims=True)
    small = narrow[0] + narrow[1] + narrow[2] + narrow[3]
    lane = lax.broadcasted_iota(jnp.int32, small.shape, 1)
    small = jnp.where(lane == E, scaled, small).T
    router_ref[...] = small[0:E]
    one_ref[...] = small[E : E + 1] / gain_ref[...].astype(F32)
    two_ref[...] = small[E + 1 : E + 2]


def finish(order, parts, w_query, key_weight, value_weight, gain):
    return call(
        finish_kernel,
        "finish",
        [order, *parts, w_query, key_weight, value_weight, gain],
        [SCALARS] + [None] * (Z + 4),
        [
            shape((ROWS, D), F32),
            shape((ROWS, KEY_VALUE_HEADS * HEAD_DIM), F32),
            shape((ROWS, KEY_VALUE_HEADS * HEAD_DIM), F32),
            shape((ROWS, D), F32),
            shape((E, ROWS), F32),
            shape((1, ROWS), F32),
            shape((1, ROWS), F32),
        ],
        scratch=[pltpu.VMEM((Z, ROWS, LANES), F32)],
        flops=ROWS * SLICE * Z,
        moved=3 << 20,
    )


def unpack_kernel(share_ref, *refs):
    parts, outs = refs[:LINE], refs[LINE:]

    def store(value):
        for at in range(3):
            outs[at][0] = value[:, at * H : (at + 1) * H]

    @pl.when(pl.program_id(0) < PLAIN)
    def _():
        store(share_ref[0].astype(F32))

    @pl.when(pl.program_id(0) >= PLAIN)
    def _():
        total = parts[0][0].astype(F32)
        for ref in parts[1:]:
            total = total + ref[0].astype(F32)
        store(total)


def unpack(share, parts):
    block = (1, ROWS, 3 * H)
    return pl.pallas_call(
        unpack_kernel,
        grid=(LOCAL,),
        in_specs=[pl.BlockSpec(block, lambda e: (jnp.minimum(e, PLAIN - 1), 0, 0))]
        + [pl.BlockSpec(block, lambda e: (jnp.maximum(e - PLAIN, 0), 0, 0))] * LINE,
        out_specs=[per_expert(ROWS, H)] * 3,
        out_shape=[shape((LOCAL, ROWS, H), F32)] * 3,
        compiler_params=params(),
        cost_estimate=cost(LOCAL * ROWS * 3 * H, 5 << 20),
        name="unpack",
    )(share, *parts)


def spread_tables(all_routes, me):
    lane = jnp.arange(LANES, dtype=jnp.int32)
    member = jnp.sum((all_routes[..., None] == lane).astype(F32), axis=2)
    mine = me * LOCAL + jnp.arange(LOCAL, dtype=jnp.int32)
    own = jnp.sum((all_routes[..., None] == mine).astype(F32), axis=2)
    earlier = (np.arange(T)[:, None] > np.arange(T)[None, :]).astype(np.float32)
    before = jnp.einsum(
        "ts,rse->rte", jnp.asarray(earlier, BF16), own.astype(BF16), preferred_element_type=F32
    )
    slots = jnp.where(own > 0.5, before.astype(jnp.int32), -1)
    slots = jnp.swapaxes(slots, 1, 2)[:, :, None, :]
    place = slots == jnp.arange(CAP, dtype=jnp.int32)[None, None, :, None]
    return member, place.astype(BF16).reshape(PEERS, SLOTS, T)


def body(
    tokens,
    cotangent,
    routes,
    norm_one,
    w_query,
    key_weight,
    value_weight,
    w_out,
    norm_two,
    w_router,
    w_gate,
    w_up,
    w_down,
):
    me = lax.axis_index("expert")
    place_in_group = lax.axis_index("fsdp")
    z = me % Z
    core = place_in_group % 2
    cosine, signed = (jnp.asarray(table) for table in rope_tables())

    first, second = pack(
        z.astype(jnp.int32)[None],
        w_out,
        w_query,
        key_weight,
        value_weight,
        w_router.T,
        norm_one[None, :],
        norm_two[None, :],
    )
    def spread_over_chips(value):
        pair = jnp.stack([value, send_chip(value, LINE)])
        own = [send_chip(pair, hop) for hop in range(LINE)]
        return own, [swap_core(value) for value in own]

    own, other = spread_over_chips(first)
    out_own, _ = spread_over_chips(after(second, own[1]))
    sources = jnp.stack([chip_at(place_in_group, hop, True) for hop in range(CHIPS)])
    order = jnp.concatenate([2 * sources + core, 2 * sources + 1 - core]).astype(jnp.int32)
    dests = jnp.stack([chip_at(place_in_group, hop) for hop in range(CHIPS)]).astype(jnp.int32)
    twins = jnp.concatenate([2 * dests + core, 2 * dests + 1 - core])
    expert_pack = lax.all_gather(
        jnp.concatenate([w_gate, w_up, jnp.swapaxes(w_down, 1, 2)], axis=2),
        "fsdp",
        axis=1,
        tiled=True,
    )

    behind = jnp.stack([(z + Z - hop) % Z for hop in range(Z)]).astype(jnp.int32)
    ahead = jnp.stack([(z + hop) % Z for hop in range(Z)]).astype(jnp.int32)

    marks = jnp.pad(routes, ((0, 0), (0, LANES - TOPK))).astype(BF16)
    early = jnp.concatenate([cotangent, marks], axis=1)
    whole_row = jnp.concatenate([tokens, early], axis=1)
    whole_row = after(whole_row, first)
    xs = [send(whole_row, hop) for hop in (0, 1, 3)]
    xs.insert(2, send(whole_row, 2))
    w, gains, h1, qkv, ob = project(order, cosine, signed, own, other, xs)
    obs = [send(ob, hop) for hop in range(Z)]
    out_other = [swap_core(after(value, ob)) for value in out_own]
    early_other = send(after(early, xs[3]), Z)
    w_out_slice, ob_full, *x1_columns = out_project(behind, order, out_own, out_other, obs)
    x1_pieces = [send(x1_columns[hop], hop, True) for hop in range(Z)]
    early_other = after(early_other, x1_pieces[1])
    early_other = [send(early_other, hop) for hop in range(Z)]
    x1, h2 = residual(ahead, tokens, gains, x1_pieces)
    h2_other = send(h2, Z)
    h2_line = [send(h2, hop) for hop in range(Z)]
    h2_other = [send(h2_other, hop) for hop in range(Z)]

    all_routes = jnp.stack(
        [r[:, 2 * D : 2 * D + TOPK].astype(jnp.int32) for r in xs]
        + [r[:, D : D + TOPK].astype(jnp.int32) for r in early_other]
    )
    member, place = spread_tables(all_routes, me)
    row_expert = me * LOCAL + jnp.arange(SLOTS, dtype=jnp.int32) // CAP
    chosen = (row_expert[:, None] == jnp.arange(LANES, dtype=jnp.int32)[None, :]).astype(F32)
    dyr = spread_rows(after(place, h2_line[1]), xs, early_other)

    gates, gate0, b0 = gate_rows(0, w, member, chosen, place, h2_line)
    _, gate1, b1 = gate_rows(1, w, member, chosen, place, h2_other)
    b, slot_gate = (b0, b1), (gate0, gate1)
    weights = after(cut_out(ahead, after(w_out_slice, x1)), b1)
    slot_gate = after(slot_gate, *weights)
    weights = [send(weights[hop], hop) for hop in range(Z)]
    number = me.astype(jnp.int32)[None]
    gy, db, grad_pack = experts(number, b, dyr, slot_gate, expert_pack)
    extra_gy, extra_db, keep_extra, give_extra = extra_experts(
        after(number, db), b, dyr, slot_gate, twins, expert_pack
    )
    db_parts = collect(place, after((db, extra_db), *weights[1:]), "collect_grads")
    grad_cross = [send(db_parts[Z + hop], hop, True) for hop in range(Z)]
    grad_line = after(db_parts[:Z], *grad_cross[1:])
    grad_line = [send(grad_line[hop], hop, True) for hop in range(Z)]
    got_extra = swap_core(give_extra)
    grad_other = send(add_all(grad_cross, "line_grads"), Z)
    expert_share = lax.psum_scatter(
        after(grad_pack, *weights[1:]), "fsdp", scatter_dimension=1, tiled=True
    )
    results = collect(place, (gy, extra_gy), "collect_results")
    grad_line = after(grad_line, results)
    dx1, dlogits, scaled, da = token_back(x1, cotangent, gates, w, gains, [*grad_line, grad_other])
    das = [send(da, hop) for hop in range(Z)]
    extra_line, extra_cross = extra_halves(keep_extra, after(got_extra, da))
    shadows = shadow(after(qkv, extra_cross), h2, dlogits, scaled)
    results = after(results, shadows[1], *das[1:])
    results_cross = [send(results[Z + hop], hop, True) for hop in range(Z)]
    *returns, keep, give = head_back(
        behind,
        core.astype(jnp.int32)[None],
        qkv,
        h1,
        w,
        ob_full,
        shadows,
        cosine,
        signed,
        das,
        weights,
        results[:Z],
    )
    parts = split(dests, keep, swap_core(after(give, *results_cross[1:])))
    extra_got = send_chip(extra_cross, LINE)
    parts = after(parts, expert_share)
    lines = [send_chip(parts[hop], hop) for hop in range(LINE)]
    results_other = send(add_all(results_cross, "line_results"), Z)
    first, third = send(returns[1], 1, True), send(returns[3], 3, True)
    lines[0] = after(lines[0], first, third)
    second = send(after(returns[2], first, third), 2, True)
    returns = [returns[0], first, second, third]
    share = sum_lines(lines)
    extra_parts = extra_lines(extra_line, after(extra_got, share[1]))
    share = add_all([share[0], send_chip(share[1], LINE)], "sum_chips")
    share = add_all([share, send(share, Z)], "sum_halves")
    extra_first, extra_third = (send_chip(extra_parts[hop], hop) for hop in (1, 3))
    share = after(share, second)
    extra_second = send_chip(extra_parts[2], 2)
    extra_parts = [extra_parts[0], extra_first, extra_second, extra_third]
    shares = [send(share, hop) for hop in range(Z)]
    grad_gate, grad_up, grad_down = unpack(expert_share, extra_parts)
    grad_tokens = token_grad(tokens, gains, dx1, returns)
    mixed_out = mix(x1, returns, results_other)
    shares = after(shares, grad_tokens, mixed_out, grad_gate)
    grad_query, grad_key, grad_value, grad_out, router, one, two = finish(
        behind, shares, w_query, key_weight, value_weight, norm_one[None, :]
    )

    return (
        mixed_out,
        grad_tokens,
        one.reshape(ROWS),
        grad_query,
        grad_key,
        grad_value,
        grad_out,
        two.reshape(ROWS),
        router.T,
        grad_gate,
        grad_up,
        jnp.swapaxes(grad_down, 1, 2),
    )


def solution(mesh):
    return jax.shard_map(
        body,
        mesh=mesh,
        in_specs=(
            P(("expert", "fsdp"), None),
            P(("expert", "fsdp"), None),
            P(("expert", "fsdp"), None),
            P("fsdp"),
            P("fsdp", None),
            P("fsdp", None),
            P("fsdp", None),
            P("fsdp", None),
            P("fsdp"),
            P("fsdp", None),
            P("expert", "fsdp", None),
            P("expert", "fsdp", None),
            P("expert", None, "fsdp"),
        ),
        out_specs=(
            P(("expert", "fsdp"), None),
            P(("expert", "fsdp"), None),
            P("fsdp"),
            P("fsdp", None),
            P("fsdp", None),
            P("fsdp", None),
            P("fsdp", None),
            P("fsdp"),
            P("fsdp", None),
            P("expert", "fsdp", None),
            P("expert", "fsdp", None),
            P("expert", None, "fsdp"),
        ),
        check_vma=False,
    )
```
